128 devices in a mesh: seq: 32 (over x_lo, z, y), head: 4 (over x_hi, core).
Axes of the slice: x: 4 (x_hi: 2, x_lo: 2; x = x_hi * 2 + x_lo), y: 4, z: 4, core: 2. Of those that a mesh axis runs over, the one named last changes fastest.
Arguments:
- queries: bfloat16 [4096, 3584], P('seq', 'head'), may hold values from -80 to 80
- key_vectors: bfloat16 [4096, 512], P('seq', 'head'), may hold values from -4 to 4
- value_vectors: bfloat16 [4096, 512], P('seq', 'head'), may hold values from -10 to 10
- out_cotangent: bfloat16 [4096, 3584], P('seq', 'head'), may hold values from -6 to 6
- latent_mask: int32 [4096], P('seq'), may hold values from 0 to 1, as said below
- clean_latents: float32 [2048, 64], P('seq'), may hold values from -6 to 6
- noise_draws: float32 [2048, 256], P('seq'), may hold values from -6 to 6
- timesteps: int32 [2048, 4], P('seq'), may hold values from 0 to 999
- latent_in: bfloat16 [64, 3584], replicated, may hold values from -0.75 to 0.75
- norm_gain: float32 [3584], replicated, may hold values from 0.1 to 1.9
- gate_weight: bfloat16 [3584, 5632], P('seq', 'head'), may hold values from -0.09375 to 0.09375
- up_weight: bfloat16 [3584, 5632], P('seq', 'head'), may hold values from -0.09375 to 0.09375
- down_weight: bfloat16 [3584, 5632], P('seq', 'head'), may hold values from -0.078125 to 0.078125
- out_gain: float32 [3584], replicated, may hold values from 0.1 to 1.9
- latent_out: bfloat16 [3584, 64], replicated, may hold values from -0.09375 to 0.09375
Outputs:
- attention_out: bfloat16 [4096, 3584], P('seq', 'head')
- grad_queries: bfloat16 [4096, 3584], P('seq', 'head')
- grad_keys: bfloat16 [4096, 512], P('seq', 'head')
- grad_values: bfloat16 [4096, 512], P('seq', 'head')
- prediction: float32 [2048, 256], P('seq', 'head')
The draws below stay inside these ranges and needn't reach their ends.
Inputs may be any that keep to these rules, and one draw needn't show every extreme that they name: `latent_mask`: within each block of 128 positions the positions with mask 1 form one contiguous run of 64/4 (rounded down) to 64 positions; in every draw some block holds exactly 64.
All inputs are finite; a program needn't handle non-finite values.
Results may differ from the reference program's by a relative error of at most 0.035.
Values may be sent and summed in bfloat16 or wider, within the bound.
A program may use at most 128 MiB of HBM per device.

```python
import math
import jax
import jax.numpy as jnp
from jax import lax

HEADS = 28
KVH = 4
HD = 128
D = 3584
FFW = 5632
LAT = 64
NOISE = 4
TOK_DEV = 128
CAP = 64
TOKENS = 4096
SLOTS = 2048
FF_DEV = 1408
N_SEQ = 32
N_HEAD = 4


def shared_keys(key):
    return jnp.clip(jax.random.normal(key, (TOKENS, KVH * HD), jnp.float32), -4.0, 4.0)


def draw_key_vectors(key, part):
    base = shared_keys(key)
    return base.astype(jnp.bfloat16)


def draw_queries(key, part):
    key = jax.random.fold_in(key, 9)
    fresh = jnp.clip(jax.random.normal(key, (TOKENS, HEADS * HD), jnp.float32), -4.0, 4.0)
    return fresh.astype(jnp.bfloat16)


def draw_latent_mask(key, part):
    key = jax.random.fold_in(key, 3)
    blocks = TOKENS // TOK_DEV
    count_key, full_key, start_key = jax.random.split(key, 3)
    counts = jax.random.randint(count_key, (blocks,), CAP // 4, CAP + 1, dtype=jnp.int32)
    chosen = jax.random.randint(full_key, (), 0, blocks, dtype=jnp.int32)
    counts = jnp.where(jnp.arange(blocks, dtype=jnp.int32) == chosen, CAP, counts)
    starts = jax.random.randint(start_key, (blocks,), 0, TOK_DEV - counts + 1, dtype=jnp.int32)
    positions = jnp.arange(TOK_DEV, dtype=jnp.int32)[None, :]
    inside = (positions >= starts[:, None]) & (positions < (starts + counts)[:, None])
    return inside.astype(jnp.int32).reshape(TOKENS)


def place_ends(entries, rng, low, largest):
    longest = entries.shape.index(max(entries.shape))
    spots = []
    for shift in (0, 1):
        where = [jax.random.randint(jax.random.fold_in(rng, axis), (), 0, length) for axis, length in enumerate(entries.shape)]
        where[longest] = (where[longest] + shift) % entries.shape[longest]
        spots.append(tuple(where))
    return entries.at[spots[0]].set(low).at[spots[1]].set(largest)


def level_of(key, dims, pieces, least, largest):
    level = 1.0
    for axis_at, parts in pieces:
        heights = jax.random.uniform(jax.random.fold_in(jax.random.fold_in(key, 6), axis_at), (parts,), jnp.float32, least / len(pieces), largest / len(pieces))
        level = level * jnp.repeat(jnp.exp(heights), dims[axis_at] // parts).reshape((-1,) + (1,) * (len(dims) - 1 - axis_at))
    return level


def bell_draw(own_key, shape, deviation, most, cuts=(), held_as=jnp.bfloat16):
    entries = deviation * jax.random.normal(own_key, shape, jnp.float32)
    if cuts:
        entries = entries * level_of(own_key, shape, cuts, -0.22, 0.18)
    return jnp.clip(entries, -most, most).astype(held_as)


def setup_inputs(seed: int = 0) -> dict:
    arg_keys = jax.random.split(jax.random.key(seed), 16)
    queries = draw_queries(jax.random.fold_in(arg_keys[15], 71), 0)
    key_vectors = draw_key_vectors(jax.random.fold_in(arg_keys[15], 71), 0)
    value_vectors = bell_draw(arg_keys[2], (TOKENS, KVH * HD), 2.0, 10.0, ((0, 32), (1, 4)))
    out_cotangent = bell_draw(arg_keys[3], (TOKENS, HEADS * HD), 1.0, 6.0, ((0, 32), (1, 4)))
    latent_mask = draw_latent_mask(jax.random.fold_in(arg_keys[15], 71), 0)
    clean_latents = bell_draw(arg_keys[5], (SLOTS, LAT), 1.0, 6.0, ((0, 32),), jnp.float32)
    noise_draws = bell_draw(arg_keys[6], (SLOTS, NOISE * LAT), 1.0, 6.0, ((0, 32),), jnp.float32)
    timesteps = place_ends(jax.random.randint(arg_keys[7], (SLOTS, NOISE), 0, 1000), jax.random.fold_in(arg_keys[7], 1), 0, 999).astype(jnp.int32)
    latent_in = bell_draw(arg_keys[8], (LAT, D), LAT ** -0.5, 0.75)
    norm_gain = jnp.clip(1.0 + 0.18 * jax.random.normal(arg_keys[9], (D,), jnp.float32), 0.1, 1.9)
    gate_weight = bell_draw(arg_keys[10], (D, FFW), D ** -0.5, 0.09375, ((0, 32), (1, 4)))
    up_weight = bell_draw(arg_keys[11], (D, FFW), D ** -0.5, 0.09375, ((0, 32), (1, 4)))
    down_weight = bell_draw(arg_keys[12], (D, FFW), FFW ** -0.5, 0.078125, ((0, 32), (1, 4)))
    out_gain = jnp.clip(1.0 + 0.18 * jax.random.normal(arg_keys[13], (D,), jnp.float32), 0.1, 1.9)
    latent_out = bell_draw(arg_keys[14], (D, LAT), D ** -0.5, 0.09375)
    return dict(queries=queries, key_vectors=key_vectors, value_vectors=value_vectors, out_cotangent=out_cotangent, latent_mask=latent_mask, clean_latents=clean_latents, noise_draws=noise_draws, timesteps=timesteps, latent_in=latent_in, norm_gain=norm_gain, gate_weight=gate_weight, up_weight=up_weight, down_weight=down_weight, out_gain=out_gain, latent_out=latent_out)


def round_keep(values):
    return lax.optimization_barrier(values.astype(jnp.bfloat16)).astype(jnp.float32)

def rms_scale(rows, gain):
    return rows * lax.rsqrt(lax.optimization_barrier(jnp.mean(rows * rows, axis=-1, keepdims=True)) + 1e-06) * gain

def reference(queries, key_vectors, value_vectors, out_cotangent, latent_mask, clean_latents, noise_draws, timesteps, latent_in, norm_gain, gate_weight, up_weight, down_weight, out_gain, latent_out):
    per_group = HEADS // KVH
    score_scale = 1.0 / math.sqrt(HD)
    outputs = []
    grads_query = []
    conditions = []
    slot_valid = []
    key_total = jnp.zeros((TOKENS, KVH, HD), jnp.float32)
    value_total = jnp.zeros((TOKENS, KVH, HD), jnp.float32)
    slot_ids = jnp.arange(CAP, dtype=jnp.int32)
    for block in range(N_SEQ):
        lower = block * TOK_DEV
        upper = lower + TOK_DEV
        query_rows = queries[lower:upper].reshape(TOK_DEV, KVH, per_group, HD).astype(jnp.float32)
        grad_rows = out_cotangent[lower:upper].reshape(TOK_DEV, KVH, per_group, HD).astype(jnp.float32)
        key_rows = key_vectors[:upper].reshape(upper, KVH, HD).astype(jnp.float32)
        value_rows = value_vectors[:upper].reshape(upper, KVH, HD).astype(jnp.float32)
        scores = jnp.einsum('qgjd,kgd->gjqk', query_rows, key_rows) * score_scale
        query_pos = lower + jnp.arange(TOK_DEV, dtype=jnp.int32)
        key_pos = jnp.arange(upper, dtype=jnp.int32)
        allowed = (key_pos[None, :] <= query_pos[:, None])[None, None]
        row_max = lax.optimization_barrier(jnp.max(jnp.where(allowed, scores, -jnp.inf), axis=-1))
        soft_exp = jnp.where(allowed, jnp.exp(scores - row_max[..., None]), 0.0)
        row_total = lax.optimization_barrier(jnp.sum(soft_exp, axis=-1))
        numer = jnp.einsum('gjqk,kgd->gjqd', round_keep(soft_exp), value_rows)
        attended = numer / row_total[..., None]
        out_block = jnp.transpose(attended, (2, 0, 1, 3)).reshape(TOK_DEV, HEADS * HD).astype(jnp.bfloat16)
        outputs.append(out_block)
        log_total = row_max + jnp.log(row_total)
        out_rows = out_block.reshape(TOK_DEV, KVH, per_group, HD).astype(jnp.float32)
        row_delta = jnp.einsum('qgjd,qgjd->gjq', out_rows, grad_rows)
        probs = jnp.where(allowed, jnp.exp(scores - log_total[..., None]), 0.0)
        grad_probs = jnp.einsum('qgjd,kgd->gjqk', grad_rows, value_rows)
        grad_scores = round_keep(probs * (grad_probs - row_delta[..., None]))
        grad_query = jnp.einsum('gjqk,kgd->qgjd', grad_scores, key_rows) * score_scale
        grads_query.append(grad_query.reshape(TOK_DEV, HEADS * HD).astype(jnp.bfloat16))
        key_part = jnp.einsum('gjqk,qgjd->kgd', grad_scores, query_rows) * score_scale
        value_part = jnp.einsum('gjqk,qgjd->kgd', round_keep(probs), grad_rows)
        key_total = key_total.at[:upper].add(round_keep(key_part))
        value_total = value_total.at[:upper].add(round_keep(value_part))
        mask_block = latent_mask[lower:upper]
        slot_rank = jnp.cumsum(mask_block, dtype=jnp.int32) - 1
        chooser = ((slot_rank[None, :] == slot_ids[:, None]) & (mask_block[None, :] == 1)).astype(jnp.bfloat16)
        conditions.append(jnp.dot(chooser, out_block, preferred_element_type=jnp.float32).astype(jnp.bfloat16))
        slot_valid.append(slot_ids < jnp.sum(mask_block, dtype=jnp.int32))
    attention_out = jnp.concatenate(outputs, axis=0)
    grad_queries = jnp.concatenate(grads_query, axis=0)
    grad_keys = key_total.reshape(TOKENS, KVH * HD).astype(jnp.bfloat16)
    grad_values = value_total.reshape(TOKENS, KVH * HD).astype(jnp.bfloat16)
    condition = jnp.concatenate(conditions, axis=0).astype(jnp.float32)
    valid_rows = jnp.concatenate(slot_valid, axis=0)
    step_float = timesteps.astype(jnp.float32)
    signal_share = jnp.cos((step_float / 1000.0 + 0.008) / 1.008 * (math.pi / 2.0)) ** 2
    noise_rows = noise_draws.reshape(SLOTS, NOISE, LAT)
    noisy_rows = jnp.sqrt(signal_share)[..., None] * clean_latents[:, None, :] + jnp.sqrt(1.0 - signal_share)[..., None] * noise_rows
    noisy_rows = noisy_rows.reshape(SLOTS * NOISE, LAT).astype(jnp.bfloat16)
    lifted = jnp.dot(noisy_rows, latent_in, preferred_element_type=jnp.float32)
    half_width = D // 2
    frequencies = jnp.exp(-math.log(10000.0) * jnp.arange(half_width, dtype=jnp.float32) / half_width)
    angles = step_float.reshape(SLOTS * NOISE)[:, None] * frequencies[None, :]
    embedding = jnp.concatenate([jnp.cos(angles), jnp.sin(angles)], axis=1)
    base_rows = jnp.repeat(condition, NOISE, axis=0) + lifted + embedding
    normed = rms_scale(base_rows, norm_gain).astype(jnp.bfloat16)
    ffn_total = jnp.zeros((SLOTS * NOISE, D), jnp.float32)
    for group in range(N_HEAD):
        lower = group * FF_DEV
        upper = lower + FF_DEV
        gate_sum = jnp.dot(normed, gate_weight[:, lower:upper], preferred_element_type=jnp.float32)
        up_sum = jnp.dot(normed, up_weight[:, lower:upper], preferred_element_type=jnp.float32)
        hidden = (jax.nn.silu(gate_sum) * up_sum).astype(jnp.bfloat16)
        ffn_part = lax.dot_general(hidden, down_weight[:, lower:upper], (((1,), (1,)), ((), ())), preferred_element_type=jnp.float32)
        ffn_total = ffn_total + round_keep(ffn_part)
    mixed_rows = base_rows + ffn_total
    final_rows = rms_scale(mixed_rows, out_gain).astype(jnp.bfloat16)
    predicted = jnp.dot(final_rows, latent_out, preferred_element_type=jnp.float32).reshape(SLOTS, NOISE * LAT)
    prediction = jnp.where(valid_rows[:, None], predicted, 0.0)
    return (attention_out, grad_queries, grad_keys, grad_values, prediction)
```

```python
import math

import jax
import jax.numpy as jnp
import numpy as np
from jax import lax
from jax.experimental import pallas as pl
from jax.experimental.pallas import tpu as pltpu
from jax.sharding import PartitionSpec as P

MESH = pl.DeviceIdType.MESH
F32 = jnp.float32
BF16 = jnp.bfloat16

HD = 128
GRP = 7
TOK = 128
ROWS = GRP * TOK
D = 3584
HALF = D // 2
LAT = 64
CAP = 64
NOISE = 4
N_SEQ = 32
N_HEAD = 4
FEAT = 112
GUW = 1408
DNW = 768
MAIN = 640
KC = 256
HEADW = D // N_HEAD
SCALE = 1.0 / math.sqrt(HD)
LOG2E = math.log2(math.e)
NEG = -1e30

HALVES = {"kv": ((0, 128), (128, 128)), "gu": ((0, 64), (64, 48)), "dn": ((0, 64), (64, 48))}


def contract_rows(left, right):
    return lax.dot_general(left, right, (((0,), (0,)), ((), ())), preferred_element_type=F32)


def dot(left, right):
    return jnp.dot(left, right, preferred_element_type=F32)


def kernel(
    q_ref, k_ref, v_ref, do_ref, mask_ref, clean_ref, noise_ref, time_ref, lin_ref, ngain_ref,
    gate_ref, up_ref, down_ref, ogain_ref, lout_ref, freq_ref,
    out_ref, dq_ref, dk_ref, dv_ref, pred_ref,
    kv, gu, dn, sgu, sdn, qs, qt, dos, dot_t, probs, acc_t, dkv, drecv, cond, nz, tm, tab, oha, ohb,
    le, nm, acc, hid, rbuf,
    ssem, rsem, dssem, drsem, fssem, frsem, cssem, crsem,
):
    s = lax.axis_index("seq")
    h = lax.axis_index("head")
    xl = lax.div(s, 16)
    zy = lax.rem(s, 16)
    z = lax.div(zy, 4)
    y = lax.rem(zy, 4)
    mate = (1 - xl) * 16 + zy

    bufs = {"kv": kv, "gu": gu, "dn": dn}
    sent = []
    recv_at = {}

    def recv_slot(key):
        if key not in recv_at:
            recv_at[key] = len(recv_at)
        return rsem.at[recv_at[key]]

    def start(src, dst, key, dev):
        copy = pltpu.make_async_remote_copy(
            src_ref=src, dst_ref=dst, send_sem=ssem.at[len(sent)], recv_sem=recv_slot(key),
            device_id=dev, device_id_type=MESH,
        )
        copy.start()
        sent.append(copy)

    def landed(dst, key, dev):
        pltpu.make_async_remote_copy(
            src_ref=dst, dst_ref=dst, send_sem=ssem.at[0], recv_sem=recv_slot(key),
            device_id=dev, device_id_type=MESH,
        ).wait_recv()

    def back(pos, dist):
        return lax.rem(pos + 4 - dist, 4)

    def chunk(p, r, d1, d2, half):
        dy, dz = (d1, d2) if r == 0 else (d2, d1)
        view = bufs[p].at[r, back(z, dz) * 4 + back(y, dy)]
        if half is None:
            return view
        first, count = HALVES[p][half]
        return view.at[pl.ds(first, count)]

    def neighbour(r, axis, step):
        along_y = (axis == 1) == (r == 0)
        if along_y:
            return (xl * 16 + z * 4 + back(y, -step), h)
        return (xl * 16 + back(z, -step) * 4 + y, h)

    def send(p, r, d1, d2, axis, step, half=None):
        ref = chunk(p, r, d1, d2, half)
        e1 = (d1 + step) % 4 if axis == 1 else d1
        e2 = (d2 + step) % 4 if axis == 2 else d2
        start(ref, ref, (p, r, e1, e2, half), neighbour(r, axis, step))

    def wait(p, r, d1, d2, half=None):
        landed(chunk(p, r, d1, d2, half), (p, r, d1, d2, half), (mate, h))

    def p1_send(p, r):
        send(p, r, 0, 0, 1, 1)
        send(p, r, 0, 0, 1, -1)

    def p1_fwd(p, r):
        wait(p, r, 1, 0)
        send(p, r, 1, 0, 1, 1, 0)
        wait(p, r, 3, 0)
        send(p, r, 3, 0, 1, -1, 1)

    def p1_fin(p, r):
        wait(p, r, 2, 0, 0)
        wait(p, r, 2, 0, 1)

    def p2_send(p, r, d1):
        send(p, r, d1, 0, 2, 1)
        send(p, r, d1, 0, 2, -1)

    def p2_fwd(p, r, d1):
        wait(p, r, d1, 1)
        send(p, r, d1, 1, 2, 1, d1 % 2)
        wait(p, r, d1, 3)
        send(p, r, d1, 3, 2, -1, 1 - d1 % 2)

    def p2_fin(p, r, d1):
        wait(p, r, d1, 2, 0)
        wait(p, r, d1, 2, 1)

    def both(step, p, *rest):
        step(p, 0, *rest)
        step(p, 1, *rest)

    barrier = pltpu.get_barrier_semaphore()

    def greet(i, carry):
        other = lax.rem(s + i, N_SEQ)
        pl.semaphore_signal(barrier, inc=1, device_id=(other, h), device_id_type=MESH)
        return carry

    lax.fori_loop(1, N_SEQ, greet, 0)
    line = [(dx, dh) for dx in (0, 1) for dh in range(N_HEAD) if (dx, dh) != (0, 0)]

    def on_line(dx, dh):
        ox = lax.rem(xl + dx, 2)
        oh = lax.rem(h + dh, N_HEAD)
        return ox, oh, (ox * 16 + zy, oh)

    for dx, dh in line:
        if dh:
            pl.semaphore_signal(barrier, inc=1, device_id=on_line(dx, dh)[2], device_id_type=MESH)
    pl.semaphore_wait(barrier, N_SEQ - 1 + 6)

    kv[xl, zy, 0:TOK, :] = k_ref[...]
    kv[xl, zy, TOK : 2 * TOK, :] = v_ref[...]
    start(kv.at[xl, zy], kv.at[xl, zy], "xkv", (mate, h))

    low = lax.broadcasted_iota(jnp.int32, (FEAT, 128), 1) < 64

    def pack(f, put_gu, put_dn):
        at = f * 768
        mid_gate = gate_ref[:, MAIN : MAIN + 128].astype(F32)
        mid_up = up_ref[:, MAIN : MAIN + 128].astype(F32)
        if f == 0:
            mixed = jnp.where(low, mid_gate, pltpu.roll(mid_up, 64, 1))
        else:
            mixed = jnp.where(low, pltpu.roll(mid_gate, 64, 1), mid_up)
        put_gu(0, gate_ref[:, at : at + MAIN])
        put_gu(MAIN, up_ref[:, at : at + MAIN])
        put_gu(2 * MAIN, mixed.astype(BF16))
        put_dn(down_ref[:, f * MAIN : f * MAIN + DNW])

    def own_gu(at, value):
        gu[xl, zy, :, at : at + value.shape[1]] = value

    def own_dn(value):
        dn[xl, zy] = value

    def mate_gu(at, value):
        sgu[:, at : at + value.shape[1]] = value

    def mate_dn(value):
        sdn[...] = value

    for f in (0, 1):

        @pl.when(xl == f)
        def _():
            pack(1 - f, mate_gu, mate_dn)
            pack(f, own_gu, own_dn)

    start(sgu, gu.at[xl, zy], "xgu", (mate, h))

    share = jnp.cos((time_ref[...].astype(F32) / 1000.0 + 0.008) / 1.008 * (math.pi / 2.0)) ** 2
    signal, noise_part = jnp.sqrt(share), jnp.sqrt(1.0 - share)
    nz[xl] = jnp.zeros((NOISE * CAP, 128), BF16)
    tm[xl] = jnp.zeros((CAP, 128), jnp.int32)
    tm[xl, :, 0:NOISE] = time_ref[...]
    for n in range(NOISE):
        row = signal[:, n : n + 1] * clean_ref[...] + noise_part[:, n : n + 1] * noise_ref[:, n * LAT : (n + 1) * LAT]
        nz[xl, n * CAP : (n + 1) * CAP, 0:LAT] = row.astype(BF16)
    start(nz.at[xl], nz.at[xl], "xnz", (mate, h))
    start(tm.at[xl], tm.at[xl], "xtm", (mate, h))

    landed(kv.at[1 - xl, zy], "xkv", (mate, h))
    both(p1_send, "kv")
    both(p2_send, "kv", 0)
    start(sdn, dn.at[xl, zy], "xdn", (mate, h))

    for j in range(GRP):
        cols = slice(j * HD, (j + 1) * HD)
        qs[cols, :] = q_ref[:, cols]
        dos[cols, :] = do_ref[:, cols]
        qt[:, cols] = q_ref[:, cols].astype(F32).T.astype(BF16)
        dot_t[:, cols] = do_ref[:, cols].astype(F32).T.astype(BF16)

    both(p1_fwd, "kv")
    both(p2_send, "kv", 1)
    both(p2_send, "kv", 3)
    landed(gu.at[1 - xl, zy], "xgu", (mate, h))
    both(p1_send, "gu")

    steps = lax.broadcasted_iota(jnp.int32, (32, HALF), 0).astype(F32)
    for k, mult in ((0, 32.0), (2, 1.0)):
        angle = (steps * mult) * freq_ref[...]
        for kk, value in ((k, jnp.cos(angle)), (k + 1, jnp.sin(angle))):
            high = value.astype(BF16)
            rest = value - high.astype(F32)
            middle = rest.astype(BF16)
            tab[kk, 0:32, :] = high
            tab[kk, 32:64, :] = middle
            tab[kk, 64:96, :] = (rest - middle.astype(F32)).astype(BF16)
            tab[kk, 96:128, :] = jnp.zeros((32, HALF), BF16)

    both(p1_fin, "kv")
    both(p2_send, "kv", 2)
    for d in (0, 1, 3, 2):
        both(p2_fwd, "kv", d)
    both(p1_fwd, "gu")
    both(p2_send, "gu", 0)

    landed(nz.at[1 - xl], "xnz", (mate, h))
    landed(tm.at[1 - xl], "xtm", (mate, h))
    lane = lax.broadcasted_iota(jnp.int32, (CAP, 128), 1)
    for b in (0, 1):
        for n in range(NOISE):
            rows = slice((b * NOISE + n) * CAP, (b * NOISE + n + 1) * CAP)
            step = tm[b, :, n : n + 1]
            for ref, digit in ((oha, step >> 5), (ohb, step & 31)):
                ref[rows, :] = jnp.where((lane & 31) == digit, jnp.where(lane < 96, 1.0, 0.0), 0.0).astype(BF16)

    both(p2_send, "gu", 1)
    both(p2_send, "gu", 3)

    def embed(j, carry):
        c0 = pl.ds(pl.multiple_of(j * 256, 256), 256)
        c1 = pl.ds(pl.multiple_of(HALF + j * 256, 256), 256)
        noisy = nz[...].reshape(2 * NOISE * CAP, 128)[:, 0:LAT]
        ca, sa = dot(oha[...], tab[0, :, c0]), dot(oha[...], tab[1, :, c0])
        cb, sb = dot(ohb[...], tab[2, :, c0]), dot(ohb[...], tab[3, :, c0])
        le[:, c0] = ca * cb - sa * sb + dot(noisy, lin_ref[:, c0])
        le[:, c1] = sa * cb + ca * sb + dot(noisy, lin_ref[:, c1])
        return carry

    lax.fori_loop(0, HALF // 256, embed, 0)

    for d in (0, 1, 3, 2):
        both(p2_fin, "kv", d)
    both(p1_fin, "gu")
    both(p2_send, "gu", 2)
    landed(dn.at[1 - xl, zy], "xdn", (mate, h))
    both(p1_send, "dn")

    n_steps = lax.div(s, 2) + 1

    def keys_of(c):
        blocks = kv.at[lax.div(c, 8), pl.ds(lax.rem(c, 8) * 2, 2)]
        return blocks[:, 0:TOK, :].reshape(KC, HD), blocks[:, TOK : 2 * TOK, :].reshape(KC, HD)

    def scores_of(c, masked):
        score = dot(keys_of(c)[0], qt[...]) * (SCALE * LOG2E)
        if masked:
            key_pos = c * KC + lax.broadcasted_iota(jnp.int32, (KC, ROWS), 0)
            query_pos = s * TOK + (lax.broadcasted_iota(jnp.int32, (KC, ROWS), 1) & (TOK - 1))
            score = jnp.where(key_pos <= query_pos, score, NEG)
        return score

    def fold(values, reduce):
        return reduce(values.reshape(KC // 8, 8, ROWS), axis=0)

    def max_step(c, run, masked=False):
        return jnp.maximum(run, fold(scores_of(c, masked), jnp.max))

    row_max = lax.fori_loop(0, n_steps - 1, max_step, jnp.full((8, ROWS), NEG, F32))
    row_max = max_step(n_steps - 1, row_max, True)
    row_max = jnp.max(row_max, axis=0, keepdims=True)
    both(p2_fwd, "gu", 0)

    acc_t[...] = jnp.zeros_like(acc_t)

    def sum_step(c, run, masked=False):
        soft = jnp.exp2(scores_of(c, masked) - row_max)
        soft_b = soft.astype(BF16)
        probs[pl.ds(pl.multiple_of(c * KC, KC), KC), :] = soft_b
        acc_t[...] += contract_rows(keys_of(c)[1], soft_b)
        return run + fold(soft, jnp.sum)

    total = lax.fori_loop(0, n_steps - 1, sum_step, jnp.zeros((8, ROWS), F32))
    total = sum_step(n_steps - 1, total, True)
    total = jnp.sum(total, axis=0, keepdims=True)
    inverse = 1.0 / total
    out_t = (acc_t[...] / total).astype(BF16)
    delta = jnp.sum(out_t.astype(F32) * dot_t[...].astype(F32), axis=0, keepdims=True)
    for j in range(GRP):
        cols = slice(j * HD, (j + 1) * HD)
        out_ref[:, cols] = out_t[:, cols].astype(F32).T.astype(BF16)

    mask = mask_ref[...]
    ones = jnp.broadcast_to(mask.astype(F32), (8, TOK)).astype(BF16)
    before = lax.broadcasted_iota(jnp.int32, (TOK, TOK), 0) <= lax.broadcasted_iota(jnp.int32, (TOK, TOK), 1)
    rank = dot(ones, jnp.where(before, 1.0, 0.0).astype(BF16))[0:1, :] - 1.0
    slot = lax.broadcasted_iota(jnp.int32, (CAP, TOK), 0).astype(F32)
    chosen = jnp.where(rank == slot, jnp.where(mask == 1, 1.0, 0.0), 0.0)
    valid = jnp.sum(chosen, axis=1, keepdims=True) > 0.5
    cond[xl, h] = dot(chosen.astype(BF16), out_ref[...]).astype(BF16)
    cond_sent = []
    for i, (dx, dh) in enumerate(line):
        copy = pltpu.make_async_remote_copy(
            src_ref=cond.at[xl, h], dst_ref=cond.at[xl, h], send_sem=cssem.at[i],
            recv_sem=crsem.at[xl * N_HEAD + h], device_id=on_line(dx, dh)[2], device_id_type=MESH,
        )
        copy.start()
        cond_sent.append(copy)

    both(p2_fwd, "gu", 1)
    both(p1_fwd, "dn")
    both(p2_send, "dn", 0)

    acc_t[...] = jnp.zeros_like(acc_t)

    def term_copy(kb):
        return pltpu.make_async_remote_copy(
            src_ref=dkv.at[kb], dst_ref=drecv.at[s], send_sem=dssem.at[kb], recv_sem=drsem.at[s],
            device_id=(kb, h), device_id_type=MESH,
        )

    def grad_step(c, carry):
        keys, values = keys_of(c)
        prob = probs[pl.ds(pl.multiple_of(c * KC, KC), KC), :].astype(F32) * inverse
        ds = (prob * (dot(values, dot_t[...]) - delta)).astype(BF16)
        acc_t[...] += contract_rows(keys, ds)
        dkv[pl.ds(2 * c, 2), 0:TOK, :] = (dot(ds, qs[...]) * SCALE).astype(BF16).reshape(2, TOK, HD)
        dkv[pl.ds(2 * c, 2), TOK : 2 * TOK, :] = dot(prob.astype(BF16), dos[...]).astype(BF16).reshape(2, TOK, HD)
        for i in (0, 1):

            @pl.when(2 * c + i < s)
            def _():
                term_copy(2 * c + i).start()

        return carry

    for part in range(4):
        lax.fori_loop(part * 4, jnp.minimum(n_steps, part * 4 + 4), grad_step, 0)
        if part == 0:
            both(p2_fwd, "gu", 3)
            both(p2_send, "dn", 1)
            both(p2_send, "dn", 3)
        elif part == 1:
            both(p2_fwd, "gu", 2)
            both(p1_fin, "dn")
            both(p2_send, "dn", 2)
        elif part == 2:
            both(p2_fwd, "dn", 0)

    for j in range(GRP):
        cols = slice(j * HD, (j + 1) * HD)
        dq_ref[:, cols] = (acc_t[:, cols] * SCALE).T.astype(BF16)

    for dx, dh in line:
        ox, oh, dev = on_line(dx, dh)
        pltpu.make_async_remote_copy(
            src_ref=cond.at[ox, oh], dst_ref=cond.at[ox, oh], send_sem=cssem.at[0],
            recv_sem=crsem.at[ox * N_HEAD + oh], device_id=dev, device_id_type=MESH,
        ).wait_recv()

    def norm_rows(g, carry):
        rows = pl.ds(pl.multiple_of(g * CAP, CAP), CAP)
        square = jnp.zeros((CAP, 1), F32)
        for hh in range(N_HEAD):
            cols = slice(hh * HEADW, (hh + 1) * HEADW)
            base = le[rows, cols] + cond[lax.div(g, NOISE), hh].astype(F32)
            le[rows, cols] = base
            square += jnp.sum(base * base, axis=1, keepdims=True)
        scale = lax.rsqrt(square * (1.0 / D) + 1e-06)
        for hh in range(N_HEAD):
            cols = slice(hh * HEADW, (hh + 1) * HEADW)
            nm[rows, cols] = (le[rows, cols] * scale * ngain_ref[:, cols]).astype(BF16)
        return carry

    lax.fori_loop(0, 2 * NOISE, norm_rows, 0)
    both(p2_fwd, "dn", 1)
    for d in (0, 1, 3, 2):
        both(p2_fin, "gu", d)

    for k in range(4):
        piece = gu[k // 2, (k % 2) * 8 : (k % 2) * 8 + 8].reshape(8 * FEAT, GUW)
        part = dot(nm[:, k * 896 : (k + 1) * 896], piece)
        if k == 0:
            acc[...] = part
        else:
            acc[...] += part
        if k == 1:
            both(p2_fwd, "dn", 3)

    def silu(value):
        return value / (1.0 + jnp.exp(-value))

    both(p2_fwd, "dn", 2)
    mixed = acc[:, 2 * MAIN :]
    turned = pltpu.roll(mixed, 64, 1)
    lower_half = lax.broadcasted_iota(jnp.int32, (2 * NOISE * CAP, 128), 1) < 64

    @pl.when(xl == 0)
    def _():
        hid[:, 0:MAIN] = (silu(acc[:, 0:MAIN]) * acc[:, MAIN : 2 * MAIN]).astype(BF16)
        hid[:, MAIN:DNW] = jnp.where(lower_half, silu(mixed) * turned, 0.0).astype(BF16)

    @pl.when(xl == 1)
    def _():
        hid[:, 128:DNW] = (silu(acc[:, 0:MAIN]) * acc[:, MAIN : 2 * MAIN]).astype(BF16)
        hid[:, 0:128] = jnp.where(lower_half, 0.0, silu(turned) * mixed).astype(BF16)

    for d in (0, 1, 3, 2):
        both(p2_fin, "dn", d)

    part_sent = []
    for k in range(4):
        cols = slice(k * 896, (k + 1) * 896)
        piece = dn[k // 2, (k % 2) * 8 : (k % 2) * 8 + 8].reshape(8 * FEAT, DNW)
        part = lax.dot_general(hid[...], piece, (((1,), (1,)), ((), ())), preferred_element_type=F32)
        nm[:, cols] = part.astype(BF16)
        for i, (dx, dh) in enumerate(line):
            ox, oh, dev = on_line(dx, dh)
            rows = pl.ds(pl.multiple_of((ox * NOISE + oh) * CAP, CAP), CAP)
            me = xl * N_HEAD + h
            copy = pltpu.make_async_remote_copy(
                src_ref=nm.at[rows, cols], dst_ref=rbuf.at[me, k], send_sem=fssem.at[k * 7 + i],
                recv_sem=frsem.at[me * 4 + k], device_id=dev, device_id_type=MESH,
            )
            copy.start()
            part_sent.append(copy)

    def add_terms(i, run):
        pltpu.make_async_remote_copy(
            src_ref=drecv.at[i], dst_ref=drecv.at[i], send_sem=dssem.at[0], recv_sem=drsem.at[i],
            device_id=(mate, h), device_id_type=MESH,
        ).wait_recv()
        return run + drecv[i].astype(F32)

    terms = lax.fori_loop(s + 1, N_SEQ, add_terms, dkv[s].astype(F32))
    dk_ref[...] = terms[0:TOK].astype(BF16)
    dv_ref[...] = terms[TOK : 2 * TOK].astype(BF16)

    own = pl.ds(pl.multiple_of((xl * NOISE + h) * CAP, CAP), CAP)
    square = jnp.zeros((CAP, 1), F32)
    for k in range(4):
        cols = slice(k * 896, (k + 1) * 896)
        rows = le[own, cols] + nm[own, cols].astype(F32)
        for dx, dh in line:
            ox, oh, dev = on_line(dx, dh)
            src = ox * N_HEAD + oh
            pltpu.make_async_remote_copy(
                src_ref=rbuf.at[src, k], dst_ref=rbuf.at[src, k], send_sem=fssem.at[0],
                recv_sem=frsem.at[src * 4 + k], device_id=dev, device_id_type=MESH,
            ).wait_recv()
            rows += rbuf[src, k].astype(F32)
        le[own, cols] = rows
        square += jnp.sum(rows * rows, axis=1, keepdims=True)
    scale = lax.rsqrt(square * (1.0 / D) + 1e-06)
    result = jnp.zeros((CAP, LAT), F32)
    for k in range(4):
        cols = slice(k * 896, (k + 1) * 896)
        final = (le[own, cols] * scale * ogain_ref[:, cols]).astype(BF16)
        result += dot(final, lout_ref[cols, :])
    pred_ref[...] = jnp.where(valid, result, 0.0)

    for copy in sent + cond_sent + part_sent:
        copy.wait_send()

    def term_left(kb, carry):
        term_copy(kb).wait_send()
        return carry

    lax.fori_loop(0, s, term_left, 0)


def shards(
    queries, key_vectors, value_vectors, out_cotangent, latent_mask, clean_latents, noise_draws, timesteps,
    latent_in, norm_gain, gate_weight, up_weight, down_weight, out_gain, latent_out,
):
    frequencies = np.exp(-math.log(10000.0) * np.arange(HALF, dtype=np.float32) / HALF).astype(np.float32)
    vmem = pl.BlockSpec(memory_space=pltpu.VMEM)
    dma = pltpu.SemaphoreType.DMA
    n_sems = 140
    return pl.pallas_call(
        kernel,
        out_shape=(
            jax.ShapeDtypeStruct((TOK, ROWS), BF16),
            jax.ShapeDtypeStruct((TOK, ROWS), BF16),
            jax.ShapeDtypeStruct((TOK, HD), BF16),
            jax.ShapeDtypeStruct((TOK, HD), BF16),
            jax.ShapeDtypeStruct((CAP, LAT), F32),
        ),
        in_specs=[vmem] * 16,
        out_specs=(vmem,) * 5,
        scratch_shapes=[
            pltpu.VMEM((2, 16, 2 * TOK, HD), BF16),
            pltpu.VMEM((2, 16, FEAT, GUW), BF16),
            pltpu.VMEM((2, 16, FEAT, DNW), BF16),
            pltpu.VMEM((FEAT, GUW), BF16),
            pltpu.VMEM((FEAT, DNW), BF16),
            pltpu.VMEM((ROWS, HD), BF16),
            pltpu.VMEM((HD, ROWS), BF16),
            pltpu.VMEM((ROWS, HD), BF16),
            pltpu.VMEM((HD, ROWS), BF16),
            pltpu.VMEM((N_SEQ * TOK, ROWS), BF16),
            pltpu.VMEM((HD, ROWS), F32),
            pltpu.VMEM((N_SEQ, 2 * TOK, HD), BF16),
            pltpu.VMEM((N_SEQ, 2 * TOK, HD), BF16),
            pltpu.VMEM((2, N_HEAD, CAP, HEADW), BF16),
            pltpu.VMEM((2, NOISE * CAP, 128), BF16),
            pltpu.VMEM((2, CAP, 128), jnp.int32),
            pltpu.VMEM((4, 128, HALF), BF16),
            pltpu.VMEM((2 * NOISE * CAP, 128), BF16),
            pltpu.VMEM((2 * NOISE * CAP, 128), BF16),
            pltpu.VMEM((2 * NOISE * CAP, D), F32),
            pltpu.VMEM((2 * NOISE * CAP, D), BF16),
            pltpu.VMEM((2 * NOISE * CAP, GUW), F32),
            pltpu.VMEM((2 * NOISE * CAP, DNW), BF16),
            pltpu.VMEM((8, 4, CAP, 896), BF16),
            dma((n_sems,)),
            dma((n_sems,)),
            dma((N_SEQ,)),
            dma((N_SEQ,)),
            dma((28,)),
            dma((32,)),
            dma((7,)),
            dma((8,)),
        ],
        compiler_params=pltpu.CompilerParams(
            collective_id=0, has_side_effects=True, vmem_limit_bytes=63 * 1024 * 1024
        ),
    )(
        queries, key_vectors, value_vectors, out_cotangent, latent_mask.reshape(1, TOK), clean_latents, noise_draws,
        timesteps, latent_in, norm_gain.reshape(1, D), gate_weight, up_weight, down_weight, out_gain.reshape(1, D),
        latent_out, jnp.asarray(frequencies.reshape(1, HALF)),
    )


def solution(mesh):
    placed = (
        P("seq", "head"),
        P("seq", "head"),
        P("seq", "head"),
        P("seq", "head"),
        P("seq"),
        P("seq", None),
        P("seq", None),
        P("seq", None),
        P(),
        P(),
        P("seq", "head"),
        P("seq", "head"),
        P("seq", "head"),
        P(),
        P(),
    )
    return jax.shard_map(
        shards,
        mesh=mesh,
        in_specs=placed,
        out_specs=(P("seq", "head"),) * 5,
        check_vma=False,
    )
```

```python
import math

import jax
import jax.numpy as jnp
import numpy as np
from jax import lax
from jax.experimental import pallas as pl
from jax.experimental.pallas import tpu as pltpu
from jax.sharding import PartitionSpec as P

MESH = pl.DeviceIdType.MESH
F32 = jnp.float32
BF16 = jnp.bfloat16

HD = 128
GRP = 7
TOK = 128
ROWS = GRP * TOK
D = 3584
HALF = D // 2
LAT = 64
CAP = 64
NOISE = 4
N_SEQ = 32
N_HEAD = 4
FEAT = 112
GUW = 1408
DNW = 768
MAIN = 640
KC = 256
HEADW = D // N_HEAD
SCALE = 1.0 / math.sqrt(HD)
LOG2E = math.log2(math.e)
NEG = -1e30

HALVES = {"kv": ((0, 128), (128, 128)), "gu": ((0, 64), (64, 48)), "dn": ((0, 64), (64, 48))}


def contract_rows(left, right):
    return lax.dot_general(left, right, (((0,), (0,)), ((), ())), preferred_element_type=F32)


def dot(left, right):
    return jnp.dot(left, right, preferred_element_type=F32)


def kernel(
    q_ref, k_ref, v_ref, do_ref, mask_ref, clean_ref, noise_ref, time_ref, lin_ref, ngain_ref,
    gate_ref, up_ref, down_ref, ogain_ref, lout_ref, freq_ref,
    out_ref, dq_ref, dk_ref, dv_ref, pred_ref,
    kv, gu, dn, sgu, sdn, qs, qt, dos, dot_t, probs, acc_t, dkv, drecv, cond, nz, tm, tab, oha, ohb,
    le, nm, acc, hid, s1, s23, r1, r2, r3, fin, xterm,
    ssem, rsem, dssem, drsem, cssem, crsem,
):
    s = lax.axis_index("seq")
    h = lax.axis_index("head")
    xl = lax.div(s, 16)
    zy = lax.rem(s, 16)
    core = lax.rem(h, 2)
    x = lax.div(h, 2) * 2 + xl
    z = lax.div(zy, 4)
    y = lax.rem(zy, 4)
    mate = (1 - xl) * 16 + zy

    bufs = {"kv": kv, "gu": gu, "dn": dn}
    sem_at = {}
    leaving = {}

    def copy_of(src, dst, key, dev):
        at = sem_at.setdefault(key, len(sem_at))
        return pltpu.make_async_remote_copy(
            src_ref=src, dst_ref=dst, send_sem=ssem.at[at], recv_sem=rsem.at[at], device_id=dev, device_id_type=MESH
        )

    def start(make, key):
        src, dst, dev = make()
        copy_of(src, dst, key, dev).start()
        leaving[key] = make

    def landed(dst, key, dev):
        copy_of(dst, dst, key, dev).wait_recv()

    def all_left():
        for key, make in leaving.items():
            src, dst, dev = make()
            copy_of(src, dst, key, dev).wait_send()

    def back(pos, dist):
        return lax.rem(pos + 4 - dist, 4)

    def chunk(p, r, d1, d2, half):
        dy, dz = (d1, d2) if r == 0 else (d2, d1)
        pz, py = back(z, dz), back(y, dy)
        view = bufs[p].at[r, py * 4 + pz if p == "dn" and r == 0 else pz * 4 + py]
        if half is None:
            return view
        first, count = HALVES[p][half]
        return view.at[pl.ds(first, count)]

    def neighbour(r, axis, step):
        along_y = (axis == 1) == (r == 0)
        if along_y:
            return (xl * 16 + z * 4 + back(y, -step), h)
        return (xl * 16 + back(z, -step) * 4 + y, h)

    def send(p, r, d1, d2, axis, step, half=None):
        e1 = (d1 + step) % 4 if axis == 1 else d1
        e2 = (d2 + step) % 4 if axis == 2 else d2

        def make():
            ref = chunk(p, r, d1, d2, half)
            return ref, ref, neighbour(r, axis, step)

        start(make, (p, r, e1, e2, half))

    def wait(p, r, d1, d2, half=None):
        landed(chunk(p, r, d1, d2, half), (p, r, d1, d2, half), (mate, h))

    def p1_send(p, r):
        send(p, r, 0, 0, 1, 1)
        send(p, r, 0, 0, 1, -1)

    def p1_own(p):
        for r in (0, 1):
            pl.when(xl == r)(lambda r=r: p1_send(p, r))

    def p1_other(p):
        for r in (0, 1):
            pl.when(xl != r)(lambda r=r: p1_send(p, r))

    def p1_fwd(p, r):
        wait(p, r, 1, 0)
        send(p, r, 1, 0, 1, 1, 0)
        wait(p, r, 3, 0)
        send(p, r, 3, 0, 1, -1, 1)

    def p1_fin(p, r):
        wait(p, r, 2, 0, 0)
        wait(p, r, 2, 0, 1)

    def p2_send(p, r, d1):
        send(p, r, d1, 0, 2, 1)
        send(p, r, d1, 0, 2, -1)

    def p2_fwd(p, r, d1):
        wait(p, r, d1, 1)
        send(p, r, d1, 1, 2, 1, d1 % 2)
        wait(p, r, d1, 3)
        send(p, r, d1, 3, 2, -1, 1 - d1 % 2)

    def p2_fin(p, r, d1):
        wait(p, r, d1, 2, 0)
        wait(p, r, d1, 2, 1)

    def both(step, p, *rest):
        step(p, 0, *rest)
        step(p, 1, *rest)

    barrier = pltpu.get_barrier_semaphore()

    def greet(i, carry):
        other = xl * 16 + lax.rem(zy + i, 16)
        pl.semaphore_signal(barrier, inc=1, device_id=(other, h), device_id_type=MESH)
        return carry

    lax.fori_loop(1, 16, greet, 0)
    line = [(dx, dh) for dx in (0, 1) for dh in range(N_HEAD) if (dx, dh) != (0, 0)]

    def on_line(dx, dh):
        ox = lax.rem(xl + dx, 2)
        oh = lax.rem(h + dh, N_HEAD)
        return ox, oh, (ox * 16 + zy, oh)

    for dx, dh in line:
        pl.semaphore_signal(barrier, inc=1, device_id=on_line(dx, dh)[2], device_id_type=MESH)
    pl.semaphore_wait(barrier, 15 + 7)

    kv[xl, zy, 0:TOK, :] = k_ref[...]
    kv[xl, zy, TOK : 2 * TOK, :] = v_ref[...]

    def same(ref):
        return lambda: (ref, ref, (mate, h))

    start(same(kv.at[xl, zy]), "xkv")
    p1_own("kv")
    dn_at = jnp.where(xl == 0, y * 4 + z, zy)

    low = lax.broadcasted_iota(jnp.int32, (FEAT, 128), 1) < 64

    def pack_gu(f, put):
        at = f * 768
        mid_gate = gate_ref[:, MAIN : MAIN + 128].astype(F32)
        mid_up = up_ref[:, MAIN : MAIN + 128].astype(F32)
        if f == 0:
            mixed = jnp.where(low, mid_gate, pltpu.roll(mid_up, 64, 1))
        else:
            mixed = jnp.where(low, pltpu.roll(mid_gate, 64, 1), mid_up)
        put(0, gate_ref[:, at : at + MAIN])
        put(MAIN, up_ref[:, at : at + MAIN])
        put(2 * MAIN, mixed.astype(BF16))

    def own_gu(at, value):
        gu[xl, zy, :, at : at + value.shape[1]] = value

    def mate_gu(at, value):
        sgu[:, at : at + value.shape[1]] = value

    for f in (0, 1):
        pl.when(xl == f)(lambda f=f: pack_gu(f, own_gu))
    p1_own("gu")
    for f in (0, 1):
        pl.when(xl == f)(lambda f=f: pack_gu(1 - f, mate_gu))
    start(lambda: (sgu, gu.at[xl, zy], (mate, h)), "xgu")

    share = jnp.cos((time_ref[...].astype(F32) / 1000.0 + 0.008) / 1.008 * (math.pi / 2.0)) ** 2
    signal, noise_part = jnp.sqrt(share), jnp.sqrt(1.0 - share)
    nz[xl] = jnp.zeros((NOISE * CAP, 128), BF16)
    tm[xl] = jnp.zeros((CAP, 128), jnp.int32)
    tm[xl, :, 0:NOISE] = time_ref[...]
    for n in range(NOISE):
        row = signal[:, n : n + 1] * clean_ref[...] + noise_part[:, n : n + 1] * noise_ref[:, n * LAT : (n + 1) * LAT]
        nz[xl, n * CAP : (n + 1) * CAP, 0:LAT] = row.astype(BF16)
    start(same(nz.at[xl]), "xnz")
    start(same(tm.at[xl]), "xtm")

    landed(kv.at[1 - xl, zy], "xkv", (mate, h))
    p1_other("kv")
    both(p2_send, "kv", 0)

    for f in (0, 1):

        @pl.when(xl == f)
        def _():
            sdn[...] = down_ref[:, (1 - f) * MAIN : (1 - f) * MAIN + DNW]
            dn[xl, dn_at] = down_ref[:, f * MAIN : f * MAIN + DNW]

    start(lambda: (sdn, dn.at[xl, dn_at], (mate, h)), "xdn")

    for j in range(GRP):
        cols = slice(j * HD, (j + 1) * HD)
        qs[cols, :] = q_ref[:, cols]
        dos[cols, :] = do_ref[:, cols]
        qt[:, cols] = q_ref[:, cols].astype(F32).T.astype(BF16)
        dot_t[:, cols] = do_ref[:, cols].astype(F32).T.astype(BF16)

    both(p1_fwd, "kv")
    both(p2_send, "kv", 1)
    both(p2_send, "kv", 3)
    landed(gu.at[1 - xl, zy], "xgu", (mate, h))
    p1_other("gu")

    steps = lax.broadcasted_iota(jnp.int32, (32, HALF), 0).astype(F32)
    for k, mult in ((0, 32.0), (2, 1.0)):
        angle = (steps * mult) * freq_ref[...]
        for kk, value in ((k, jnp.cos(angle)), (k + 1, jnp.sin(angle))):
            high = value.astype(BF16)
            rest = value - high.astype(F32)
            middle = rest.astype(BF16)
            tab[kk, 0:32, :] = high
            tab[kk, 32:64, :] = middle
            tab[kk, 64:96, :] = (rest - middle.astype(F32)).astype(BF16)
            tab[kk, 96:128, :] = jnp.zeros((32, HALF), BF16)

    both(p1_fin, "kv")
    both(p2_send, "kv", 2)
    for d in (0, 1, 3, 2):
        both(p2_fwd, "kv", d)
    both(p1_fwd, "gu")
    both(p2_send, "gu", 0)

    landed(nz.at[1 - xl], "xnz", (mate, h))
    landed(tm.at[1 - xl], "xtm", (mate, h))
    lane = lax.broadcasted_iota(jnp.int32, (CAP, 128), 1)
    for b in (0, 1):
        for n in range(NOISE):
            place = (n % 2) * 4 + (n // 2) * 2 + b
            rows = slice(place * CAP, (place + 1) * CAP)
            step = tm[b, :, n : n + 1]
            for ref, digit in ((oha, step >> 5), (ohb, step & 31)):
                ref[rows, :] = jnp.where((lane & 31) == digit, jnp.where(lane < 96, 1.0, 0.0), 0.0).astype(BF16)

    both(p2_send, "gu", 1)
    both(p2_send, "gu", 3)

    nz_rows = jnp.concatenate(
        [nz[g % 2, ((g // 2 % 2) * 2 + g // 4) * CAP : ((g // 2 % 2) * 2 + g // 4 + 1) * CAP, 0:LAT] for g in range(8)], axis=0
    )

    def embed(j, carry):
        c0 = pl.ds(pl.multiple_of(j * 256, 256), 256)
        c1 = pl.ds(pl.multiple_of(HALF + j * 256, 256), 256)
        noisy = nz_rows
        ca, sa = dot(oha[...], tab[0, :, c0]), dot(oha[...], tab[1, :, c0])
        cb, sb = dot(ohb[...], tab[2, :, c0]), dot(ohb[...], tab[3, :, c0])
        le[:, c0] = ca * cb - sa * sb + dot(noisy, lin_ref[:, c0])
        le[:, c1] = sa * cb + ca * sb + dot(noisy, lin_ref[:, c1])
        return carry

    lax.fori_loop(0, HALF // 256, embed, 0)

    for d in (0, 1, 3, 2):
        both(p2_fin, "kv", d)
    both(p1_fin, "gu")
    both(p2_send, "gu", 2)
    landed(dn.at[1 - xl, jnp.where(xl == 1, y * 4 + z, zy)], "xdn", (mate, h))
    both(p1_send, "dn")

    n_steps = lax.div(s, 2) + 1

    def keys_of(c):
        blocks = kv.at[lax.div(c, 8), pl.ds(lax.rem(c, 8) * 2, 2)]
        return blocks[:, 0:TOK, :].reshape(KC, HD), blocks[:, TOK : 2 * TOK, :].reshape(KC, HD)

    def scores_of(c, masked):
        score = dot(keys_of(c)[0], qt[...]) * (SCALE * LOG2E)
        if masked:
            key_pos = c * KC + lax.broadcasted_iota(jnp.int32, (KC, ROWS), 0)
            query_pos = s * TOK + (lax.broadcasted_iota(jnp.int32, (KC, ROWS), 1) & (TOK - 1))
            score = jnp.where(key_pos <= query_pos, score, NEG)
        return score

    def fold(values, reduce):
        return reduce(values.reshape(KC // 8, 8, ROWS), axis=0)

    def max_step(c, run, masked=False):
        return jnp.maximum(run, fold(scores_of(c, masked), jnp.max))

    row_max = lax.fori_loop(0, n_steps - 1, max_step, jnp.full((8, ROWS), NEG, F32))
    row_max = max_step(n_steps - 1, row_max, True)
    row_max = jnp.max(row_max, axis=0, keepdims=True)
    both(p2_fwd, "gu", 0)

    acc_t[...] = jnp.zeros_like(acc_t)

    def sum_step(c, run, masked=False):
        soft = jnp.exp2(scores_of(c, masked) - row_max)
        soft_b = soft.astype(BF16)
        probs[pl.ds(pl.multiple_of(c * KC, KC), KC), :] = soft_b
        acc_t[...] += contract_rows(keys_of(c)[1], soft_b)
        return run + fold(soft, jnp.sum)

    total = lax.fori_loop(0, n_steps - 1, sum_step, jnp.zeros((8, ROWS), F32))
    total = sum_step(n_steps - 1, total, True)
    total = jnp.sum(total, axis=0, keepdims=True)
    inverse = 1.0 / total
    out_t = (acc_t[...] / total).astype(BF16)
    delta = jnp.sum(out_t.astype(F32) * dot_t[...].astype(F32), axis=0, keepdims=True)
    for j in range(GRP):
        cols = slice(j * HD, (j + 1) * HD)
        out_ref[:, cols] = out_t[:, cols].astype(F32).T.astype(BF16)

    mask = mask_ref[...]
    ones = jnp.broadcast_to(mask.astype(F32), (8, TOK)).astype(BF16)
    before = lax.broadcasted_iota(jnp.int32, (TOK, TOK), 0) <= lax.broadcasted_iota(jnp.int32, (TOK, TOK), 1)
    rank = dot(ones, jnp.where(before, 1.0, 0.0).astype(BF16))[0:1, :] - 1.0
    slot = lax.broadcasted_iota(jnp.int32, (CAP, TOK), 0).astype(F32)
    chosen = jnp.where(rank == slot, jnp.where(mask == 1, 1.0, 0.0), 0.0)
    valid = jnp.sum(chosen, axis=1, keepdims=True) > 0.5
    cond[xl, h] = dot(chosen.astype(BF16), out_ref[...]).astype(BF16)
    cond_sent = []
    for i, (dx, dh) in enumerate(line):
        copy = pltpu.make_async_remote_copy(
            src_ref=cond.at[xl, h], dst_ref=cond.at[xl, h], send_sem=cssem.at[i],
            recv_sem=crsem.at[xl * N_HEAD + h], device_id=on_line(dx, dh)[2], device_id_type=MESH,
        )
        copy.start()
        cond_sent.append(copy)

    both(p2_fwd, "gu", 1)
    both(p1_fwd, "dn")
    both(p2_send, "dn", 0)

    acc_t[...] = jnp.zeros_like(acc_t)

    def grad_step(c, carry):
        keys, values = keys_of(c)
        prob = probs[pl.ds(pl.multiple_of(c * KC, KC), KC), :].astype(F32) * inverse
        ds = (prob * (dot(values, dot_t[...]) - delta)).astype(BF16)
        acc_t[...] += contract_rows(keys, ds)
        dkv[pl.ds(2 * c, 2), 0:TOK, :] = (dot(ds, qs[...]) * SCALE).astype(BF16).reshape(2, TOK, HD)
        dkv[pl.ds(2 * c, 2), TOK : 2 * TOK, :] = dot(prob.astype(BF16), dos[...]).astype(BF16).reshape(2, TOK, HD)
        return carry

    for part in range(4):
        lax.fori_loop(part * 4, jnp.minimum(n_steps, part * 4 + 4), grad_step, 0)
        if part == 0:
            both(p2_fwd, "gu", 3)
            both(p2_send, "dn", 1)
            both(p2_send, "dn", 3)
        elif part == 1:
            both(p2_fwd, "gu", 2)
            both(p1_fin, "dn")
            both(p2_send, "dn", 2)
        elif part == 2:
            both(p2_fwd, "dn", 0)

    for j in range(GRP):
        cols = slice(j * HD, (j + 1) * HD)
        dq_ref[:, cols] = (acc_t[:, cols] * SCALE).T.astype(BF16)

    for dx, dh in line:
        ox, oh, dev = on_line(dx, dh)
        pltpu.make_async_remote_copy(
            src_ref=cond.at[ox, oh], dst_ref=cond.at[ox, oh], send_sem=cssem.at[0],
            recv_sem=crsem.at[ox * N_HEAD + oh], device_id=dev, device_id_type=MESH,
        ).wait_recv()

    def norm_rows(g, carry):
        rows = pl.ds(pl.multiple_of(g * CAP, CAP), CAP)
        square = jnp.zeros((CAP, 1), F32)
        for hh in range(N_HEAD):
            cols = slice(hh * HEADW, (hh + 1) * HEADW)
            base = le[rows, cols] + cond[lax.rem(g, 2), hh].astype(F32)
            le[rows, cols] = base
            square += jnp.sum(base * base, axis=1, keepdims=True)
        scale = lax.rsqrt(square * (1.0 / D) + 1e-06)
        for hh in range(N_HEAD):
            cols = slice(hh * HEADW, (hh + 1) * HEADW)
            nm[rows, cols] = (le[rows, cols] * scale * ngain_ref[:, cols]).astype(BF16)
        return carry

    lax.fori_loop(0, 2 * NOISE, norm_rows, 0)
    both(p2_fwd, "dn", 1)
    for d in (0, 1, 3, 2):
        both(p2_fin, "gu", d)

    for k in range(4):
        piece = gu[k // 2, (k % 2) * 8 : (k % 2) * 8 + 8].reshape(8 * FEAT, GUW)
        part = dot(nm[:, k * 896 : (k + 1) * 896], piece)
        if k == 0:
            acc[...] = part
        else:
            acc[...] += part
        if k == 1:
            both(p2_fwd, "dn", 3)

    def silu(value):
        return value / (1.0 + jnp.exp(-value))

    both(p2_fwd, "dn", 2)
    mixed = acc[:, 2 * MAIN :]
    turned = pltpu.roll(mixed, 64, 1)
    lower_half = lax.broadcasted_iota(jnp.int32, (2 * NOISE * CAP, 128), 1) < 64

    @pl.when(xl == 0)
    def _():
        hid[:, 0:MAIN] = (silu(acc[:, 0:MAIN]) * acc[:, MAIN : 2 * MAIN]).astype(BF16)
        hid[:, MAIN:DNW] = jnp.where(lower_half, silu(mixed) * turned, 0.0).astype(BF16)

    @pl.when(xl == 1)
    def _():
        hid[:, 128:DNW] = (silu(acc[:, 0:MAIN]) * acc[:, MAIN : 2 * MAIN]).astype(BF16)
        hid[:, 0:128] = jnp.where(lower_half, 0.0, silu(turned) * mixed).astype(BF16)

    def term_copy(b, kb):
        return pltpu.make_async_remote_copy(
            src_ref=dkv.at[b * 16 + kb], dst_ref=drecv.at[b, zy], send_sem=dssem.at[b * 16 + kb],
            recv_sem=drsem.at[b * 16 + zy], device_id=(xl * 16 + kb, h), device_id_type=MESH,
        )

    def send_terms(kb, carry):
        pl.when((kb != zy) & ((xl == 1) | (kb < zy)))(lambda: term_copy(0, kb).start())
        pl.when((xl == 1) & (kb < zy))(lambda: term_copy(1, kb).start())
        return carry

    lax.fori_loop(0, 16, send_terms, 0)

    def add_terms(b):
        def step(i, run):
            pltpu.make_async_remote_copy(
                src_ref=drecv.at[b, i], dst_ref=drecv.at[b, i], send_sem=dssem.at[0], recv_sem=drsem.at[b * 16 + i],
                device_id=(mate, h), device_id_type=MESH,
            ).wait_recv()
            return run + drecv[b, i].astype(F32)

        return step

    def along_x(step):
        to = lax.rem(x + 4 + step, 4)
        return (lax.rem(to, 2) * 16 + zy, lax.div(to, 2) * 2 + core)

    def rows_of(place):
        return pl.ds(pl.multiple_of(place * CAP, CAP), CAP)

    def pick(step):
        return lax.rem(x + 4 + step, 4) * CAP

    SUB = 4 * FEAT
    order = (0, 1, 3, 2)

    def lanes(k):
        return slice(k * 512, k * 512 + SUB)

    def tot(k, r, step):
        first = pl.multiple_of(r * 256 + pick(step), CAP)
        return acc[pl.ds(first, CAP), lanes(k % 2)]

    sibling = (s, h + 1 - 2 * core)

    def stage0(k):
        for r in (0, 1):
            p2_fin("dn", r, order[k])
        pieces = []
        for r in (0, 1):
            at = back(y if r == 0 else z, order[k]) * 4
            piece = dn[r, pl.ds(at, 4)].reshape(SUB, DNW)
            pieces.append(piece)
            theirs = hid[pl.ds(pl.multiple_of((1 - core) * 256, 256), 256), :]
            part = lax.dot_general(theirs, piece, (((1,), (1,)), ((), ())), preferred_element_type=F32)
            s1[k, r] = part.astype(BF16)
            start(lambda r=r: (s1.at[k, r], r1.at[k, r], sibling), ("r1", k, r))
        for r in (0, 1):
            ours = hid[pl.ds(pl.multiple_of(core * 256, 256), 256), :]
            acc[r * 256 : r * 256 + 256, lanes(k % 2)] = lax.dot_general(ours, pieces[r], (((1,), (1,)), ((), ())), preferred_element_type=F32)

    def stage1(k):
        for r in (0, 1):
            landed(r1.at[k, r], ("r1", k, r), sibling)
            acc[r * 256 : r * 256 + 256, lanes(k % 2)] += r1[k, r].astype(F32)
            s23[0, k, r] = tot(k, r, 2).astype(BF16)
            start(lambda r=r: (s23.at[0, k, r], r2.at[k, r], along_x(1 - 2 * r)), ("r2", k, r))

    def stage2(k):
        for r in (0, 1):
            landed(r2.at[k, r], ("r2", k, r), along_x(1))
            for way, step in ((0, 1), (1, -1)):
                near = tot(k, r, step)
                if way == r:
                    near += r2[k, r].astype(F32)
                s23[1 + way, k, r] = near.astype(BF16)
                start(
                    lambda r=r, way=way, step=step: (s23.at[1 + way, k, r], r3.at[k, r, way], along_x(step)),
                    ("r3", k, r, way),
                )
            fin[r, back(y if r == 0 else z, order[k])] = tot(k, r, 0)

    def stage3(k):
        for r in (0, 1):
            at = back(y if r == 0 else z, order[k])
            for way in (0, 1):
                landed(r3.at[k, r, way], ("r3", k, r, way), along_x(1))
                fin[r, at] += r3[k, r, way].astype(F32)

    for k in range(6):
        if 2 <= k:
            stage2(k - 2)
        if k < 4:
            stage0(k)
        if 1 <= k < 5:
            stage1(k - 1)

    @pl.when(xl == 1)
    def _():
        run = lax.fori_loop(0, zy, add_terms(0), dkv[zy].astype(F32))
        run = lax.fori_loop(zy + 1, 16, add_terms(0), run)
        xterm[0] = run.astype(BF16)

    def cross():
        return xterm.at[0], xterm.at[1], (mate, h)

    pl.when(xl == 1)(lambda: copy_of(*cross()[:2], "xterm", cross()[2]).start())

    for k in range(4):
        stage3(k)

    def put_terms(run):
        dk_ref[...] = run[0:TOK].astype(BF16)
        dv_ref[...] = run[TOK : 2 * TOK].astype(BF16)

    @pl.when(xl == 1)
    def _():
        put_terms(lax.fori_loop(zy + 1, 16, add_terms(1), dkv[16 + zy].astype(F32)))

    own = rows_of(core * 4 + x)
    for at in range(4):
        for other in range(4):
            c0 = other * SUB + at * FEAT
            le[own, c0 : c0 + FEAT] += fin[0, at, :, other * FEAT : (other + 1) * FEAT]
        c1 = HALF + at * SUB
        le[own, c1 : c1 + SUB] += fin[1, at]
    square = jnp.zeros((CAP, 1), F32)
    for k in range(4):
        rows = le[own, k * 896 : (k + 1) * 896]
        square += jnp.sum(rows * rows, axis=1, keepdims=True)
    scale = lax.rsqrt(square * (1.0 / D) + 1e-06)
    result = jnp.zeros((CAP, LAT), F32)
    for k in range(4):
        cols = slice(k * 896, (k + 1) * 896)
        final = (le[own, cols] * scale * ogain_ref[:, cols]).astype(BF16)
        result += lax.dot_general(final, lout_ref[:, cols], (((1,), (1,)), ((), ())), preferred_element_type=F32)
    pred_ref[...] = jnp.where(valid, result, 0.0)

    @pl.when(xl == 0)
    def _():
        run = lax.fori_loop(zy + 1, 16, add_terms(0), dkv[zy].astype(F32))
        landed(xterm.at[1], "xterm", (mate, h))
        put_terms(run + xterm[1].astype(F32))

    all_left()
    pl.when(xl == 1)(lambda: copy_of(*cross()[:2], "xterm", cross()[2]).wait_send())
    for copy in cond_sent:
        copy.wait_send()

    def terms_left(kb, carry):
        pl.when((kb != zy) & ((xl == 1) | (kb < zy)))(lambda: term_copy(0, kb).wait_send())
        pl.when((xl == 1) & (kb < zy))(lambda: term_copy(1, kb).wait_send())
        return carry

    lax.fori_loop(0, 16, terms_left, 0)


def shards(
    queries, key_vectors, value_vectors, out_cotangent, latent_mask, clean_latents, noise_draws, timesteps,
    latent_in, norm_gain, gate_weight, up_weight, down_weight, out_gain, latent_out,
):
    frequencies = np.exp(-math.log(10000.0) * np.arange(HALF, dtype=np.float32) / HALF).astype(np.float32)
    vmem = pl.BlockSpec(memory_space=pltpu.VMEM)
    dma = pltpu.SemaphoreType.DMA
    n_sems = 176
    return pl.pallas_call(
        kernel,
        out_shape=(
            jax.ShapeDtypeStruct((TOK, ROWS), BF16),
            jax.ShapeDtypeStruct((TOK, ROWS), BF16),
            jax.ShapeDtypeStruct((TOK, HD), BF16),
            jax.ShapeDtypeStruct((TOK, HD), BF16),
            jax.ShapeDtypeStruct((CAP, LAT), F32),
        ),
        in_specs=[vmem] * 16,
        out_specs=(vmem,) * 5,
        scratch_shapes=[
            pltpu.VMEM((2, 16, 2 * TOK, HD), BF16),
            pltpu.VMEM((2, 16, FEAT, GUW), BF16),
            pltpu.VMEM((2, 16, FEAT, DNW), BF16),
            pltpu.VMEM((FEAT, GUW), BF16),
            pltpu.VMEM((FEAT, DNW), BF16),
            pltpu.VMEM((ROWS, HD), BF16),
            pltpu.VMEM((HD, ROWS), BF16),
            pltpu.VMEM((ROWS, HD), BF16),
            pltpu.VMEM((HD, ROWS), BF16),
            pltpu.VMEM((N_SEQ * TOK, ROWS), BF16),
            pltpu.VMEM((HD, ROWS), F32),
            pltpu.VMEM((N_SEQ, 2 * TOK, HD), BF16),
            pltpu.VMEM((2, 16, 2 * TOK, HD), BF16),
            pltpu.VMEM((2, N_HEAD, CAP, HEADW), BF16),
            pltpu.VMEM((2, NOISE * CAP, 128), BF16),
            pltpu.VMEM((2, CAP, 128), jnp.int32),
            pltpu.VMEM((4, 128, HALF), BF16),
            pltpu.VMEM((2 * NOISE * CAP, 128), BF16),
            pltpu.VMEM((2 * NOISE * CAP, 128), BF16),
            pltpu.VMEM((2 * NOISE * CAP, D), F32),
            pltpu.VMEM((2 * NOISE * CAP, D), BF16),
            pltpu.VMEM((2 * NOISE * CAP, GUW), F32),
            pltpu.VMEM((2 * NOISE * CAP, DNW), BF16),
            pltpu.VMEM((4, 2, 4 * CAP, 4 * FEAT), BF16),
            pltpu.VMEM((3, 4, 2, CAP, 4 * FEAT), BF16),
            pltpu.VMEM((4, 2, 4 * CAP, 4 * FEAT), BF16),
            pltpu.VMEM((4, 2, CAP, 4 * FEAT), BF16),
            pltpu.VMEM((4, 2, 2, CAP, 4 * FEAT), BF16),
            pltpu.VMEM((2, 4, CAP, 4 * FEAT), F32),
            pltpu.VMEM((2, 2 * TOK, HD), BF16),
            dma((n_sems,)),
            dma((n_sems,)),
            dma((N_SEQ,)),
            dma((N_SEQ,)),
            dma((7,)),
            dma((8,)),
        ],
        compiler_params=pltpu.CompilerParams(
            collective_id=0, has_side_effects=True, vmem_limit_bytes=63 * 1024 * 1024
        ),
    )(
        queries, key_vectors, value_vectors, out_cotangent, latent_mask.reshape(1, TOK), clean_latents, noise_draws,
        timesteps, latent_in, norm_gain.reshape(1, D), gate_weight, up_weight, down_weight, out_gain.reshape(1, D),
        latent_out.T, jnp.asarray(frequencies.reshape(1, HALF)),
    )


def solution(mesh):
    placed = (
        P("seq", "head"),
        P("seq", "head"),
        P("seq", "head"),
        P("seq", "head"),
        P("seq"),
        P("seq", None),
        P("seq", None),
        P("seq", None),
        P(),
        P(),
        P("seq", "head"),
        P("seq", "head"),
        P("seq", "head"),
        P(),
        P(),
    )
    return jax.shard_map(
        shards,
        mesh=mesh,
        in_specs=placed,
        out_specs=(P("seq", "head"),) * 5,
        check_vma=False,
    )
```

```python
import math

import jax
import jax.numpy as jnp
import numpy as np
from jax import lax
from jax.experimental import pallas as pl
from jax.experimental.pallas import tpu as pltpu
from jax.sharding import PartitionSpec as P

MESH = pl.DeviceIdType.MESH
F32 = jnp.float32
BF16 = jnp.bfloat16

HD = 128
GRP = 7
TOK = 128
ROWS = GRP * TOK
D = 3584
HALF = D // 2
LAT = 64
CAP = 64
NOISE = 4
N_SEQ = 32
N_HEAD = 4
FEAT = 112
GUW = 1408
DNW = 768
MAIN = 640
KC = 256
HEADW = D // N_HEAD
SCALE = 1.0 / math.sqrt(HD)
LOG2E = math.log2(math.e)
NEG = -1e30

HALVES = {"kv": ((0, 128), (128, 128)), "gu": ((0, 64), (64, 48)), "dn": ((0, 64), (64, 48))}


def contract_rows(left, right):
    return lax.dot_general(left, right, (((0,), (0,)), ((), ())), preferred_element_type=F32)


def dot(left, right):
    return jnp.dot(left, right, preferred_element_type=F32)


def kernel(
    q_ref, k_ref, v_ref, do_ref, mask_ref, clean_ref, noise_ref, time_ref, lin_ref, ngain_ref,
    gate_ref, up_ref, down_ref, ogain_ref, lout_ref, freq_ref,
    out_ref, dq_ref, dk_ref, dv_ref, pred_ref,
    kv, gu, dn, sgu, sdn, qs, qt, dos, dot_t, probs, acc_t, dkv, drecv, cond, nz, tm, tab, oha, ohb,
    le, nm, acc, hid, s1, s23, r1, r2, r3, fin, xterm, mterm,
    ssem, rsem, dssem, drsem, cssem, crsem, xssem, xrsem,
):
    s = lax.axis_index("seq")
    h = lax.axis_index("head")
    xl = lax.div(s, 16)
    zy = lax.rem(s, 16)
    core = lax.rem(h, 2)
    x = lax.div(h, 2) * 2 + xl
    z = lax.div(zy, 4)
    y = lax.rem(zy, 4)
    mate = (1 - xl) * 16 + zy

    bufs = {"kv": kv, "gu": gu, "dn": dn}
    sem_at = {}
    leaving = {}

    def copy_of(src, dst, key, dev):
        at = sem_at.setdefault(key, len(sem_at))
        return pltpu.make_async_remote_copy(
            src_ref=src, dst_ref=dst, send_sem=ssem.at[at], recv_sem=rsem.at[at], device_id=dev, device_id_type=MESH
        )

    def start(make, key):
        src, dst, dev = make()
        copy_of(src, dst, key, dev).start()
        leaving[key] = make

    def landed(dst, key, dev):
        copy_of(dst, dst, key, dev).wait_recv()

    def all_left():
        for key, make in leaving.items():
            src, dst, dev = make()
            copy_of(src, dst, key, dev).wait_send()

    def back(pos, dist):
        return lax.rem(pos + 4 - dist, 4)

    def chunk(p, r, d1, d2, half):
        dy, dz = (d1, d2) if r == 0 else (d2, d1)
        pz, py = back(z, dz), back(y, dy)
        view = bufs[p].at[r, py * 4 + pz if p == "dn" and r == 0 else pz * 4 + py]
        if half is None:
            return view
        first, count = HALVES[p][half]
        return view.at[pl.ds(first, count)]

    def neighbour(r, axis, step):
        along_y = (axis == 1) == (r == 0)
        if along_y:
            return (xl * 16 + z * 4 + back(y, -step), h)
        return (xl * 16 + back(z, -step) * 4 + y, h)

    def send(p, r, d1, d2, axis, step, half=None):
        e1 = (d1 + step) % 4 if axis == 1 else d1
        e2 = (d2 + step) % 4 if axis == 2 else d2

        def make():
            ref = chunk(p, r, d1, d2, half)
            return ref, ref, neighbour(r, axis, step)

        start(make, (p, r, e1, e2, half))

    def wait(p, r, d1, d2, half=None):
        landed(chunk(p, r, d1, d2, half), (p, r, d1, d2, half), (mate, h))

    def p1_send(p, r):
        send(p, r, 0, 0, 1, 1)
        send(p, r, 0, 0, 1, -1)

    def first_sends(p, r):
        p1_send(p, r)
        p2_send(p, r, 0)

    def own(step, p, *rest):
        for r in (0, 1):
            pl.when(xl == r)(lambda r=r: step(p, r, *rest))

    def other(step, p, *rest):
        for r in (0, 1):
            pl.when(xl != r)(lambda r=r: step(p, r, *rest))

    def p1_fwd(p, r):
        wait(p, r, 1, 0)
        send(p, r, 1, 0, 1, 1, 0)
        wait(p, r, 3, 0)
        send(p, r, 3, 0, 1, -1, 1)

    def p1_fin(p, r):
        wait(p, r, 2, 0, 0)
        wait(p, r, 2, 0, 1)

    def p2_send(p, r, d1):
        send(p, r, d1, 0, 2, 1)
        send(p, r, d1, 0, 2, -1)

    def p2_fwd(p, r, d1):
        wait(p, r, d1, 1)
        send(p, r, d1, 1, 2, 1, d1 % 2)
        wait(p, r, d1, 3)
        send(p, r, d1, 3, 2, -1, 1 - d1 % 2)

    def p2_fin(p, r, d1):
        wait(p, r, d1, 2, 0)
        wait(p, r, d1, 2, 1)

    def both(step, p, *rest):
        step(p, 0, *rest)
        step(p, 1, *rest)

    barrier = pltpu.get_barrier_semaphore()

    line = [(dx, dh) for dx in (0, 1) for dh in range(N_HEAD) if (dx, dh) != (0, 0)]

    def on_line(dx, dh):
        ox = lax.rem(xl + dx, 2)
        oh = lax.rem(h + dh, N_HEAD)
        return ox, oh, (ox * 16 + zy, oh)

    for dx, dh in line:
        pl.semaphore_signal(barrier, inc=1, device_id=on_line(dx, dh)[2], device_id_type=MESH)
    for axis in (1, 2):
        for step in (1, -1):
            pl.semaphore_signal(barrier, inc=1, device_id=neighbour(0, axis, step), device_id_type=MESH)
    pl.semaphore_wait(barrier, 7 + 4)

    low = lax.broadcasted_iota(jnp.int32, (FEAT, 128), 1) < 64

    def pack_gu(f, put):
        at = f * 768
        mid_gate = gate_ref[:, MAIN : MAIN + 128].astype(F32)
        mid_up = up_ref[:, MAIN : MAIN + 128].astype(F32)
        if f == 0:
            mixed = jnp.where(low, mid_gate, pltpu.roll(mid_up, 64, 1))
        else:
            mixed = jnp.where(low, pltpu.roll(mid_gate, 64, 1), mid_up)
        put(0, gate_ref[:, at : at + MAIN])
        put(MAIN, up_ref[:, at : at + MAIN])
        put(2 * MAIN, mixed.astype(BF16))

    def own_gu(at, value):
        gu[xl, zy, :, at : at + value.shape[1]] = value

    def mate_gu(at, value):
        sgu[:, at : at + value.shape[1]] = value

    def same(ref):
        return lambda: (ref, ref, (mate, h))

    dn_at = jnp.where(xl == 0, y * 4 + z, zy)
    kv[xl, zy, 0:TOK, :] = k_ref[...]
    kv[xl, zy, TOK : 2 * TOK, :] = v_ref[...]
    start(same(kv.at[xl, zy]), "xkv")
    own(first_sends, "kv")
    for f in (0, 1):
        pl.when(xl == f)(lambda f=f: pack_gu(f, own_gu))
    own(first_sends, "gu")
    for f in (0, 1):
        pl.when(xl == f)(lambda f=f: pack_gu(1 - f, mate_gu))
    start(lambda: (sgu, gu.at[xl, zy], (mate, h)), "xgu")
    landed(kv.at[1 - xl, zy], "xkv", (mate, h))
    other(first_sends, "kv")
    own(p1_fwd, "kv")
    own(p2_send, "kv", 1)
    own(p2_send, "kv", 3)

    for f in (0, 1):

        @pl.when(xl == f)
        def _():
            sdn[...] = down_ref[:, (1 - f) * MAIN : (1 - f) * MAIN + DNW]
            dn[xl, dn_at] = down_ref[:, f * MAIN : f * MAIN + DNW]

    start(lambda: (sdn, dn.at[xl, dn_at], (mate, h)), "xdn")

    digits = jnp.concatenate([time_ref[...] >> 5, time_ref[...] & 31], axis=0).astype(F32).astype(BF16)
    unit = lax.broadcasted_iota(jnp.int32, (2 * NOISE, 128), 0) == lax.broadcasted_iota(jnp.int32, (2 * NOISE, 128), 1)
    columns = contract_rows(digits, jnp.where(unit, 1.0, 0.0).astype(BF16))
    steps_own = columns[:, 0:NOISE] * 32.0 + columns[:, NOISE : 2 * NOISE]
    share = jnp.cos((steps_own / 1000.0 + 0.008) / 1.008 * (math.pi / 2.0)) ** 2
    signal, noise_part = jnp.sqrt(share), jnp.sqrt(1.0 - share)
    nz[xl] = jnp.zeros((NOISE * CAP, 128), BF16)
    tm[xl] = columns.astype(jnp.int32)
    for n in range(NOISE):
        row = signal[:, n : n + 1] * clean_ref[...] + noise_part[:, n : n + 1] * noise_ref[:, n * LAT : (n + 1) * LAT]
        nz[xl, n * CAP : (n + 1) * CAP, 0:LAT] = row.astype(BF16)
    start(same(nz.at[xl]), "xnz")
    start(same(tm.at[xl]), "xtm")


    for j in range(GRP):
        cols = slice(j * HD, (j + 1) * HD)
        qs[cols, :] = q_ref[:, cols]
        dos[cols, :] = do_ref[:, cols]
        qt[:, cols] = q_ref[:, cols].astype(F32).T.astype(BF16)
        dot_t[:, cols] = do_ref[:, cols].astype(F32).T.astype(BF16)

    landed(gu.at[1 - xl, zy], "xgu", (mate, h))
    other(first_sends, "gu")
    other(p1_fwd, "kv")
    other(p2_send, "kv", 1)
    other(p2_send, "kv", 3)
    both(p1_fin, "kv")
    both(p2_send, "kv", 2)
    own(p1_fwd, "gu")
    own(p2_send, "gu", 1)

    steps = lax.broadcasted_iota(jnp.int32, (32, HALF), 0).astype(F32)
    for k, mult in ((0, 32.0), (2, 1.0)):
        angle = (steps * mult) * freq_ref[...]
        for kk, value in ((k, jnp.cos(angle)), (k + 1, jnp.sin(angle))):
            high = value.astype(BF16)
            rest = value - high.astype(F32)
            middle = rest.astype(BF16)
            tab[kk, 0:32, :] = high
            tab[kk, 32:64, :] = middle
            tab[kk, 64:96, :] = (rest - middle.astype(F32)).astype(BF16)
            tab[kk, 96:128, :] = jnp.zeros((32, HALF), BF16)

    both(p2_fwd, "kv", 0)
    both(p2_fwd, "kv", 1)
    own(p2_send, "gu", 3)
    both(p2_fwd, "kv", 3)
    both(p2_fwd, "kv", 2)
    own(p1_fin, "gu")
    other(p1_fwd, "gu")
    other(p2_send, "gu", 1)
    own(p2_send, "gu", 2)
    other(p2_send, "gu", 3)

    landed(nz.at[1 - xl], "xnz", (mate, h))
    landed(tm.at[1 - xl], "xtm", (mate, h))
    lane = lax.broadcasted_iota(jnp.int32, (CAP, 128), 1)
    for b in (0, 1):
        for n in range(NOISE):
            place = (n % 2) * 4 + (n // 2) * 2 + b
            rows = slice(place * CAP, (place + 1) * CAP)
            for ref, digit in ((oha, tm[b, :, n : n + 1]), (ohb, tm[b, :, NOISE + n : NOISE + n + 1])):
                ref[rows, :] = jnp.where((lane & 31) == digit, jnp.where(lane < 96, 1.0, 0.0), 0.0).astype(BF16)

    nz_rows = jnp.concatenate(
        [nz[g % 2, ((g // 2 % 2) * 2 + g // 4) * CAP : ((g // 2 % 2) * 2 + g // 4 + 1) * CAP, 0:LAT] for g in range(8)], axis=0
    )

    def embed(j, carry):
        c0 = pl.ds(pl.multiple_of(j * 256, 256), 256)
        c1 = pl.ds(pl.multiple_of(HALF + j * 256, 256), 256)
        noisy = nz_rows
        ca, sa = dot(oha[...], tab[0, :, c0]), dot(oha[...], tab[1, :, c0])
        cb, sb = dot(ohb[...], tab[2, :, c0]), dot(ohb[...], tab[3, :, c0])
        le[:, c0] = ca * cb - sa * sb + dot(noisy, lin_ref[:, c0])
        le[:, c1] = sa * cb + ca * sb + dot(noisy, lin_ref[:, c1])
        return carry

    lax.fori_loop(0, HALF // 256, embed, 0)

    other(p1_fin, "gu")
    other(p2_send, "gu", 2)
    landed(dn.at[1 - xl, jnp.where(xl == 1, y * 4 + z, zy)], "xdn", (mate, h))
    both(p1_send, "dn")
    both(p2_fwd, "gu", 0)
    for d in (0, 1, 3, 2):
        both(p2_fin, "kv", d)

    n_steps = lax.div(s, 2) + 1

    def keys_of(c):
        blocks = kv.at[lax.div(c, 8), pl.ds(lax.rem(c, 8) * 2, 2)]
        return blocks[:, 0:TOK, :].reshape(KC, HD), blocks[:, TOK : 2 * TOK, :].reshape(KC, HD)

    def scores_of(c, masked):
        score = dot(keys_of(c)[0], qt[...]) * (SCALE * LOG2E)
        if masked:
            key_pos = c * KC + lax.broadcasted_iota(jnp.int32, (KC, ROWS), 0)
            query_pos = s * TOK + (lax.broadcasted_iota(jnp.int32, (KC, ROWS), 1) & (TOK - 1))
            score = jnp.where(key_pos <= query_pos, score, NEG)
        return score

    def fold(values, reduce):
        return reduce(values.reshape(KC // 8, 8, ROWS), axis=0)

    def max_step(c, run, masked=False):
        return jnp.maximum(run, fold(scores_of(c, masked), jnp.max))

    row_max = lax.fori_loop(0, n_steps - 1, max_step, jnp.full((8, ROWS), NEG, F32))
    row_max = max_step(n_steps - 1, row_max, True)
    row_max = jnp.max(row_max, axis=0, keepdims=True)
    both(p2_fwd, "gu", 1)
    both(p1_fwd, "dn")

    acc_t[...] = jnp.zeros_like(acc_t)

    def sum_step(c, run, masked=False):
        soft = jnp.exp2(scores_of(c, masked) - row_max)
        soft_b = soft.astype(BF16)
        probs[pl.ds(pl.multiple_of(c * KC, KC), KC), :] = soft_b
        acc_t[...] += contract_rows(keys_of(c)[1], soft_b)
        return run + fold(soft, jnp.sum)

    total = lax.fori_loop(0, n_steps - 1, sum_step, jnp.zeros((8, ROWS), F32))
    total = sum_step(n_steps - 1, total, True)
    total = jnp.sum(total, axis=0, keepdims=True)
    inverse = 1.0 / total
    out_t = (acc_t[...] / total).astype(BF16)
    delta = jnp.sum(out_t.astype(F32) * dot_t[...].astype(F32), axis=0, keepdims=True)
    for j in range(GRP):
        cols = slice(j * HD, (j + 1) * HD)
        out_ref[:, cols] = out_t[:, cols].astype(F32).T.astype(BF16)

    mask = mask_ref[...]
    ones = jnp.broadcast_to(mask.astype(F32), (8, TOK)).astype(BF16)
    before = lax.broadcasted_iota(jnp.int32, (TOK, TOK), 0) <= lax.broadcasted_iota(jnp.int32, (TOK, TOK), 1)
    rank = dot(ones, jnp.where(before, 1.0, 0.0).astype(BF16))[0:1, :] - 1.0
    slot = lax.broadcasted_iota(jnp.int32, (CAP, TOK), 0).astype(F32)
    chosen = jnp.where(rank == slot, jnp.where(mask == 1, 1.0, 0.0), 0.0)
    valid = jnp.sum(chosen, axis=1, keepdims=True) > 0.5
    cond[xl, h] = dot(chosen.astype(BF16), out_ref[...]).astype(BF16)
    cond_sent = []
    for i, (dx, dh) in enumerate(line):
        copy = pltpu.make_async_remote_copy(
            src_ref=cond.at[xl, h], dst_ref=cond.at[xl, h], send_sem=cssem.at[i],
            recv_sem=crsem.at[xl * N_HEAD + h], device_id=on_line(dx, dh)[2], device_id_type=MESH,
        )
        copy.start()
        cond_sent.append(copy)

    both(p2_fwd, "gu", 3)
    both(p2_send, "dn", 0)

    acc_t[...] = jnp.zeros_like(acc_t)

    def grad_step(c, carry):
        keys, values = keys_of(c)
        prob = probs[pl.ds(pl.multiple_of(c * KC, KC), KC), :].astype(F32) * inverse
        ds = (prob * (dot(values, dot_t[...]) - delta)).astype(BF16)
        acc_t[...] += contract_rows(keys, ds)
        dkv[pl.ds(2 * c, 2), 0:TOK, :] = (dot(ds, qs[...]) * SCALE).astype(BF16).reshape(2, TOK, HD)
        dkv[pl.ds(2 * c, 2), TOK : 2 * TOK, :] = dot(prob.astype(BF16), dos[...]).astype(BF16).reshape(2, TOK, HD)
        return carry

    def crosses(kb):
        return (kb < zy) | ((kb > zy) & (lax.rem(kb + zy, 2) == 1))

    def cross_copy(kb):
        return pltpu.make_async_remote_copy(
            src_ref=dkv.at[kb], dst_ref=mterm.at[kb], send_sem=xssem.at[kb], recv_sem=xrsem.at[kb],
            device_id=(mate, h), device_id_type=MESH,
        )

    for part in range(4):
        lax.fori_loop(part * 4, jnp.minimum(n_steps, part * 4 + 4), grad_step, 0)
        if part == 0:
            both(p2_fwd, "gu", 2)
            both(p2_send, "dn", 1)
            both(p2_send, "dn", 3)
        elif part == 1:
            both(p1_fin, "dn")
            both(p2_send, "dn", 2)

            def send_cross(kb, carry):
                pl.when((xl == 1) & crosses(kb))(lambda: cross_copy(kb).start())
                return carry

            lax.fori_loop(0, 16, send_cross, 0)
        elif part == 2:
            both(p2_fwd, "dn", 0)

    for j in range(GRP):
        cols = slice(j * HD, (j + 1) * HD)
        dq_ref[:, cols] = (acc_t[:, cols] * SCALE).T.astype(BF16)

    for dx, dh in line:
        ox, oh, dev = on_line(dx, dh)
        pltpu.make_async_remote_copy(
            src_ref=cond.at[ox, oh], dst_ref=cond.at[ox, oh], send_sem=cssem.at[0],
            recv_sem=crsem.at[ox * N_HEAD + oh], device_id=dev, device_id_type=MESH,
        ).wait_recv()

    def norm_rows(g, carry):
        rows = pl.ds(pl.multiple_of(g * CAP, CAP), CAP)
        square = jnp.zeros((CAP, 1), F32)
        for hh in range(N_HEAD):
            cols = slice(hh * HEADW, (hh + 1) * HEADW)
            base = le[rows, cols] + cond[lax.rem(g, 2), hh].astype(F32)
            le[rows, cols] = base
            square += jnp.sum(base * base, axis=1, keepdims=True)
        scale = lax.rsqrt(square * (1.0 / D) + 1e-06)
        for hh in range(N_HEAD):
            cols = slice(hh * HEADW, (hh + 1) * HEADW)
            nm[rows, cols] = (le[rows, cols] * scale * ngain_ref[cols].reshape(1, HEADW)).astype(BF16)
        return carry

    lax.fori_loop(0, 2 * NOISE, norm_rows, 0)
    for d in (0, 1, 3, 2):
        both(p2_fin, "gu", d)

    for k in range(4):
        piece = gu[k // 2, (k % 2) * 8 : (k % 2) * 8 + 8].reshape(8 * FEAT, GUW)
        part = dot(nm[:, k * 896 : (k + 1) * 896], piece)
        if k == 0:
            acc[...] = part
        else:
            acc[...] += part
        if k == 1:
            both(p2_fwd, "dn", 1)

    def silu(value):
        return value / (1.0 + jnp.exp(-value))

    mixed = acc[:, 2 * MAIN :]
    turned = pltpu.roll(mixed, 64, 1)
    lower_half = lax.broadcasted_iota(jnp.int32, (2 * NOISE * CAP, 128), 1) < 64

    @pl.when(xl == 0)
    def _():
        hid[:, 0:MAIN] = (silu(acc[:, 0:MAIN]) * acc[:, MAIN : 2 * MAIN]).astype(BF16)
        hid[:, MAIN:DNW] = jnp.where(lower_half, silu(mixed) * turned, 0.0).astype(BF16)

    @pl.when(xl == 1)
    def _():
        hid[:, 128:DNW] = (silu(acc[:, 0:MAIN]) * acc[:, MAIN : 2 * MAIN]).astype(BF16)
        hid[:, 0:128] = jnp.where(lower_half, 0.0, silu(turned) * mixed).astype(BF16)

    def term_copy(b, kb):
        return pltpu.make_async_remote_copy(
            src_ref=dkv.at[b * 16 + kb], dst_ref=drecv.at[b, zy], send_sem=dssem.at[b * 16 + kb],
            recv_sem=drsem.at[b * 16 + zy], device_id=(xl * 16 + kb, h), device_id_type=MESH,
        )

    def forward_copy(kb):
        return pltpu.make_async_remote_copy(
            src_ref=mterm.at[kb], dst_ref=drecv.at[0, zy], send_sem=dssem.at[kb], recv_sem=drsem.at[zy],
            device_id=(kb, h), device_id_type=MESH,
        )

    def join_terms(kb, carry):
        cross_copy(kb).wait_recv()
        mterm[kb] = (mterm[kb].astype(F32) + dkv[kb].astype(F32)).astype(BF16)
        forward_copy(kb).start()
        return carry

    def pass_terms(kb, carry):
        @pl.when(lax.rem(kb + zy, 2) == 1)
        def _():
            cross_copy(kb).wait_recv()
            forward_copy(kb).start()

        return carry

    def send_terms(kb, carry):
        pl.when((kb > zy) & (lax.rem(kb + zy, 2) == 0))(lambda: term_copy(0, kb).start())
        pl.when(kb < zy)(lambda: term_copy(1, kb).start())
        return carry

    def all_terms():
        @pl.when(xl == 0)
        def _():
            lax.fori_loop(0, zy, join_terms, 0)
            lax.fori_loop(zy + 1, 16, pass_terms, 0)

        @pl.when(xl == 1)
        def _():
            lax.fori_loop(0, 16, send_terms, 0)

    def add_terms(b):
        def step(i, run):
            pltpu.make_async_remote_copy(
                src_ref=drecv.at[b, i], dst_ref=drecv.at[b, i], send_sem=dssem.at[0], recv_sem=drsem.at[b * 16 + i],
                device_id=(mate, h), device_id_type=MESH,
            ).wait_recv()
            return run + drecv[b, i].astype(F32)

        return step

    def add_alternate(parity):
        def step(i, run):
            return lax.cond(lax.rem(i + zy, 2) == parity, lambda value: add_terms(0)(i, value), lambda value: value, run)

        return step

    def along_x(step):
        to = lax.rem(x + 4 + step, 4)
        return (lax.rem(to, 2) * 16 + zy, lax.div(to, 2) * 2 + core)

    def rows_of(place):
        return pl.ds(pl.multiple_of(place * CAP, CAP), CAP)

    def pick(step):
        return lax.rem(x + 4 + step, 4) * CAP

    SUB = 4 * FEAT
    order = (0, 1, 3, 2)

    def lanes(k):
        return slice(k * 512, k * 512 + SUB)

    def tot(k, r, step):
        first = pl.multiple_of(r * 256 + pick(step), CAP)
        return acc[pl.ds(first, CAP), lanes(k % 2)]

    sibling = (s, h + 1 - 2 * core)

    def stage0(k):
        for r in (0, 1):
            p2_fin("dn", r, order[k])
        pieces = []
        for r in (0, 1):
            at = back(y if r == 0 else z, order[k]) * 4
            piece = dn[r, pl.ds(at, 4)].reshape(SUB, DNW)
            pieces.append(piece)
            theirs = hid[pl.ds(pl.multiple_of((1 - core) * 256, 256), 256), :]
            part = lax.dot_general(theirs, piece, (((1,), (1,)), ((), ())), preferred_element_type=F32)
            s1[k, r] = part.astype(BF16)
            start(lambda r=r: (s1.at[k, r], r1.at[k, r], sibling), ("r1", k, r))
        for r in (0, 1):
            ours = hid[pl.ds(pl.multiple_of(core * 256, 256), 256), :]
            acc[r * 256 : r * 256 + 256, lanes(k % 2)] = lax.dot_general(ours, pieces[r], (((1,), (1,)), ((), ())), preferred_element_type=F32)

    def stage1(k):
        for r in (0, 1):
            landed(r1.at[k, r], ("r1", k, r), sibling)
            acc[r * 256 : r * 256 + 256, lanes(k % 2)] += r1[k, r].astype(F32)
            s23[0, k, r] = tot(k, r, 2).astype(BF16)
            start(lambda r=r: (s23.at[0, k, r], r2.at[k, r], along_x(1 - 2 * r)), ("r2", k, r))

    def stage2(k):
        for r in (0, 1):
            landed(r2.at[k, r], ("r2", k, r), along_x(1))
            for way, step in ((0, 1), (1, -1)):
                near = tot(k, r, step)
                if way == r:
                    near += r2[k, r].astype(F32)
                s23[1 + way, k, r] = near.astype(BF16)
                start(
                    lambda r=r, way=way, step=step: (s23.at[1 + way, k, r], r3.at[k, r, way], along_x(step)),
                    ("r3", k, r, way),
                )
            fin[r, back(y if r == 0 else z, order[k])] = tot(k, r, 0)

    def stage3(k):
        for r in (0, 1):
            at = back(y if r == 0 else z, order[k])
            for way in (0, 1):
                landed(r3.at[k, r, way], ("r3", k, r, way), along_x(1))
                fin[r, at] += r3[k, r, way].astype(F32)

    for k in range(6):
        if 2 <= k:
            stage2(k - 2)
        if k < 4:
            stage0(k)
        if k < 2:
            both(p2_fwd, "dn", order[k + 2])
        if k == 1:
            all_terms()
        if 1 <= k < 5:
            stage1(k - 1)

    @pl.when(xl == 1)
    def _():
        xterm[0] = lax.fori_loop(0, zy, add_alternate(0), dkv[zy].astype(F32)).astype(BF16)

    def cross():
        return xterm.at[0], xterm.at[1], (mate, h)

    pl.when(xl == 1)(lambda: copy_of(*cross()[:2], "xterm", cross()[2]).start())

    for k in range(4):
        stage3(k)

    def put_terms(run):
        dk_ref[...] = run[0:TOK].astype(BF16)
        dv_ref[...] = run[TOK : 2 * TOK].astype(BF16)

    @pl.when(xl == 1)
    def _():
        put_terms(lax.fori_loop(zy + 1, 16, add_terms(1), dkv[16 + zy].astype(F32)))

    own = rows_of(core * 4 + x)
    for at in range(4):
        for other in range(4):
            c0 = other * SUB + at * FEAT
            le[own, c0 : c0 + FEAT] += fin[0, at, :, other * FEAT : (other + 1) * FEAT]
        c1 = HALF + at * SUB
        le[own, c1 : c1 + SUB] += fin[1, at]
    square = jnp.zeros((CAP, 1), F32)
    for k in range(4):
        rows = le[own, k * 896 : (k + 1) * 896]
        square += jnp.sum(rows * rows, axis=1, keepdims=True)
    scale = lax.rsqrt(square * (1.0 / D) + 1e-06)
    result = jnp.zeros((CAP, LAT), F32)
    for k in range(4):
        cols = slice(k * 896, (k + 1) * 896)
        final = (le[own, cols] * scale * ogain_ref[cols].reshape(1, 896)).astype(BF16)
        result += lax.dot_general(final, lout_ref[:, cols], (((1,), (1,)), ((), ())), preferred_element_type=F32)
    pred_ref[...] = jnp.where(valid, result, 0.0)

    @pl.when(xl == 0)
    def _():
        run = lax.fori_loop(zy + 1, 16, add_terms(0), dkv[zy].astype(F32))
        run = lax.fori_loop(0, zy, add_alternate(1), run)
        landed(xterm.at[1], "xterm", (mate, h))
        put_terms(run + xterm[1].astype(F32))

    all_left()
    pl.when(xl == 1)(lambda: copy_of(*cross()[:2], "xterm", cross()[2]).wait_send())
    for copy in cond_sent:
        copy.wait_send()

    def terms_left(kb, carry):
        pl.when((xl == 1) & crosses(kb))(lambda: cross_copy(kb).wait_send())
        pl.when((xl == 0) & crosses(kb))(lambda: forward_copy(kb).wait_send())
        pl.when((xl == 1) & (kb > zy) & (lax.rem(kb + zy, 2) == 0))(lambda: term_copy(0, kb).wait_send())
        pl.when((xl == 1) & (kb < zy))(lambda: term_copy(1, kb).wait_send())
        return carry

    lax.fori_loop(0, 16, terms_left, 0)


def hand_over(*refs):
    for i in range(5):
        refs[5 + i][...] = refs[i][...]


def shards(
    queries, key_vectors, value_vectors, out_cotangent, latent_mask, clean_latents, noise_draws, timesteps,
    latent_in, norm_gain, gate_weight, up_weight, down_weight, out_gain, latent_out,
):
    frequencies = np.exp(-math.log(10000.0) * np.arange(HALF, dtype=np.float32) / HALF).astype(np.float32)
    vmem = pl.BlockSpec(memory_space=pltpu.VMEM)
    dma = pltpu.SemaphoreType.DMA
    n_sems = 176
    results = pl.pallas_call(
        kernel,
        out_shape=(
            jax.ShapeDtypeStruct((TOK, ROWS), BF16),
            jax.ShapeDtypeStruct((TOK, ROWS), BF16),
            jax.ShapeDtypeStruct((TOK, HD), BF16),
            jax.ShapeDtypeStruct((TOK, HD), BF16),
            jax.ShapeDtypeStruct((CAP, LAT), F32),
        ),
        in_specs=[vmem] * 16,
        out_specs=(vmem,) * 5,
        scratch_shapes=[
            pltpu.VMEM((2, 16, 2 * TOK, HD), BF16),
            pltpu.VMEM((2, 16, FEAT, GUW), BF16),
            pltpu.VMEM((2, 16, FEAT, DNW), BF16),
            pltpu.VMEM((FEAT, GUW), BF16),
            pltpu.VMEM((FEAT, DNW), BF16),
            pltpu.VMEM((ROWS, HD), BF16),
            pltpu.VMEM((HD, ROWS), BF16),
            pltpu.VMEM((ROWS, HD), BF16),
            pltpu.VMEM((HD, ROWS), BF16),
            pltpu.VMEM((N_SEQ * TOK, ROWS), BF16),
            pltpu.VMEM((HD, ROWS), F32),
            pltpu.VMEM((N_SEQ, 2 * TOK, HD), BF16),
            pltpu.VMEM((2, 16, 2 * TOK, HD), BF16),
            pltpu.VMEM((2, N_HEAD, CAP, HEADW), BF16),
            pltpu.VMEM((2, NOISE * CAP, 128), BF16),
            pltpu.VMEM((2, CAP, 128), jnp.int32),
            pltpu.VMEM((4, 128, HALF), BF16),
            pltpu.VMEM((2 * NOISE * CAP, 128), BF16),
            pltpu.VMEM((2 * NOISE * CAP, 128), BF16),
            pltpu.VMEM((2 * NOISE * CAP, D), F32),
            pltpu.VMEM((2 * NOISE * CAP, D), BF16),
            pltpu.VMEM((2 * NOISE * CAP, GUW), F32),
            pltpu.VMEM((2 * NOISE * CAP, DNW), BF16),
            pltpu.VMEM((4, 2, 4 * CAP, 4 * FEAT), BF16),
            pltpu.VMEM((3, 4, 2, CAP, 4 * FEAT), BF16),
            pltpu.VMEM((4, 2, 4 * CAP, 4 * FEAT), BF16),
            pltpu.VMEM((4, 2, CAP, 4 * FEAT), BF16),
            pltpu.VMEM((4, 2, 2, CAP, 4 * FEAT), BF16),
            pltpu.VMEM((2, 4, CAP, 4 * FEAT), F32),
            pltpu.VMEM((2, 2 * TOK, HD), BF16),
            pltpu.VMEM((16, 2 * TOK, HD), BF16),
            dma((n_sems,)),
            dma((n_sems,)),
            dma((N_SEQ,)),
            dma((N_SEQ,)),
            dma((7,)),
            dma((8,)),
            dma((16,)),
            dma((16,)),
        ],
        compiler_params=pltpu.CompilerParams(
            collective_id=0, has_side_effects=True, vmem_limit_bytes=63 * 1024 * 1024
        ),
    )(
        queries, key_vectors, value_vectors, out_cotangent, latent_mask.reshape(1, TOK), clean_latents, noise_draws,
        timesteps.T, latent_in, norm_gain, gate_weight, up_weight, down_weight, out_gain,
        latent_out.T, jnp.asarray(frequencies.reshape(1, HALF)),
    )
    return pl.pallas_call(
        hand_over,
        out_shape=tuple(jax.ShapeDtypeStruct(a.shape, a.dtype) for a in results),
        in_specs=[vmem] * 5,
        out_specs=(vmem,) * 5,
        compiler_params=pltpu.CompilerParams(vmem_limit_bytes=63 * 1024 * 1024),
    )(*results)


def solution(mesh):
    placed = (
        P("seq", "head"),
        P("seq", "head"),
        P("seq", "head"),
        P("seq", "head"),
        P("seq"),
        P("seq", None),
        P("seq", None),
        P("seq", None),
        P(),
        P(),
        P("seq", "head"),
        P("seq", "head"),
        P("seq", "head"),
        P(),
        P(),
    )
    return jax.shard_map(
        shards,
        mesh=mesh,
        in_specs=placed,
        out_specs=(P("seq", "head"),) * 5,
        check_vma=False,
    )
```

```python
import math

import jax
import jax.numpy as jnp
import numpy as np
from jax import lax
from jax.experimental import pallas as pl
from jax.experimental.pallas import tpu as pltpu
from jax.sharding import PartitionSpec as P

MESH = pl.DeviceIdType.MESH
F32 = jnp.float32
BF16 = jnp.bfloat16

HD = 128
GRP = 7
TOK = 128
ROWS = GRP * TOK
D = 3584
HALF = D // 2
LAT = 64
CAP = 64
NOISE = 4
N_SEQ = 32
N_HEAD = 4
FEAT = 112
GUW = 1408
DNW = 768
MAIN = 640
KC = 256
HEADW = D // N_HEAD
SCALE = 1.0 / math.sqrt(HD)
LOG2E = math.log2(math.e)
NEG = -1e30

HALVES = {"kv": ((0, 128), (128, 128)), "gu": ((0, 64), (64, 48)), "dn": ((0, 64), (64, 48))}


def contract_rows(left, right):
    return lax.dot_general(left, right, (((0,), (0,)), ((), ())), preferred_element_type=F32)


def dot(left, right):
    return jnp.dot(left, right, preferred_element_type=F32)


def kernel(
    q_ref, k_ref, v_ref, do_ref, mask_ref, clean_ref, noise_ref, time_ref, lin_ref, ngain_ref,
    gate_ref, up_ref, down_ref, ogain_ref, lout_ref, freq_ref,
    out_ref, dq_ref, dk_ref, dv_ref, pred_ref,
    kv, gu, dn, sgu, sdn, qs, qt, dos, dot_t, probs, acc_t, dkv, drecv, cond, nz, tm, tab, oha, ohb,
    le, nm, acc, hid, s1, s23, r1, r2, r3, fin, og, lo, mterm,
    ssem, rsem, dssem, drsem, cssem, crsem, xssem, xrsem,
):
    s = lax.axis_index("seq")
    h = lax.axis_index("head")
    xl = lax.div(s, 16)
    zy = lax.rem(s, 16)
    core = lax.rem(h, 2)
    x = lax.div(h, 2) * 2 + xl
    z = lax.div(zy, 4)
    y = lax.rem(zy, 4)
    mate = (1 - xl) * 16 + zy

    bufs = {"kv": kv, "gu": gu, "dn": dn}
    sem_at = {}
    leaving = {}

    def copy_of(src, dst, key, dev):
        at = sem_at.setdefault(key, len(sem_at))
        return pltpu.make_async_remote_copy(
            src_ref=src, dst_ref=dst, send_sem=ssem.at[at], recv_sem=rsem.at[at], device_id=dev, device_id_type=MESH
        )

    def start(make, key):
        src, dst, dev = make()
        copy_of(src, dst, key, dev).start()
        leaving[key] = make

    def landed(dst, key, dev):
        copy_of(dst, dst, key, dev).wait_recv()

    def all_left():
        for key, make in leaving.items():
            if key[:2] != ("kv", 1):
                src, dst, dev = make()
                copy_of(src, dst, key, dev).wait_send()

        @pl.when(xl == 1)
        def _():
            for key, make in leaving.items():
                if key[:2] == ("kv", 1):
                    src, dst, dev = make()
                    copy_of(src, dst, key, dev).wait_send()

    def back(pos, dist):
        return lax.rem(pos + 4 - dist, 4)

    def chunk(p, r, d1, d2, half):
        dy, dz = (d1, d2) if r == 0 else (d2, d1)
        pz, py = back(z, dz), back(y, dy)
        view = bufs[p].at[r, py * 4 + pz if p == "dn" and r == 0 else pz * 4 + py]
        if half is None:
            return view
        first, count = HALVES[p][half]
        return view.at[pl.ds(first, count)]

    def neighbour(r, axis, step):
        along_y = (axis == 1) == (r == 0)
        if along_y:
            return (xl * 16 + z * 4 + back(y, -step), h)
        return (xl * 16 + back(z, -step) * 4 + y, h)

    def send(p, r, d1, d2, axis, step, half=None):
        e1 = (d1 + step) % 4 if axis == 1 else d1
        e2 = (d2 + step) % 4 if axis == 2 else d2

        def make():
            ref = chunk(p, r, d1, d2, half)
            return ref, ref, neighbour(r, axis, step)

        start(make, (p, r, e1, e2, half))

    def wait(p, r, d1, d2, half=None):
        landed(chunk(p, r, d1, d2, half), (p, r, d1, d2, half), (mate, h))

    def p1_send(p, r):
        send(p, r, 0, 0, 1, 1)
        send(p, r, 0, 0, 1, -1)

    def first_sends(p, r):
        p1_send(p, r)
        p2_send(p, r, 0)

    def own(step, p, *rest):
        for r in (0, 1):
            pl.when(xl == r)(lambda r=r: step(p, r, *rest))

    def other(step, p, *rest):
        for r in (0, 1):
            if p == "kv" and r == 1:
                continue
            pl.when(xl != r)(lambda r=r: step(p, r, *rest))

    def p1_fwd(p, r):
        wait(p, r, 1, 0)
        send(p, r, 1, 0, 1, 1, 0)
        wait(p, r, 3, 0)
        send(p, r, 3, 0, 1, -1, 1)

    def p1_fin(p, r):
        wait(p, r, 2, 0, 0)
        wait(p, r, 2, 0, 1)

    def p2_send(p, r, d1):
        send(p, r, d1, 0, 2, 1)
        send(p, r, d1, 0, 2, -1)

    def p2_fwd(p, r, d1):
        wait(p, r, d1, 1)
        send(p, r, d1, 1, 2, 1, d1 % 2)
        wait(p, r, d1, 3)
        send(p, r, d1, 3, 2, -1, 1 - d1 % 2)

    def p2_fin(p, r, d1):
        wait(p, r, d1, 2, 0)
        wait(p, r, d1, 2, 1)

    def both(step, p, *rest):
        step(p, 0, *rest)
        if p == "kv":
            pl.when(xl == 1)(lambda: step(p, 1, *rest))
        else:
            step(p, 1, *rest)

    barrier = pltpu.get_barrier_semaphore()

    line = [(dx, dh) for dx in (0, 1) for dh in range(N_HEAD) if (dx, dh) != (0, 0)]

    def on_line(dx, dh):
        ox = lax.rem(xl + dx, 2)
        oh = lax.rem(h + dh, N_HEAD)
        return ox, oh, (ox * 16 + zy, oh)

    for dx, dh in line:
        pl.semaphore_signal(barrier, inc=1, device_id=on_line(dx, dh)[2], device_id_type=MESH)
    for axis in (1, 2):
        for step in (1, -1):
            pl.semaphore_signal(barrier, inc=1, device_id=neighbour(0, axis, step), device_id_type=MESH)
    pl.semaphore_wait(barrier, 7 + 4)

    low = lax.broadcasted_iota(jnp.int32, (FEAT, 128), 1) < 64

    def pack_gu(f, put):
        at = f * 768
        mid_gate = gate_ref[:, MAIN : MAIN + 128].astype(F32)
        mid_up = up_ref[:, MAIN : MAIN + 128].astype(F32)
        if f == 0:
            mixed = jnp.where(low, mid_gate, pltpu.roll(mid_up, 64, 1))
        else:
            mixed = jnp.where(low, pltpu.roll(mid_gate, 64, 1), mid_up)
        put(0, gate_ref[:, at : at + MAIN])
        put(MAIN, up_ref[:, at : at + MAIN])
        put(2 * MAIN, mixed.astype(BF16))

    def own_gu(at, value):
        gu[xl, zy, :, at : at + value.shape[1]] = value

    def mate_gu(at, value):
        sgu[:, at : at + value.shape[1]] = value

    def same(ref):
        return lambda: (ref, ref, (mate, h))

    dn_at = jnp.where(xl == 0, y * 4 + z, zy)
    kv[xl, zy, 0:TOK, :] = k_ref[...]
    kv[xl, zy, TOK : 2 * TOK, :] = v_ref[...]
    start(same(kv.at[xl, zy]), "xkv")
    own(first_sends, "kv")
    for f in (0, 1):
        pl.when(xl == f)(lambda f=f: pack_gu(f, own_gu))
    own(first_sends, "gu")
    for f in (0, 1):
        pl.when(xl == f)(lambda f=f: pack_gu(1 - f, mate_gu))
    start(lambda: (sgu, gu.at[xl, zy], (mate, h)), "xgu")
    landed(kv.at[1 - xl, zy], "xkv", (mate, h))
    other(first_sends, "kv")
    own(p1_fwd, "kv")
    own(p2_send, "kv", 1)
    own(p2_send, "kv", 3)

    for f in (0, 1):

        @pl.when(xl == f)
        def _():
            sdn[...] = down_ref[:, (1 - f) * MAIN : (1 - f) * MAIN + DNW]
            dn[xl, dn_at] = down_ref[:, f * MAIN : f * MAIN + DNW]

    start(lambda: (sdn, dn.at[xl, dn_at], (mate, h)), "xdn")

    digits = jnp.concatenate([time_ref[...] >> 5, time_ref[...] & 31], axis=0).astype(F32).astype(BF16)
    unit = lax.broadcasted_iota(jnp.int32, (2 * NOISE, 128), 0) == lax.broadcasted_iota(jnp.int32, (2 * NOISE, 128), 1)
    columns = contract_rows(digits, jnp.where(unit, 1.0, 0.0).astype(BF16))
    steps_own = columns[:, 0:NOISE] * 32.0 + columns[:, NOISE : 2 * NOISE]
    share = jnp.cos((steps_own / 1000.0 + 0.008) / 1.008 * (math.pi / 2.0)) ** 2
    signal, noise_part = jnp.sqrt(share), jnp.sqrt(1.0 - share)
    nz[xl] = jnp.zeros((NOISE * CAP, 128), BF16)
    tm[xl] = columns.astype(jnp.int32)
    for n in range(NOISE):
        row = signal[:, n : n + 1] * clean_ref[...] + noise_part[:, n : n + 1] * noise_ref[:, n * LAT : (n + 1) * LAT]
        nz[xl, n * CAP : (n + 1) * CAP, 0:LAT] = row.astype(BF16)
    start(same(nz.at[xl]), "xnz")
    start(same(tm.at[xl]), "xtm")


    for j in range(GRP):
        cols = slice(j * HD, (j + 1) * HD)
        qs[cols, :] = q_ref[:, cols]
        dos[cols, :] = do_ref[:, cols]
        qt[:, cols] = q_ref[:, cols].astype(F32).T.astype(BF16)
        dot_t[:, cols] = do_ref[:, cols].astype(F32).T.astype(BF16)

    landed(gu.at[1 - xl, zy], "xgu", (mate, h))
    other(first_sends, "gu")
    other(p1_fwd, "kv")
    other(p2_send, "kv", 1)
    other(p2_send, "kv", 3)
    both(p1_fin, "kv")
    both(p2_send, "kv", 2)
    own(p1_fwd, "gu")
    own(p2_send, "gu", 1)

    steps = lax.broadcasted_iota(jnp.int32, (32, HALF), 0).astype(F32)
    for k, mult in ((0, 32.0), (2, 1.0)):
        angle = (steps * mult) * freq_ref[...]
        for kk, value in ((k, jnp.cos(angle)), (k + 1, jnp.sin(angle))):
            high = value.astype(BF16)
            rest = value - high.astype(F32)
            middle = rest.astype(BF16)
            tab[kk, 0:32, :] = high
            tab[kk, 32:64, :] = middle
            tab[kk, 64:96, :] = (rest - middle.astype(F32)).astype(BF16)
            tab[kk, 96:128, :] = jnp.zeros((32, HALF), BF16)

    both(p2_fwd, "kv", 0)
    both(p2_fwd, "kv", 1)
    own(p2_send, "gu", 3)
    both(p2_fwd, "kv", 3)
    both(p2_fwd, "kv", 2)
    own(p1_fin, "gu")
    other(p1_fwd, "gu")
    other(p2_send, "gu", 1)
    own(p2_send, "gu", 2)
    other(p2_send, "gu", 3)

    landed(nz.at[1 - xl], "xnz", (mate, h))
    landed(tm.at[1 - xl], "xtm", (mate, h))
    lane = lax.broadcasted_iota(jnp.int32, (CAP, 128), 1)
    for b in (0, 1):
        for n in range(NOISE):
            place = (n % 2) * 4 + (n // 2) * 2 + b
            rows = slice(place * CAP, (place + 1) * CAP)
            for ref, digit in ((oha, tm[b, :, n : n + 1]), (ohb, tm[b, :, NOISE + n : NOISE + n + 1])):
                ref[rows, :] = jnp.where((lane & 31) == digit, jnp.where(lane < 96, 1.0, 0.0), 0.0).astype(BF16)

    nz_rows = jnp.concatenate(
        [nz[g % 2, ((g // 2 % 2) * 2 + g // 4) * CAP : ((g // 2 % 2) * 2 + g // 4 + 1) * CAP, 0:LAT] for g in range(8)], axis=0
    )

    def embed(j, carry):
        c0 = pl.ds(pl.multiple_of(j * 256, 256), 256)
        c1 = pl.ds(pl.multiple_of(HALF + j * 256, 256), 256)
        noisy = nz_rows
        ca, sa = dot(oha[...], tab[0, :, c0]), dot(oha[...], tab[1, :, c0])
        cb, sb = dot(ohb[...], tab[2, :, c0]), dot(ohb[...], tab[3, :, c0])
        le[:, c0] = ca * cb - sa * sb + dot(noisy, lin_ref[:, c0])
        le[:, c1] = sa * cb + ca * sb + dot(noisy, lin_ref[:, c1])
        return carry

    lax.fori_loop(0, HALF // 256, embed, 0)

    other(p1_fin, "gu")
    other(p2_send, "gu", 2)
    landed(dn.at[1 - xl, jnp.where(xl == 1, y * 4 + z, zy)], "xdn", (mate, h))
    both(p1_send, "dn")
    both(p2_fwd, "gu", 0)
    for d in (0, 1, 3, 2):
        both(p2_fin, "kv", d)

    n_steps = lax.div(s, 2) + 1

    def keys_of(c):
        blocks = kv.at[lax.div(c, 8), pl.ds(lax.rem(c, 8) * 2, 2)]
        return blocks[:, 0:TOK, :].reshape(KC, HD), blocks[:, TOK : 2 * TOK, :].reshape(KC, HD)

    def scores_of(c, masked):
        score = dot(keys_of(c)[0], qt[...]) * (SCALE * LOG2E)
        if masked:
            key_pos = c * KC + lax.broadcasted_iota(jnp.int32, (KC, ROWS), 0)
            query_pos = s * TOK + (lax.broadcasted_iota(jnp.int32, (KC, ROWS), 1) & (TOK - 1))
            score = jnp.where(key_pos <= query_pos, score, NEG)
        return score

    def fold(values, reduce):
        return reduce(values.reshape(KC // 8, 8, ROWS), axis=0)

    def max_step(c, run, masked=False):
        return jnp.maximum(run, fold(scores_of(c, masked), jnp.max))

    row_max = lax.fori_loop(0, n_steps - 1, max_step, jnp.full((8, ROWS), NEG, F32))
    row_max = max_step(n_steps - 1, row_max, True)
    row_max = jnp.max(row_max, axis=0, keepdims=True)
    both(p2_fwd, "gu", 1)
    both(p1_fwd, "dn")

    acc_t[...] = jnp.zeros_like(acc_t)

    def sum_step(c, run, masked=False):
        soft = jnp.exp2(scores_of(c, masked) - row_max)
        soft_b = soft.astype(BF16)
        probs[pl.ds(pl.multiple_of(c * KC, KC), KC), :] = soft_b
        acc_t[...] += contract_rows(keys_of(c)[1], soft_b)
        return run + fold(soft, jnp.sum)

    total = lax.fori_loop(0, n_steps - 1, sum_step, jnp.zeros((8, ROWS), F32))
    total = sum_step(n_steps - 1, total, True)
    total = jnp.sum(total, axis=0, keepdims=True)
    inverse = 1.0 / total
    out_t = (acc_t[...] / total).astype(BF16)
    delta = jnp.sum(out_t.astype(F32) * dot_t[...].astype(F32), axis=0, keepdims=True)
    for j in range(GRP):
        cols = slice(j * HD, (j + 1) * HD)
        out_ref[:, cols] = out_t[:, cols].astype(F32).T.astype(BF16)

    mask = mask_ref[...]
    ones = jnp.broadcast_to(mask.astype(F32), (8, TOK)).astype(BF16)
    before = lax.broadcasted_iota(jnp.int32, (TOK, TOK), 0) <= lax.broadcasted_iota(jnp.int32, (TOK, TOK), 1)
    rank = dot(ones, jnp.where(before, 1.0, 0.0).astype(BF16))[0:1, :] - 1.0
    slot = lax.broadcasted_iota(jnp.int32, (CAP, TOK), 0).astype(F32)
    chosen = jnp.where(rank == slot, jnp.where(mask == 1, 1.0, 0.0), 0.0)
    valid = jnp.sum(chosen, axis=1, keepdims=True) > 0.5
    cond[xl, h] = dot(chosen.astype(BF16), out_ref[...]).astype(BF16)
    cond_sent = []
    for i, (dx, dh) in enumerate(line):
        copy = pltpu.make_async_remote_copy(
            src_ref=cond.at[xl, h], dst_ref=cond.at[xl, h], send_sem=cssem.at[i],
            recv_sem=crsem.at[xl * N_HEAD + h], device_id=on_line(dx, dh)[2], device_id_type=MESH,
        )
        copy.start()
        cond_sent.append(copy)

    both(p2_fwd, "gu", 3)

    acc_t[...] = jnp.zeros_like(acc_t)

    def grad_step(c, carry):
        keys, values = keys_of(c)
        prob = probs[pl.ds(pl.multiple_of(c * KC, KC), KC), :].astype(F32) * inverse
        ds = (prob * (dot(values, dot_t[...]) - delta)).astype(BF16)
        acc_t[...] += contract_rows(keys, ds)
        dkv[pl.ds(2 * c, 2), 0:TOK, :] = (dot(ds, qs[...]) * SCALE).astype(BF16).reshape(2, TOK, HD)
        dkv[pl.ds(2 * c, 2), TOK : 2 * TOK, :] = dot(prob.astype(BF16), dos[...]).astype(BF16).reshape(2, TOK, HD)
        return carry

    def cross_copy(kb):
        return pltpu.make_async_remote_copy(
            src_ref=dkv.at[kb], dst_ref=mterm.at[kb], send_sem=xssem.at[kb], recv_sem=xrsem.at[kb],
            device_id=(mate, h), device_id_type=MESH,
        )

    for part in range(4):
        lax.fori_loop(part * 4, jnp.minimum(n_steps, part * 4 + 4), grad_step, 0)
        if part == 0:
            both(p2_fwd, "gu", 2)
            both(p1_fin, "dn")
            both(p2_send, "dn", 0)
            both(p2_send, "dn", 1)
        elif part == 1:

            def send_cross(kb, carry):
                cross_copy(kb).start()
                return carry

            @pl.when(xl == 1)
            def _():
                lax.fori_loop(0, 16, send_cross, 0)

    for j in range(GRP):
        cols = slice(j * HD, (j + 1) * HD)
        dq_ref[:, cols] = (acc_t[:, cols] * SCALE).T.astype(BF16)
    both(p2_fwd, "dn", 0)
    both(p2_send, "dn", 3)

    for dx, dh in line:
        ox, oh, dev = on_line(dx, dh)
        pltpu.make_async_remote_copy(
            src_ref=cond.at[ox, oh], dst_ref=cond.at[ox, oh], send_sem=cssem.at[0],
            recv_sem=crsem.at[ox * N_HEAD + oh], device_id=dev, device_id_type=MESH,
        ).wait_recv()

    def norm_rows(g, carry):
        rows = pl.ds(pl.multiple_of(g * CAP, CAP), CAP)
        square = jnp.zeros((CAP, 1), F32)
        for hh in range(N_HEAD):
            cols = slice(hh * HEADW, (hh + 1) * HEADW)
            base = le[rows, cols] + cond[lax.rem(g, 2), hh].astype(F32)
            le[rows, cols] = base
            square += jnp.sum(base * base, axis=1, keepdims=True)
        scale = lax.rsqrt(square * (1.0 / D) + 1e-06)
        for hh in range(N_HEAD):
            cols = slice(hh * HEADW, (hh + 1) * HEADW)
            nm[rows, cols] = (le[rows, cols] * scale * ngain_ref[cols].reshape(1, HEADW)).astype(BF16)
        return carry

    lax.fori_loop(0, 2 * NOISE, norm_rows, 0)
    both(p2_fwd, "dn", 1)
    both(p2_send, "dn", 2)
    for d in (0, 1, 3, 2):
        both(p2_fin, "gu", d)

    SUB = 4 * FEAT
    mine = pl.ds(pl.multiple_of((core * 4 + x) * CAP, CAP), CAP)
    for at in range(4):
        for other_at in range(4):
            c0 = other_at * SUB + at * FEAT
            to = slice(other_at * FEAT, (other_at + 1) * FEAT)
            fin[0, at, :, to] = le[mine, c0 : c0 + FEAT]
            og[0, at, :, to] = jnp.broadcast_to(ogain_ref[c0 : c0 + FEAT].reshape(1, FEAT), (8, FEAT))
            lo[0, at, :, to] = lout_ref[:, c0 : c0 + FEAT]
        c1 = HALF + at * SUB
        fin[1, at] = le[mine, c1 : c1 + SUB]
        og[1, at] = jnp.broadcast_to(ogain_ref[c1 : c1 + SUB].reshape(1, SUB), (8, SUB))
        lo[1, at] = lout_ref[:, c1 : c1 + SUB]

    for k in range(4):
        piece = gu[k // 2, (k % 2) * 8 : (k % 2) * 8 + 8].reshape(8 * FEAT, GUW)
        part = dot(nm[:, k * 896 : (k + 1) * 896], piece)
        if k == 0:
            acc[...] = part
        else:
            acc[...] += part
        if k == 2:
            both(p2_fwd, "dn", 3)

    def silu(value):
        return value / (1.0 + jnp.exp(-value))

    mixed = acc[:, 2 * MAIN :]
    turned = pltpu.roll(mixed, 64, 1)
    lower_half = lax.broadcasted_iota(jnp.int32, (2 * NOISE * CAP, 128), 1) < 64

    @pl.when(xl == 0)
    def _():
        hid[:, 0:MAIN] = (silu(acc[:, 0:MAIN]) * acc[:, MAIN : 2 * MAIN]).astype(BF16)
        hid[:, MAIN:DNW] = jnp.where(lower_half, silu(mixed) * turned, 0.0).astype(BF16)

    @pl.when(xl == 1)
    def _():
        hid[:, 128:DNW] = (silu(acc[:, 0:MAIN]) * acc[:, MAIN : 2 * MAIN]).astype(BF16)
        hid[:, 0:128] = jnp.where(lower_half, 0.0, silu(turned) * mixed).astype(BF16)

    def term_copy(b, kb):
        return pltpu.make_async_remote_copy(
            src_ref=dkv.at[b * 16 + kb], dst_ref=drecv.at[b, zy], send_sem=dssem.at[b * 16 + kb],
            recv_sem=drsem.at[b * 16 + zy], device_id=(xl * 16 + kb, h), device_id_type=MESH,
        )

    def forward_copy(kb):
        return pltpu.make_async_remote_copy(
            src_ref=mterm.at[kb], dst_ref=drecv.at[0, zy], send_sem=dssem.at[kb], recv_sem=drsem.at[zy],
            device_id=(kb, h), device_id_type=MESH,
        )

    def join_terms(kb, carry):
        cross_copy(kb).wait_recv()
        mterm[kb] = (mterm[kb].astype(F32) + dkv[kb].astype(F32)).astype(BF16)
        forward_copy(kb).start()
        return carry

    def pass_terms(kb, carry):
        cross_copy(kb).wait_recv()
        forward_copy(kb).start()
        return carry

    def send_terms(kb, carry):
        term_copy(1, kb).start()
        return carry

    def all_terms():
        @pl.when(xl == 0)
        def _():
            lax.fori_loop(0, zy, join_terms, 0)
            lax.fori_loop(zy + 1, 16, pass_terms, 0)

        @pl.when(xl == 1)
        def _():
            lax.fori_loop(0, zy, send_terms, 0)

    def add_terms(b):
        def step(i, run):
            pltpu.make_async_remote_copy(
                src_ref=drecv.at[b, i], dst_ref=drecv.at[b, i], send_sem=dssem.at[0], recv_sem=drsem.at[b * 16 + i],
                device_id=(mate, h), device_id_type=MESH,
            ).wait_recv()
            return run + drecv[b, i].astype(F32)

        return step

    def along_x(step):
        to = lax.rem(x + 4 + step, 4)
        return (lax.rem(to, 2) * 16 + zy, lax.div(to, 2) * 2 + core)

    def pick(step):
        return lax.rem(x + 4 + step, 4) * CAP

    order = (0, 1, 3, 2)

    def lanes(k):
        return slice(k * 512, k * 512 + SUB)

    def tot(k, r, step):
        first = pl.multiple_of(r * 256 + pick(step), CAP)
        return acc[pl.ds(first, CAP), lanes(k % 2)]

    sibling = (s, h + 1 - 2 * core)

    def stage0(k):
        for r in (0, 1):
            p2_fin("dn", r, order[k])
        pieces = []
        for r in (0, 1):
            at = back(y if r == 0 else z, order[k]) * 4
            piece = dn[r, pl.ds(at, 4)].reshape(SUB, DNW)
            pieces.append(piece)
            theirs = hid[pl.ds(pl.multiple_of((1 - core) * 256, 256), 256), :]
            part = lax.dot_general(theirs, piece, (((1,), (1,)), ((), ())), preferred_element_type=F32)
            s1[k, r] = part.astype(BF16)
            start(lambda r=r: (s1.at[k, r], r1.at[k, r], sibling), ("r1", k, r))
        for r in (0, 1):
            ours = hid[pl.ds(pl.multiple_of(core * 256, 256), 256), :]
            acc[r * 256 : r * 256 + 256, lanes(k % 2)] = lax.dot_general(ours, pieces[r], (((1,), (1,)), ((), ())), preferred_element_type=F32)

    def stage1(k):
        for r in (0, 1):
            landed(r1.at[k, r], ("r1", k, r), sibling)
            far = r1[k, r, pl.ds(pl.multiple_of(pick(2), CAP), CAP), :].astype(F32)
            s23[0, k, r] = (tot(k, r, 2) + far).astype(BF16)
            start(lambda r=r: (s23.at[0, k, r], r2.at[k, r], along_x(1 - 2 * r)), ("r2", k, r))
        for r in (0, 1):
            acc[r * 256 : r * 256 + 256, lanes(k % 2)] += r1[k, r].astype(F32)

    def stage2(k):
        for r in (0, 1):
            landed(r2.at[k, r], ("r2", k, r), along_x(1))
            for way, step in ((0, 1), (1, -1)):
                near = tot(k, r, step)
                if way == r:
                    near += r2[k, r].astype(F32)
                s23[1 + way, k, r] = near.astype(BF16)
                start(
                    lambda r=r, way=way, step=step: (s23.at[1 + way, k, r], r3.at[k, r, way], along_x(step)),
                    ("r3", k, r, way),
                )
            fin[r, back(y if r == 0 else z, order[k])] += tot(k, r, 0)

    def stage3(k):
        for r in (0, 1):
            at = back(y if r == 0 else z, order[k])
            for way in (0, 1):
                landed(r3.at[k, r, way], ("r3", k, r, way), along_x(1))
                fin[r, at] += r3[k, r, way].astype(F32)

    for k in range(6):
        if 2 <= k:
            stage2(k - 2)
        if k < 4:
            stage0(k)
        if k == 0:
            both(p2_fwd, "dn", 2)
            all_terms()
        if 1 <= k < 5:
            stage1(k - 1)

    for k in range(4):
        stage3(k)

    square = jnp.zeros((CAP, 1), F32)
    for r in (0, 1):
        for at in range(4):
            rows = fin[r, at]
            square += jnp.sum(rows * rows, axis=1, keepdims=True)
    scale = lax.rsqrt(square * (1.0 / D) + 1e-06)
    result = jnp.zeros((CAP, LAT), F32)
    for r in (0, 1):
        for at in range(4):
            final = (fin[r, at] * scale * og[r, at, 0:1, :]).astype(BF16)
            result += lax.dot_general(final, lo[r, at], (((1,), (1,)), ((), ())), preferred_element_type=F32)
    pred_ref[...] = jnp.where(valid, result, 0.0)

    def put_terms(run):
        dk_ref[...] = run[0:TOK].astype(BF16)
        dv_ref[...] = run[TOK : 2 * TOK].astype(BF16)

    @pl.when(xl == 1)
    def _():
        put_terms(lax.fori_loop(zy + 1, 16, add_terms(1), dkv[16 + zy].astype(F32)))

    @pl.when(xl == 0)
    def _():
        cross_copy(zy).wait_recv()
        run = dkv[zy].astype(F32) + mterm[zy].astype(F32)
        run = lax.fori_loop(0, zy, add_terms(0), run)
        put_terms(lax.fori_loop(zy + 1, 16, add_terms(0), run))

    all_left()
    for copy in cond_sent:
        copy.wait_send()

    def left(copy):
        def step(kb, carry):
            copy(kb).wait_send()
            return carry

        return step

    @pl.when(xl == 1)
    def _():
        lax.fori_loop(0, 16, left(cross_copy), 0)
        lax.fori_loop(0, zy, left(lambda kb: term_copy(1, kb)), 0)

    @pl.when(xl == 0)
    def _():
        lax.fori_loop(0, zy, left(forward_copy), 0)
        lax.fori_loop(zy + 1, 16, left(forward_copy), 0)


def hand_over(*refs):
    for i in range(5):
        refs[5 + i][...] = refs[i][...]


def shards(
    queries, key_vectors, value_vectors, out_cotangent, latent_mask, clean_latents, noise_draws, timesteps,
    latent_in, norm_gain, gate_weight, up_weight, down_weight, out_gain, latent_out,
):
    frequencies = np.exp(-math.log(10000.0) * np.arange(HALF, dtype=np.float32) / HALF).astype(np.float32)
    vmem = pl.BlockSpec(memory_space=pltpu.VMEM)
    dma = pltpu.SemaphoreType.DMA
    n_sems = 176
    results = pl.pallas_call(
        kernel,
        out_shape=(
            jax.ShapeDtypeStruct((TOK, ROWS), BF16),
            jax.ShapeDtypeStruct((TOK, ROWS), BF16),
            jax.ShapeDtypeStruct((TOK, HD), BF16),
            jax.ShapeDtypeStruct((TOK, HD), BF16),
            jax.ShapeDtypeStruct((CAP, LAT), F32),
        ),
        in_specs=[vmem] * 16,
        out_specs=(vmem,) * 5,
        scratch_shapes=[
            pltpu.VMEM((2, 16, 2 * TOK, HD), BF16),
            pltpu.VMEM((2, 16, FEAT, GUW), BF16),
            pltpu.VMEM((2, 16, FEAT, DNW), BF16),
            pltpu.VMEM((FEAT, GUW), BF16),
            pltpu.VMEM((FEAT, DNW), BF16),
            pltpu.VMEM((ROWS, HD), BF16),
            pltpu.VMEM((HD, ROWS), BF16),
            pltpu.VMEM((ROWS, HD), BF16),
            pltpu.VMEM((HD, ROWS), BF16),
            pltpu.VMEM((N_SEQ * TOK, ROWS), BF16),
            pltpu.VMEM((HD, ROWS), F32),
            pltpu.VMEM((N_SEQ, 2 * TOK, HD), BF16),
            pltpu.VMEM((2, 16, 2 * TOK, HD), BF16),
            pltpu.VMEM((2, N_HEAD, CAP, HEADW), BF16),
            pltpu.VMEM((2, NOISE * CAP, 128), BF16),
            pltpu.VMEM((2, CAP, 128), jnp.int32),
            pltpu.VMEM((4, 128, HALF), BF16),
            pltpu.VMEM((2 * NOISE * CAP, 128), BF16),
            pltpu.VMEM((2 * NOISE * CAP, 128), BF16),
            pltpu.VMEM((2 * NOISE * CAP, D), F32),
            pltpu.VMEM((2 * NOISE * CAP, D), BF16),
            pltpu.VMEM((2 * NOISE * CAP, GUW), F32),
            pltpu.VMEM((2 * NOISE * CAP, DNW), BF16),
            pltpu.VMEM((4, 2, 4 * CAP, 4 * FEAT), BF16),
            pltpu.VMEM((3, 4, 2, CAP, 4 * FEAT), BF16),
            pltpu.VMEM((4, 2, 4 * CAP, 4 * FEAT), BF16),
            pltpu.VMEM((4, 2, CAP, 4 * FEAT), BF16),
            pltpu.VMEM((4, 2, 2, CAP, 4 * FEAT), BF16),
            pltpu.VMEM((2, 4, CAP, 4 * FEAT), F32),
            pltpu.VMEM((2, 4, 8, 4 * FEAT), F32),
            pltpu.VMEM((2, 4, LAT, 4 * FEAT), BF16),
            pltpu.VMEM((16, 2 * TOK, HD), BF16),
            dma((n_sems,)),
            dma((n_sems,)),
            dma((N_SEQ,)),
            dma((N_SEQ,)),
            dma((7,)),
            dma((8,)),
            dma((16,)),
            dma((16,)),
        ],
        compiler_params=pltpu.CompilerParams(
            collective_id=0, has_side_effects=True, vmem_limit_bytes=63 * 1024 * 1024
        ),
    )(
        queries, key_vectors, value_vectors, out_cotangent, latent_mask.reshape(1, TOK), clean_latents, noise_draws,
        timesteps.T, latent_in, norm_gain, gate_weight, up_weight, down_weight, out_gain,
        latent_out.T, jnp.asarray(frequencies.reshape(1, HALF)),
    )
    return pl.pallas_call(
        hand_over,
        out_shape=tuple(jax.ShapeDtypeStruct(a.shape, a.dtype) for a in results),
        in_specs=[vmem] * 5,
        out_specs=(vmem,) * 5,
        compiler_params=pltpu.CompilerParams(vmem_limit_bytes=63 * 1024 * 1024),
    )(*results)


def solution(mesh):
    placed = (
        P("seq", "head"),
        P("seq", "head"),
        P("seq", "head"),
        P("seq", "head"),
        P("seq"),
        P("seq", None),
        P("seq", None),
        P("seq", None),
        P(),
        P(),
        P("seq", "head"),
        P("seq", "head"),
        P("seq", "head"),
        P(),
        P(),
    )
    return jax.shard_map(
        shards,
        mesh=mesh,
        in_specs=placed,
        out_specs=(P("seq", "head"),) * 5,
        check_vma=False,
    )
```

```python
import math

import jax
import jax.numpy as jnp
import numpy as np
from jax import lax
from jax.experimental import pallas as pl
from jax.experimental.pallas import tpu as pltpu
from jax.sharding import PartitionSpec as P

MESH = pl.DeviceIdType.MESH
F32 = jnp.float32
BF16 = jnp.bfloat16

HD = 128
GRP = 7
TOK = 128
ROWS = GRP * TOK
D = 3584
HALF = D // 2
LAT = 64
CAP = 64
NOISE = 4
N_SEQ = 32
N_HEAD = 4
FEAT = 112
GUW = 1408
DNW = 768
MAIN = 640
KC = 256
HEADW = D // N_HEAD
SCALE = 1.0 / math.sqrt(HD)
LOG2E = math.log2(math.e)
NEG = -1e30

HALVES = {"kv": ((0, 128), (128, 128)), "gu": ((0, 64), (64, 48)), "dn": ((0, 64), (64, 48))}


def contract_rows(left, right):
    return lax.dot_general(left, right, (((0,), (0,)), ((), ())), preferred_element_type=F32)


def dot(left, right):
    return jnp.dot(left, right, preferred_element_type=F32)


def kernel(
    q_hbm, k_ref, v_ref, do_hbm, mask_ref, clean_hbm, noise_hbm, time_ref, lin_hbm, ngain_ref,
    gate_ref, up_ref, down_hbm, ogain_ref, lout_hbm, freq_ref,
    out_ref, dq_ref, dk_ref, dv_ref, pred_ref,
    kv, gu, dn, sgu, sdn, qs, qt, dos, dot_t, probs, acc_t, dkv, drecv, cond, nz, tm, tab, oha, ohb,
    le, nm, acc, hid, s1, s23, r1, r2, r3, fin, og, lo, mterm, tsum,
    q_ref, do_ref, clean_ref, noise_ref, lin_ref, down_ref, lout_ref,
    ssem, rsem, dssem, drsem, cssem, crsem, xssem, xrsem, fsem,
):
    fetched = [
        pltpu.make_async_copy(src, dst, fsem.at[i])
        for i, (src, dst) in enumerate(
            (
                (down_hbm, down_ref),
                (clean_hbm, clean_ref),
                (noise_hbm, noise_ref),
                (q_hbm, q_ref),
                (do_hbm, do_ref),
                (lin_hbm, lin_ref),
                (lout_hbm, lout_ref),
            )
        )
    ]
    for copy in fetched:
        copy.start()
    s = lax.axis_index("seq")
    h = lax.axis_index("head")
    xl = lax.div(s, 16)
    zy = lax.rem(s, 16)
    core = lax.rem(h, 2)
    x = lax.div(h, 2) * 2 + xl
    z = lax.div(zy, 4)
    y = lax.rem(zy, 4)
    mate = (1 - xl) * 16 + zy

    bufs = {"kv": kv, "gu": gu, "dn": dn}
    sem_at = {}
    leaving = {}

    def copy_of(src, dst, key, dev):
        at = sem_at.setdefault(key, len(sem_at))
        return pltpu.make_async_remote_copy(
            src_ref=src, dst_ref=dst, send_sem=ssem.at[at], recv_sem=rsem.at[at], device_id=dev, device_id_type=MESH
        )

    def start(make, key):
        src, dst, dev = make()
        copy_of(src, dst, key, dev).start()
        leaving[key] = make

    def landed(dst, key, dev):
        copy_of(dst, dst, key, dev).wait_recv()

    def all_left():
        for key, make in leaving.items():
            if key[:2] != ("kv", 1):
                src, dst, dev = make()
                copy_of(src, dst, key, dev).wait_send()

        @pl.when(xl == 1)
        def _():
            for key, make in leaving.items():
                if key[:2] == ("kv", 1):
                    src, dst, dev = make()
                    copy_of(src, dst, key, dev).wait_send()

    def back(pos, dist):
        return lax.rem(pos + 4 - dist, 4)

    def chunk(p, r, d1, d2, half):
        dy, dz = (d1, d2) if r == 0 else (d2, d1)
        pz, py = back(z, dz), back(y, dy)
        view = bufs[p].at[r, py * 4 + pz if p == "dn" and r == 0 else pz * 4 + py]
        if half is None:
            return view
        first, count = HALVES[p][half]
        return view.at[pl.ds(first, count)]

    def neighbour(r, axis, step):
        along_y = (axis == 1) == (r == 0)
        if along_y:
            return (xl * 16 + z * 4 + back(y, -step), h)
        return (xl * 16 + back(z, -step) * 4 + y, h)

    def send(p, r, d1, d2, axis, step, half=None):
        e1 = (d1 + step) % 4 if axis == 1 else d1
        e2 = (d2 + step) % 4 if axis == 2 else d2

        def make():
            ref = chunk(p, r, d1, d2, half)
            return ref, ref, neighbour(r, axis, step)

        start(make, (p, r, e1, e2, half))

    def wait(p, r, d1, d2, half=None):
        landed(chunk(p, r, d1, d2, half), (p, r, d1, d2, half), (mate, h))

    def p1_send(p, r):
        send(p, r, 0, 0, 1, 1)
        send(p, r, 0, 0, 1, -1)

    def first_sends(p, r):
        p1_send(p, r)
        p2_send(p, r, 0)

    def own(step, p, *rest):
        for r in (0, 1):
            pl.when(xl == r)(lambda r=r: step(p, r, *rest))

    def other(step, p, *rest):
        for r in (0, 1):
            if p == "kv" and r == 1:
                continue
            pl.when(xl != r)(lambda r=r: step(p, r, *rest))

    def p1_fwd(p, r):
        wait(p, r, 1, 0)
        send(p, r, 1, 0, 1, 1, 0)
        wait(p, r, 3, 0)
        send(p, r, 3, 0, 1, -1, 1)

    def p1_fin(p, r):
        wait(p, r, 2, 0, 0)
        wait(p, r, 2, 0, 1)

    def p2_send(p, r, d1):
        send(p, r, d1, 0, 2, 1)
        send(p, r, d1, 0, 2, -1)

    def p2_fwd(p, r, d1):
        wait(p, r, d1, 1)
        send(p, r, d1, 1, 2, 1, d1 % 2)
        wait(p, r, d1, 3)
        send(p, r, d1, 3, 2, -1, 1 - d1 % 2)

    def p2_fin(p, r, d1):
        wait(p, r, d1, 2, 0)
        wait(p, r, d1, 2, 1)

    def both(step, p, *rest):
        step(p, 0, *rest)
        if p == "kv":
            pl.when(xl == 1)(lambda: step(p, 1, *rest))
        else:
            step(p, 1, *rest)

    barrier = pltpu.get_barrier_semaphore()

    line = [(dx, dh) for dx in (0, 1) for dh in range(N_HEAD) if (dx, dh) != (0, 0)]

    def on_line(dx, dh):
        ox = lax.rem(xl + dx, 2)
        oh = lax.rem(h + dh, N_HEAD)
        return ox, oh, (ox * 16 + zy, oh)

    for dx, dh in line:
        pl.semaphore_signal(barrier, inc=1, device_id=on_line(dx, dh)[2], device_id_type=MESH)
    for axis in (1, 2):
        for step in (1, -1):
            pl.semaphore_signal(barrier, inc=1, device_id=neighbour(0, axis, step), device_id_type=MESH)
    pl.semaphore_wait(barrier, 7 + 4)

    low = lax.broadcasted_iota(jnp.int32, (FEAT, 128), 1) < 64

    def pack_gu(f, put):
        at = f * 768
        mid_gate = gate_ref[:, MAIN : MAIN + 128].astype(F32)
        mid_up = up_ref[:, MAIN : MAIN + 128].astype(F32)
        if f == 0:
            mixed = jnp.where(low, mid_gate, pltpu.roll(mid_up, 64, 1))
        else:
            mixed = jnp.where(low, pltpu.roll(mid_gate, 64, 1), mid_up)
        put(0, gate_ref[:, at : at + MAIN])
        put(MAIN, up_ref[:, at : at + MAIN])
        put(2 * MAIN, mixed.astype(BF16))

    def own_gu(at, value):
        gu[xl, zy, :, at : at + value.shape[1]] = value

    def mate_gu(at, value):
        sgu[:, at : at + value.shape[1]] = value

    def same(ref):
        return lambda: (ref, ref, (mate, h))

    dn_at = jnp.where(xl == 0, y * 4 + z, zy)
    kv[xl, zy, 0:TOK, :] = k_ref[...]
    kv[xl, zy, TOK : 2 * TOK, :] = v_ref[...]
    start(same(kv.at[xl, zy]), "xkv")
    own(first_sends, "kv")
    for f in (0, 1):
        pl.when(xl == f)(lambda f=f: pack_gu(f, own_gu))
    own(first_sends, "gu")
    for f in (0, 1):
        pl.when(xl == f)(lambda f=f: pack_gu(1 - f, mate_gu))
    start(lambda: (sgu, gu.at[xl, zy], (mate, h)), "xgu")
    landed(kv.at[1 - xl, zy], "xkv", (mate, h))
    other(first_sends, "kv")
    own(p1_fwd, "kv")
    own(p2_send, "kv", 1)
    own(p2_send, "kv", 3)

    for copy in fetched:
        copy.wait()
    for f in (0, 1):

        @pl.when(xl == f)
        def _():
            sdn[...] = down_ref[:, (1 - f) * MAIN : (1 - f) * MAIN + DNW]
            dn[xl, dn_at] = down_ref[:, f * MAIN : f * MAIN + DNW]

    start(lambda: (sdn, dn.at[xl, dn_at], (mate, h)), "xdn")

    digits = jnp.concatenate([time_ref[...] >> 5, time_ref[...] & 31], axis=0).astype(F32).astype(BF16)
    unit = lax.broadcasted_iota(jnp.int32, (2 * NOISE, 128), 0) == lax.broadcasted_iota(jnp.int32, (2 * NOISE, 128), 1)
    columns = contract_rows(digits, jnp.where(unit, 1.0, 0.0).astype(BF16))
    steps_own = columns[:, 0:NOISE] * 32.0 + columns[:, NOISE : 2 * NOISE]
    share = jnp.cos((steps_own / 1000.0 + 0.008) / 1.008 * (math.pi / 2.0)) ** 2
    signal, noise_part = jnp.sqrt(share), jnp.sqrt(1.0 - share)
    nz[xl] = jnp.zeros((NOISE * CAP, 128), BF16)
    tm[xl] = columns.astype(jnp.int32)
    for n in range(NOISE):
        row = signal[:, n : n + 1] * clean_ref[...] + noise_part[:, n : n + 1] * noise_ref[:, n * LAT : (n + 1) * LAT]
        nz[xl, n * CAP : (n + 1) * CAP, 0:LAT] = row.astype(BF16)
    start(same(nz.at[xl]), "xnz")
    start(same(tm.at[xl]), "xtm")


    for j in range(GRP):
        cols = slice(j * HD, (j + 1) * HD)
        qs[cols, :] = q_ref[:, cols]
        dos[cols, :] = do_ref[:, cols]
        qt[:, cols] = q_ref[:, cols].astype(F32).T.astype(BF16)
        dot_t[:, cols] = do_ref[:, cols].astype(F32).T.astype(BF16)

    landed(gu.at[1 - xl, zy], "xgu", (mate, h))
    other(first_sends, "gu")
    other(p1_fwd, "kv")
    other(p2_send, "kv", 1)
    other(p2_send, "kv", 3)
    both(p1_fin, "kv")
    both(p2_send, "kv", 2)
    own(p1_fwd, "gu")
    own(p2_send, "gu", 1)

    steps = lax.broadcasted_iota(jnp.int32, (32, HALF), 0).astype(F32)
    for k, mult in ((0, 32.0), (2, 1.0)):
        angle = (steps * mult) * freq_ref[...]
        for kk, value in ((k, jnp.cos(angle)), (k + 1, jnp.sin(angle))):
            high = value.astype(BF16)
            rest = value - high.astype(F32)
            middle = rest.astype(BF16)
            tab[kk, 0:32, :] = high
            tab[kk, 32:64, :] = middle
            tab[kk, 64:96, :] = (rest - middle.astype(F32)).astype(BF16)
            tab[kk, 96:128, :] = jnp.zeros((32, HALF), BF16)

    both(p2_fwd, "kv", 0)
    both(p2_fwd, "kv", 1)
    own(p2_send, "gu", 3)
    both(p2_fwd, "kv", 3)
    both(p2_fwd, "kv", 2)
    own(p1_fin, "gu")
    other(p1_fwd, "gu")
    other(p2_send, "gu", 1)
    own(p2_send, "gu", 2)
    other(p2_send, "gu", 3)

    landed(nz.at[1 - xl], "xnz", (mate, h))
    landed(tm.at[1 - xl], "xtm", (mate, h))
    lane = lax.broadcasted_iota(jnp.int32, (CAP, 128), 1)
    for b in (0, 1):
        for n in range(NOISE):
            place = (n % 2) * 4 + (n // 2) * 2 + b
            rows = slice(place * CAP, (place + 1) * CAP)
            for ref, digit in ((oha, tm[b, :, n : n + 1]), (ohb, tm[b, :, NOISE + n : NOISE + n + 1])):
                ref[rows, :] = jnp.where((lane & 31) == digit, jnp.where(lane < 96, 1.0, 0.0), 0.0).astype(BF16)

    nz_rows = jnp.concatenate(
        [nz[g % 2, ((g // 2 % 2) * 2 + g // 4) * CAP : ((g // 2 % 2) * 2 + g // 4 + 1) * CAP, 0:LAT] for g in range(8)], axis=0
    )

    def embed(j, carry):
        c0 = pl.ds(pl.multiple_of(j * 256, 256), 256)
        c1 = pl.ds(pl.multiple_of(HALF + j * 256, 256), 256)
        noisy = nz_rows
        ca, sa = dot(oha[...], tab[0, :, c0]), dot(oha[...], tab[1, :, c0])
        cb, sb = dot(ohb[...], tab[2, :, c0]), dot(ohb[...], tab[3, :, c0])
        le[:, c0] = ca * cb - sa * sb + dot(noisy, lin_ref[:, c0])
        le[:, c1] = sa * cb + ca * sb + dot(noisy, lin_ref[:, c1])
        return carry

    lax.fori_loop(0, HALF // 256, embed, 0)

    other(p1_fin, "gu")
    other(p2_send, "gu", 2)
    landed(dn.at[1 - xl, jnp.where(xl == 1, y * 4 + z, zy)], "xdn", (mate, h))
    both(p1_send, "dn")
    both(p2_fwd, "gu", 0)
    for d in (0, 1, 3, 2):
        both(p2_fin, "kv", d)

    n_steps = lax.div(s, 2) + 1

    def keys_of(c):
        blocks = kv.at[lax.div(c, 8), pl.ds(lax.rem(c, 8) * 2, 2)]
        return blocks[:, 0:TOK, :].reshape(KC, HD), blocks[:, TOK : 2 * TOK, :].reshape(KC, HD)

    def scores_of(c, masked):
        score = dot(keys_of(c)[0], qt[...]) * (SCALE * LOG2E)
        if masked:
            key_pos = c * KC + lax.broadcasted_iota(jnp.int32, (KC, ROWS), 0)
            query_pos = s * TOK + (lax.broadcasted_iota(jnp.int32, (KC, ROWS), 1) & (TOK - 1))
            score = jnp.where(key_pos <= query_pos, score, NEG)
        return score

    def fold(values, reduce):
        return reduce(values.reshape(KC // 8, 8, ROWS), axis=0)

    def max_step(c, run, masked=False):
        return jnp.maximum(run, fold(scores_of(c, masked), jnp.max))

    row_max = lax.fori_loop(0, n_steps - 1, max_step, jnp.full((8, ROWS), NEG, F32))
    row_max = max_step(n_steps - 1, row_max, True)
    row_max = jnp.max(row_max, axis=0, keepdims=True)
    both(p2_fwd, "gu", 1)
    both(p1_fwd, "dn")

    acc_t[...] = jnp.zeros_like(acc_t)

    def sum_step(c, run, masked=False):
        soft = jnp.exp2(scores_of(c, masked) - row_max)
        soft_b = soft.astype(BF16)
        probs[pl.ds(pl.multiple_of(c * KC, KC), KC), :] = soft_b
        acc_t[...] += contract_rows(keys_of(c)[1], soft_b)
        return run + fold(soft, jnp.sum)

    total = lax.fori_loop(0, n_steps - 1, sum_step, jnp.zeros((8, ROWS), F32))
    total = sum_step(n_steps - 1, total, True)
    total = jnp.sum(total, axis=0, keepdims=True)
    inverse = 1.0 / total
    out_t = (acc_t[...] / total).astype(BF16)
    delta = jnp.sum(out_t.astype(F32) * dot_t[...].astype(F32), axis=0, keepdims=True)
    for j in range(GRP):
        cols = slice(j * HD, (j + 1) * HD)
        out_ref[:, cols] = out_t[:, cols].astype(F32).T.astype(BF16)

    mask = mask_ref[...]
    ones = jnp.broadcast_to(mask.astype(F32), (8, TOK)).astype(BF16)
    before = lax.broadcasted_iota(jnp.int32, (TOK, TOK), 0) <= lax.broadcasted_iota(jnp.int32, (TOK, TOK), 1)
    rank = dot(ones, jnp.where(before, 1.0, 0.0).astype(BF16))[0:1, :] - 1.0
    slot = lax.broadcasted_iota(jnp.int32, (CAP, TOK), 0).astype(F32)
    chosen = jnp.where(rank == slot, jnp.where(mask == 1, 1.0, 0.0), 0.0)
    valid = jnp.sum(chosen, axis=1, keepdims=True) > 0.5
    cond[xl, h] = dot(chosen.astype(BF16), out_ref[...]).astype(BF16)
    cond_sent = []
    for i, (dx, dh) in enumerate(line):
        copy = pltpu.make_async_remote_copy(
            src_ref=cond.at[xl, h], dst_ref=cond.at[xl, h], send_sem=cssem.at[i],
            recv_sem=crsem.at[xl * N_HEAD + h], device_id=on_line(dx, dh)[2], device_id_type=MESH,
        )
        copy.start()
        cond_sent.append(copy)

    both(p2_fwd, "gu", 3)

    acc_t[...] = jnp.zeros_like(acc_t)

    def grad_step(c, carry):
        keys, values = keys_of(c)
        prob = probs[pl.ds(pl.multiple_of(c * KC, KC), KC), :].astype(F32) * inverse
        ds = (prob * (dot(values, dot_t[...]) - delta)).astype(BF16)
        acc_t[...] += contract_rows(keys, ds)
        dkv[pl.ds(2 * c, 2), 0:TOK, :] = (dot(ds, qs[...]) * SCALE).astype(BF16).reshape(2, TOK, HD)
        dkv[pl.ds(2 * c, 2), TOK : 2 * TOK, :] = dot(prob.astype(BF16), dos[...]).astype(BF16).reshape(2, TOK, HD)
        return carry

    def cross_copy(kb):
        return pltpu.make_async_remote_copy(
            src_ref=dkv.at[kb], dst_ref=mterm.at[kb], send_sem=xssem.at[kb], recv_sem=xrsem.at[kb],
            device_id=(mate, h), device_id_type=MESH,
        )

    for part in range(4):
        lax.fori_loop(part * 4, jnp.minimum(n_steps, part * 4 + 4), grad_step, 0)
        if part == 0:
            both(p2_fwd, "gu", 2)
            both(p1_fin, "dn")
            both(p2_send, "dn", 0)
            both(p2_send, "dn", 1)
        elif part == 1:

            def send_cross(kb, carry):
                cross_copy(kb).start()
                return carry

            @pl.when(xl == 1)
            def _():
                lax.fori_loop(0, 16, send_cross, 0)

    for j in range(GRP):
        cols = slice(j * HD, (j + 1) * HD)
        dq_ref[:, cols] = (acc_t[:, cols] * SCALE).T.astype(BF16)

    for dx, dh in line:
        ox, oh, dev = on_line(dx, dh)
        pltpu.make_async_remote_copy(
            src_ref=cond.at[ox, oh], dst_ref=cond.at[ox, oh], send_sem=cssem.at[0],
            recv_sem=crsem.at[ox * N_HEAD + oh], device_id=dev, device_id_type=MESH,
        ).wait_recv()

    def norm_rows(g, carry):
        rows = pl.ds(pl.multiple_of(g * CAP, CAP), CAP)
        square = jnp.zeros((CAP, 1), F32)
        for hh in range(N_HEAD):
            cols = slice(hh * HEADW, (hh + 1) * HEADW)
            base = le[rows, cols] + cond[lax.rem(g, 2), hh].astype(F32)
            le[rows, cols] = base
            square += jnp.sum(base * base, axis=1, keepdims=True)
        scale = lax.rsqrt(square * (1.0 / D) + 1e-06)
        for hh in range(N_HEAD):
            cols = slice(hh * HEADW, (hh + 1) * HEADW)
            nm[rows, cols] = (le[rows, cols] * scale * ngain_ref[cols].reshape(1, HEADW)).astype(BF16)
        return carry

    lax.fori_loop(0, 2 * NOISE, norm_rows, 0)
    for d in (0, 1, 3, 2):
        both(p2_fin, "gu", d)

    SUB = 4 * FEAT
    mine = pl.ds(pl.multiple_of((core * 4 + x) * CAP, CAP), CAP)
    for at in range(4):
        for other_at in range(4):
            c0 = other_at * SUB + at * FEAT
            to = slice(other_at * FEAT, (other_at + 1) * FEAT)
            fin[0, at, :, to] = le[mine, c0 : c0 + FEAT]
            og[0, at, :, to] = jnp.broadcast_to(ogain_ref[c0 : c0 + FEAT].reshape(1, FEAT), (8, FEAT))
            lo[0, at, :, to] = lout_ref[:, c0 : c0 + FEAT]
        c1 = HALF + at * SUB
        fin[1, at] = le[mine, c1 : c1 + SUB]
        og[1, at] = jnp.broadcast_to(ogain_ref[c1 : c1 + SUB].reshape(1, SUB), (8, SUB))
        lo[1, at] = lout_ref[:, c1 : c1 + SUB]

    for k in range(4):
        piece = gu[k // 2, (k % 2) * 8 : (k % 2) * 8 + 8].reshape(8 * FEAT, GUW)
        part = dot(nm[:, k * 896 : (k + 1) * 896], piece)
        if k == 0:
            acc[...] = part
        else:
            acc[...] += part
        if k == 1:
            both(p2_fwd, "dn", 0)
            both(p2_send, "dn", 3)

    both(p2_fwd, "dn", 1)
    both(p2_send, "dn", 2)

    def silu(value):
        return value / (1.0 + jnp.exp(-value))

    mixed = acc[:, 2 * MAIN :]
    turned = pltpu.roll(mixed, 64, 1)
    lower_half = lax.broadcasted_iota(jnp.int32, (2 * NOISE * CAP, 128), 1) < 64

    @pl.when(xl == 0)
    def _():
        hid[:, 0:MAIN] = (silu(acc[:, 0:MAIN]) * acc[:, MAIN : 2 * MAIN]).astype(BF16)
        hid[:, MAIN:DNW] = jnp.where(lower_half, silu(mixed) * turned, 0.0).astype(BF16)

    @pl.when(xl == 1)
    def _():
        hid[:, 128:DNW] = (silu(acc[:, 0:MAIN]) * acc[:, MAIN : 2 * MAIN]).astype(BF16)
        hid[:, 0:128] = jnp.where(lower_half, 0.0, silu(turned) * mixed).astype(BF16)

    def term_copy(b, kb):
        return pltpu.make_async_remote_copy(
            src_ref=dkv.at[b * 16 + kb], dst_ref=drecv.at[b, zy], send_sem=dssem.at[b * 16 + kb],
            recv_sem=drsem.at[b * 16 + zy], device_id=(xl * 16 + kb, h), device_id_type=MESH,
        )

    def forward_copy(kb):
        return pltpu.make_async_remote_copy(
            src_ref=mterm.at[kb], dst_ref=drecv.at[0, zy], send_sem=dssem.at[kb], recv_sem=drsem.at[zy],
            device_id=(kb, h), device_id_type=MESH,
        )

    def some_terms(first, last):
        def step(i, carry):
            kb = lax.rem(zy + i, 16)

            @pl.when(xl == 0)
            def _():
                cross_copy(kb).wait_recv()

                @pl.when(kb < zy)
                def _():
                    mterm[kb] = (mterm[kb].astype(F32) + dkv[kb].astype(F32)).astype(BF16)

                forward_copy(kb).start()

            pl.when((xl == 1) & (kb < zy))(lambda: term_copy(1, kb).start())
            return carry

        lax.fori_loop(first, last, step, 0)

    def add_terms(first, last):
        def step(i, carry):
            src = lax.rem(zy + 16 - i, 16)

            @pl.when((xl == 0) | (src > zy))
            def _():
                pltpu.make_async_remote_copy(
                    src_ref=drecv.at[xl, src], dst_ref=drecv.at[xl, src], send_sem=dssem.at[0],
                    recv_sem=drsem.at[xl * 16 + src], device_id=(mate, h), device_id_type=MESH,
                ).wait_recv()
                tsum[...] += drecv[xl, src].astype(F32)

            return carry

        lax.fori_loop(first, last, step, 0)

    def along_x(step):
        to = lax.rem(x + 4 + step, 4)
        return (lax.rem(to, 2) * 16 + zy, lax.div(to, 2) * 2 + core)

    def pick(step):
        return lax.rem(x + 4 + step, 4) * CAP

    order = (0, 1, 3, 2)

    def lanes(k):
        return slice(k * 512, k * 512 + SUB)

    def tot(k, r, step):
        first = pl.multiple_of(r * 256 + pick(step), CAP)
        return acc[pl.ds(first, CAP), lanes(k % 2)]

    sibling = (s, h + 1 - 2 * core)

    def stage0(k):
        for r in (0, 1):
            p2_fin("dn", r, order[k])
        pieces = []
        for r in (0, 1):
            at = back(y if r == 0 else z, order[k]) * 4
            piece = dn[r, pl.ds(at, 4)].reshape(SUB, DNW)
            pieces.append(piece)
            theirs = hid[pl.ds(pl.multiple_of((1 - core) * 256, 256), 256), :]
            part = lax.dot_general(theirs, piece, (((1,), (1,)), ((), ())), preferred_element_type=F32)
            s1[k, r] = part.astype(BF16)
            start(lambda r=r: (s1.at[k, r], r1.at[k, r], sibling), ("r1", k, r))
        for r in (0, 1):
            ours = hid[pl.ds(pl.multiple_of(core * 256, 256), 256), :]
            acc[r * 256 : r * 256 + 256, lanes(k % 2)] = lax.dot_general(ours, pieces[r], (((1,), (1,)), ((), ())), preferred_element_type=F32)

    def stage1(k):
        for r in (0, 1):
            landed(r1.at[k, r], ("r1", k, r), sibling)
            far = r1[k, r, pl.ds(pl.multiple_of(pick(2), CAP), CAP), :].astype(F32)
            s23[0, k, r] = (tot(k, r, 2) + far).astype(BF16)
            start(lambda r=r: (s23.at[0, k, r], r2.at[k, r], along_x(1 - 2 * r)), ("r2", k, r))
        for r in (0, 1):
            acc[r * 256 : r * 256 + 256, lanes(k % 2)] += r1[k, r].astype(F32)

    def stage2(k):
        for r in (0, 1):
            landed(r2.at[k, r], ("r2", k, r), along_x(1))
            for way, step in ((0, 1), (1, -1)):
                near = tot(k, r, step)
                if way == r:
                    near += r2[k, r].astype(F32)
                s23[1 + way, k, r] = near.astype(BF16)
                start(
                    lambda r=r, way=way, step=step: (s23.at[1 + way, k, r], r3.at[k, r, way], along_x(step)),
                    ("r3", k, r, way),
                )
            fin[r, back(y if r == 0 else z, order[k])] += tot(k, r, 0)

    def stage3(k):
        for r in (0, 1):
            at = back(y if r == 0 else z, order[k])
            for way in (0, 1):
                landed(r3.at[k, r, way], ("r3", k, r, way), along_x(1))
                fin[r, at] += r3[k, r, way].astype(F32)

    stage0(0)
    both(p2_fwd, "dn", 3)
    stage1(0)
    stage0(1)
    stage2(0)
    stage1(1)
    both(p2_fwd, "dn", 2)
    some_terms(1, 16)
    stage2(1)
    stage0(2)
    stage1(2)
    stage0(3)
    stage2(2)
    stage1(3)
    tsum[...] = dkv[s].astype(F32)
    add_terms(1, 4)
    stage2(3)
    add_terms(4, 8)
    for k in range(4):
        stage3(k)

    square = jnp.zeros((CAP, 1), F32)
    for r in (0, 1):
        for at in range(4):
            rows = fin[r, at]
            square += jnp.sum(rows * rows, axis=1, keepdims=True)
    scale = lax.rsqrt(square * (1.0 / D) + 1e-06)
    result = jnp.zeros((CAP, LAT), F32)
    for r in (0, 1):
        for at in range(4):
            final = (fin[r, at] * scale * og[r, at, 0:1, :]).astype(BF16)
            result += lax.dot_general(final, lo[r, at], (((1,), (1,)), ((), ())), preferred_element_type=F32)
    pred_ref[...] = jnp.where(valid, result, 0.0)

    @pl.when(xl == 0)
    def _():
        cross_copy(zy).wait_recv()
        tsum[...] += mterm[zy].astype(F32)

    add_terms(8, 16)
    dk_ref[...] = tsum[0:TOK].astype(BF16)
    dv_ref[...] = tsum[TOK : 2 * TOK].astype(BF16)

    all_left()
    for copy in cond_sent:
        copy.wait_send()

    def left(copy):
        def step(kb, carry):
            copy(kb).wait_send()
            return carry

        return step

    @pl.when(xl == 1)
    def _():
        lax.fori_loop(0, 16, left(cross_copy), 0)
        lax.fori_loop(0, zy, left(lambda kb: term_copy(1, kb)), 0)

    @pl.when(xl == 0)
    def _():
        lax.fori_loop(0, zy, left(forward_copy), 0)
        lax.fori_loop(zy + 1, 16, left(forward_copy), 0)


def hand_over(*refs):
    for i in range(5):
        refs[5 + i][...] = refs[i][...]


def shards(
    queries, key_vectors, value_vectors, out_cotangent, latent_mask, clean_latents, noise_draws, timesteps,
    latent_in, norm_gain, gate_weight, up_weight, down_weight, out_gain, latent_out,
):
    frequencies = np.exp(-math.log(10000.0) * np.arange(HALF, dtype=np.float32) / HALF).astype(np.float32)
    vmem = pl.BlockSpec(memory_space=pltpu.VMEM)
    hbm = pl.BlockSpec(memory_space=pl.ANY)
    dma = pltpu.SemaphoreType.DMA
    n_sems = 176
    results = pl.pallas_call(
        kernel,
        out_shape=(
            jax.ShapeDtypeStruct((TOK, ROWS), BF16),
            jax.ShapeDtypeStruct((TOK, ROWS), BF16),
            jax.ShapeDtypeStruct((TOK, HD), BF16),
            jax.ShapeDtypeStruct((TOK, HD), BF16),
            jax.ShapeDtypeStruct((CAP, LAT), F32),
        ),
        in_specs=[hbm if i in (0, 3, 5, 6, 8, 12, 14) else vmem for i in range(16)],
        out_specs=(vmem,) * 5,
        scratch_shapes=[
            pltpu.VMEM((2, 16, 2 * TOK, HD), BF16),
            pltpu.VMEM((2, 16, FEAT, GUW), BF16),
            pltpu.VMEM((2, 16, FEAT, DNW), BF16),
            pltpu.VMEM((FEAT, GUW), BF16),
            pltpu.VMEM((FEAT, DNW), BF16),
            pltpu.VMEM((ROWS, HD), BF16),
            pltpu.VMEM((HD, ROWS), BF16),
            pltpu.VMEM((ROWS, HD), BF16),
            pltpu.VMEM((HD, ROWS), BF16),
            pltpu.VMEM((N_SEQ * TOK, ROWS), BF16),
            pltpu.VMEM((HD, ROWS), F32),
            pltpu.VMEM((N_SEQ, 2 * TOK, HD), BF16),
            pltpu.VMEM((2, 16, 2 * TOK, HD), BF16),
            pltpu.VMEM((2, N_HEAD, CAP, HEADW), BF16),
            pltpu.VMEM((2, NOISE * CAP, 128), BF16),
            pltpu.VMEM((2, CAP, 128), jnp.int32),
            pltpu.VMEM((4, 128, HALF), BF16),
            pltpu.VMEM((2 * NOISE * CAP, 128), BF16),
            pltpu.VMEM((2 * NOISE * CAP, 128), BF16),
            pltpu.VMEM((2 * NOISE * CAP, D), F32),
            pltpu.VMEM((2 * NOISE * CAP, D), BF16),
            pltpu.VMEM((2 * NOISE * CAP, GUW), F32),
            pltpu.VMEM((2 * NOISE * CAP, DNW), BF16),
            pltpu.VMEM((4, 2, 4 * CAP, 4 * FEAT), BF16),
            pltpu.VMEM((3, 4, 2, CAP, 4 * FEAT), BF16),
            pltpu.VMEM((4, 2, 4 * CAP, 4 * FEAT), BF16),
            pltpu.VMEM((4, 2, CAP, 4 * FEAT), BF16),
            pltpu.VMEM((4, 2, 2, CAP, 4 * FEAT), BF16),
            pltpu.VMEM((2, 4, CAP, 4 * FEAT), F32),
            pltpu.VMEM((2, 4, 8, 4 * FEAT), F32),
            pltpu.VMEM((2, 4, LAT, 4 * FEAT), BF16),
            pltpu.VMEM((16, 2 * TOK, HD), BF16),
            pltpu.VMEM((2 * TOK, HD), F32),
            pltpu.VMEM((TOK, ROWS), BF16),
            pltpu.VMEM((TOK, ROWS), BF16),
            pltpu.VMEM((CAP, LAT), F32),
            pltpu.VMEM((CAP, NOISE * LAT), F32),
            pltpu.VMEM((LAT, D), BF16),
            pltpu.VMEM((FEAT, 1408), BF16),
            pltpu.VMEM((LAT, D), BF16),
            dma((n_sems,)),
            dma((n_sems,)),
            dma((N_SEQ,)),
            dma((N_SEQ,)),
            dma((7,)),
            dma((8,)),
            dma((16,)),
            dma((16,)),
            dma((7,)),
        ],
        compiler_params=pltpu.CompilerParams(
            collective_id=0, has_side_effects=True, vmem_limit_bytes=63 * 1024 * 1024
        ),
    )(
        queries, key_vectors, value_vectors, out_cotangent, latent_mask.reshape(1, TOK), clean_latents, noise_draws,
        timesteps.T, latent_in, norm_gain, gate_weight, up_weight, down_weight, out_gain,
        latent_out.T, jnp.asarray(frequencies.reshape(1, HALF)),
    )
    return pl.pallas_call(
        hand_over,
        out_shape=tuple(jax.ShapeDtypeStruct(a.shape, a.dtype) for a in results),
        in_specs=[vmem] * 5,
        out_specs=(vmem,) * 5,
        compiler_params=pltpu.CompilerParams(vmem_limit_bytes=63 * 1024 * 1024),
    )(*results)


def solution(mesh):
    placed = (
        P("seq", "head"),
        P("seq", "head"),
        P("seq", "head"),
        P("seq", "head"),
        P("seq"),
        P("seq", None),
        P("seq", None),
        P("seq", None),
        P(),
        P(),
        P("seq", "head"),
        P("seq", "head"),
        P("seq", "head"),
        P(),
        P(),
    )
    return jax.shard_map(
        shards,
        mesh=mesh,
        in_specs=placed,
        out_specs=(P("seq", "head"),) * 5,
        check_vma=False,
    )
```

```python
import math

import jax
import jax.numpy as jnp
import numpy as np
from jax import lax
from jax.experimental import pallas as pl
from jax.experimental.pallas import tpu as pltpu
from jax.sharding import PartitionSpec as P

MESH = pl.DeviceIdType.MESH
F32 = jnp.float32
BF16 = jnp.bfloat16

HD = 128
GRP = 7
TOK = 128
ROWS = GRP * TOK
D = 3584
HALF = D // 2
LAT = 64
CAP = 64
NOISE = 4
N_SEQ = 32
N_HEAD = 4
FEAT = 112
GUW = 1408
DNW = 768
MAIN = 640
KC = 256
HEADW = D // N_HEAD
SCALE = 1.0 / math.sqrt(HD)
LOG2E = math.log2(math.e)
NEG = -1e30

HALVES = {"kv": ((0, 128), (128, 128)), "gu": ((0, 64), (64, 48)), "dn": ((0, 64), (64, 48))}


def contract_rows(left, right):
    return lax.dot_general(left, right, (((0,), (0,)), ((), ())), preferred_element_type=F32)


def dot(left, right):
    return jnp.dot(left, right, preferred_element_type=F32)


def kernel(
    q_hbm, k_ref, v_ref, do_hbm, mask_ref, clean_hbm, noise_hbm, time_ref, lin_hbm, ngain_ref,
    gate_ref, up_ref, down_hbm, ogain_ref, lout_hbm, freq_ref,
    out_ref, dq_ref, dk_ref, dv_ref, pred_ref,
    kv, gu, dn, sgu, sdn, qs, qt, dos, dot_t, probs, acc_t, dkv, drecv, cond, nz, tm, tab, oha, ohb,
    le, nm, acc, hid, s1, s23, r1, r2, r3, fin, og, lo, mterm, tsum, rterm,
    q_ref, do_ref, clean_ref, noise_ref, lin_ref, down_ref, lout_ref,
    ssem, rsem, dssem, drsem, cssem, crsem, xssem, xrsem, fsem, rssem, rrsem,
):
    fetched = [
        pltpu.make_async_copy(src, dst, fsem.at[i])
        for i, (src, dst) in enumerate(
            (
                (down_hbm, down_ref),
                (clean_hbm, clean_ref),
                (noise_hbm, noise_ref),
                (q_hbm, q_ref),
                (do_hbm, do_ref),
                (lin_hbm, lin_ref),
                (lout_hbm, lout_ref),
            )
        )
    ]
    for copy in fetched:
        copy.start()
    s = lax.axis_index("seq")
    h = lax.axis_index("head")
    xl = lax.div(s, 16)
    zy = lax.rem(s, 16)
    core = lax.rem(h, 2)
    x = lax.div(h, 2) * 2 + xl
    z = lax.div(zy, 4)
    y = lax.rem(zy, 4)
    mate = (1 - xl) * 16 + zy

    bufs = {"kv": kv, "gu": gu, "dn": dn}
    sem_at = {}
    leaving = {}

    def copy_of(src, dst, key, dev):
        at = sem_at.setdefault(key, len(sem_at))
        return pltpu.make_async_remote_copy(
            src_ref=src, dst_ref=dst, send_sem=ssem.at[at], recv_sem=rsem.at[at], device_id=dev, device_id_type=MESH
        )

    def start(make, key):
        src, dst, dev = make()
        copy_of(src, dst, key, dev).start()
        leaving[key] = make

    def landed(dst, key, dev):
        copy_of(dst, dst, key, dev).wait_recv()

    def all_left():
        for key, make in leaving.items():
            if key[:2] != ("kv", 1):
                src, dst, dev = make()
                copy_of(src, dst, key, dev).wait_send()

        @pl.when(xl == 1)
        def _():
            for key, make in leaving.items():
                if key[:2] == ("kv", 1):
                    src, dst, dev = make()
                    copy_of(src, dst, key, dev).wait_send()

    def back(pos, dist):
        return lax.rem(pos + 4 - dist, 4)

    def chunk(p, r, d1, d2, half):
        dy, dz = (d1, d2) if r == 0 else (d2, d1)
        pz, py = back(z, dz), back(y, dy)
        view = bufs[p].at[r, py * 4 + pz if p == "dn" and r == 0 else pz * 4 + py]
        if half is None:
            return view
        first, count = HALVES[p][half]
        return view.at[pl.ds(first, count)]

    def neighbour(r, axis, step):
        along_y = (axis == 1) == (r == 0)
        if along_y:
            return (xl * 16 + z * 4 + back(y, -step), h)
        return (xl * 16 + back(z, -step) * 4 + y, h)

    def send(p, r, d1, d2, axis, step, half=None):
        e1 = (d1 + step) % 4 if axis == 1 else d1
        e2 = (d2 + step) % 4 if axis == 2 else d2

        def make():
            ref = chunk(p, r, d1, d2, half)
            return ref, ref, neighbour(r, axis, step)

        start(make, (p, r, e1, e2, half))

    def wait(p, r, d1, d2, half=None):
        landed(chunk(p, r, d1, d2, half), (p, r, d1, d2, half), (mate, h))

    def p1_send(p, r):
        send(p, r, 0, 0, 1, 1)
        send(p, r, 0, 0, 1, -1)

    def first_sends(p, r):
        p1_send(p, r)
        p2_send(p, r, 0)

    def own(step, p, *rest):
        for r in (0, 1):
            pl.when(xl == r)(lambda r=r: step(p, r, *rest))

    def other(step, p, *rest):
        for r in (0, 1):
            if p == "kv" and r == 1:
                continue
            pl.when(xl != r)(lambda r=r: step(p, r, *rest))

    def p1_fwd(p, r):
        wait(p, r, 1, 0)
        send(p, r, 1, 0, 1, 1, 0)
        wait(p, r, 3, 0)
        send(p, r, 3, 0, 1, -1, 1)

    def p1_fin(p, r):
        wait(p, r, 2, 0, 0)
        wait(p, r, 2, 0, 1)

    def p2_send(p, r, d1):
        send(p, r, d1, 0, 2, 1)
        send(p, r, d1, 0, 2, -1)

    def p2_fwd(p, r, d1):
        wait(p, r, d1, 1)
        send(p, r, d1, 1, 2, 1, d1 % 2)
        wait(p, r, d1, 3)
        send(p, r, d1, 3, 2, -1, 1 - d1 % 2)

    def p2_fin(p, r, d1):
        wait(p, r, d1, 2, 0)
        wait(p, r, d1, 2, 1)

    def both(step, p, *rest):
        step(p, 0, *rest)
        if p == "kv":
            pl.when(xl == 1)(lambda: step(p, 1, *rest))
        else:
            step(p, 1, *rest)

    barrier = pltpu.get_barrier_semaphore()

    line = [(dx, dh) for dx in (0, 1) for dh in range(N_HEAD) if (dx, dh) != (0, 0)]

    def on_line(dx, dh):
        ox = lax.rem(xl + dx, 2)
        oh = lax.rem(h + dh, N_HEAD)
        return ox, oh, (ox * 16 + zy, oh)

    for dx, dh in line:
        pl.semaphore_signal(barrier, inc=1, device_id=on_line(dx, dh)[2], device_id_type=MESH)
    for axis in (1, 2):
        for step in (1, -1):
            pl.semaphore_signal(barrier, inc=1, device_id=neighbour(0, axis, step), device_id_type=MESH)
    pl.semaphore_wait(barrier, 7 + 4)

    low = lax.broadcasted_iota(jnp.int32, (FEAT, 128), 1) < 64

    def pack_gu(f, put):
        at = f * 768
        mid_gate = gate_ref[:, MAIN : MAIN + 128].astype(F32)
        mid_up = up_ref[:, MAIN : MAIN + 128].astype(F32)
        if f == 0:
            mixed = jnp.where(low, mid_gate, pltpu.roll(mid_up, 64, 1))
        else:
            mixed = jnp.where(low, pltpu.roll(mid_gate, 64, 1), mid_up)
        put(0, gate_ref[:, at : at + MAIN])
        put(MAIN, up_ref[:, at : at + MAIN])
        put(2 * MAIN, mixed.astype(BF16))

    def own_gu(at, value):
        gu[xl, zy, :, at : at + value.shape[1]] = value

    def mate_gu(at, value):
        sgu[:, at : at + value.shape[1]] = value

    def same(ref):
        return lambda: (ref, ref, (mate, h))

    dn_at = jnp.where(xl == 0, y * 4 + z, zy)
    kv[xl, zy, 0:TOK, :] = k_ref[...]
    kv[xl, zy, TOK : 2 * TOK, :] = v_ref[...]
    start(same(kv.at[xl, zy]), "xkv")
    own(first_sends, "kv")
    for f in (0, 1):
        pl.when(xl == f)(lambda f=f: pack_gu(f, own_gu))
    own(first_sends, "gu")
    for f in (0, 1):
        pl.when(xl == f)(lambda f=f: pack_gu(1 - f, mate_gu))
    start(lambda: (sgu, gu.at[xl, zy], (mate, h)), "xgu")
    landed(kv.at[1 - xl, zy], "xkv", (mate, h))
    other(first_sends, "kv")
    own(p1_fwd, "kv")
    own(p2_send, "kv", 1)
    own(p2_send, "kv", 3)

    for copy in fetched:
        copy.wait()
    for f in (0, 1):

        @pl.when(xl == f)
        def _():
            sdn[...] = down_ref[:, (1 - f) * MAIN : (1 - f) * MAIN + DNW]
            dn[xl, dn_at] = down_ref[:, f * MAIN : f * MAIN + DNW]

    start(lambda: (sdn, dn.at[xl, dn_at], (mate, h)), "xdn")

    digits = jnp.concatenate([time_ref[...] >> 5, time_ref[...] & 31], axis=0).astype(F32).astype(BF16)
    unit = lax.broadcasted_iota(jnp.int32, (2 * NOISE, 128), 0) == lax.broadcasted_iota(jnp.int32, (2 * NOISE, 128), 1)
    columns = contract_rows(digits, jnp.where(unit, 1.0, 0.0).astype(BF16))
    steps_own = columns[:, 0:NOISE] * 32.0 + columns[:, NOISE : 2 * NOISE]
    share = jnp.cos((steps_own / 1000.0 + 0.008) / 1.008 * (math.pi / 2.0)) ** 2
    signal, noise_part = jnp.sqrt(share), jnp.sqrt(1.0 - share)
    nz[xl] = jnp.zeros((NOISE * CAP, 128), BF16)
    tm[xl] = columns.astype(jnp.int32)
    for n in range(NOISE):
        row = signal[:, n : n + 1] * clean_ref[...] + noise_part[:, n : n + 1] * noise_ref[:, n * LAT : (n + 1) * LAT]
        nz[xl, n * CAP : (n + 1) * CAP, 0:LAT] = row.astype(BF16)
    start(same(nz.at[xl]), "xnz")
    start(same(tm.at[xl]), "xtm")


    for j in range(GRP):
        cols = slice(j * HD, (j + 1) * HD)
        qs[cols, :] = q_ref[:, cols]
        dos[cols, :] = do_ref[:, cols]
        qt[:, cols] = q_ref[:, cols].astype(F32).T.astype(BF16)
        dot_t[:, cols] = do_ref[:, cols].astype(F32).T.astype(BF16)

    landed(gu.at[1 - xl, zy], "xgu", (mate, h))
    other(first_sends, "gu")
    other(p1_fwd, "kv")
    other(p2_send, "kv", 1)
    other(p2_send, "kv", 3)
    both(p1_fin, "kv")
    both(p2_send, "kv", 2)
    own(p1_fwd, "gu")
    own(p2_send, "gu", 1)

    steps = lax.broadcasted_iota(jnp.int32, (32, HALF), 0).astype(F32)
    for k, mult in ((0, 32.0), (2, 1.0)):
        angle = (steps * mult) * freq_ref[...]
        for kk, value in ((k, jnp.cos(angle)), (k + 1, jnp.sin(angle))):
            high = value.astype(BF16)
            rest = value - high.astype(F32)
            middle = rest.astype(BF16)
            tab[kk, 0:32, :] = high
            tab[kk, 32:64, :] = middle
            tab[kk, 64:96, :] = (rest - middle.astype(F32)).astype(BF16)
            tab[kk, 96:128, :] = jnp.zeros((32, HALF), BF16)

    both(p2_fwd, "kv", 0)
    both(p2_fwd, "kv", 1)
    own(p2_send, "gu", 3)
    both(p2_fwd, "kv", 3)
    both(p2_fwd, "kv", 2)
    own(p1_fin, "gu")
    other(p1_fwd, "gu")
    other(p2_send, "gu", 1)
    own(p2_send, "gu", 2)
    other(p2_send, "gu", 3)

    landed(nz.at[1 - xl], "xnz", (mate, h))
    landed(tm.at[1 - xl], "xtm", (mate, h))
    lane = lax.broadcasted_iota(jnp.int32, (CAP, 128), 1)
    for b in (0, 1):
        for n in range(NOISE):
            place = (n % 2) * 4 + (n // 2) * 2 + b
            rows = slice(place * CAP, (place + 1) * CAP)
            for ref, digit in ((oha, tm[b, :, n : n + 1]), (ohb, tm[b, :, NOISE + n : NOISE + n + 1])):
                ref[rows, :] = jnp.where((lane & 31) == digit, jnp.where(lane < 96, 1.0, 0.0), 0.0).astype(BF16)

    nz_rows = jnp.concatenate(
        [nz[g % 2, ((g // 2 % 2) * 2 + g // 4) * CAP : ((g // 2 % 2) * 2 + g // 4 + 1) * CAP, 0:LAT] for g in range(8)], axis=0
    )

    def embed(j, carry):
        c0 = pl.ds(pl.multiple_of(j * 256, 256), 256)
        c1 = pl.ds(pl.multiple_of(HALF + j * 256, 256), 256)
        noisy = nz_rows
        ca, sa = dot(oha[...], tab[0, :, c0]), dot(oha[...], tab[1, :, c0])
        cb, sb = dot(ohb[...], tab[2, :, c0]), dot(ohb[...], tab[3, :, c0])
        le[:, c0] = ca * cb - sa * sb + dot(noisy, lin_ref[:, c0])
        le[:, c1] = sa * cb + ca * sb + dot(noisy, lin_ref[:, c1])
        return carry

    lax.fori_loop(0, HALF // 256, embed, 0)

    other(p1_fin, "gu")
    other(p2_send, "gu", 2)
    landed(dn.at[1 - xl, jnp.where(xl == 1, y * 4 + z, zy)], "xdn", (mate, h))
    both(p1_send, "dn")
    both(p2_fwd, "gu", 0)
    for d in (0, 1, 3, 2):
        both(p2_fin, "kv", d)

    n_steps = lax.div(s, 2) + 1

    def keys_of(c):
        blocks = kv.at[lax.div(c, 8), pl.ds(lax.rem(c, 8) * 2, 2)]
        return blocks[:, 0:TOK, :].reshape(KC, HD), blocks[:, TOK : 2 * TOK, :].reshape(KC, HD)

    def scores_of(c, masked):
        score = dot(keys_of(c)[0], qt[...]) * (SCALE * LOG2E)
        if masked:
            key_pos = c * KC + lax.broadcasted_iota(jnp.int32, (KC, ROWS), 0)
            query_pos = s * TOK + (lax.broadcasted_iota(jnp.int32, (KC, ROWS), 1) & (TOK - 1))
            score = jnp.where(key_pos <= query_pos, score, NEG)
        return score

    def fold(values, reduce):
        return reduce(values.reshape(KC // 8, 8, ROWS), axis=0)

    def max_step(c, run, masked=False):
        return jnp.maximum(run, fold(scores_of(c, masked), jnp.max))

    row_max = lax.fori_loop(0, n_steps - 1, max_step, jnp.full((8, ROWS), NEG, F32))
    row_max = max_step(n_steps - 1, row_max, True)
    row_max = jnp.max(row_max, axis=0, keepdims=True)
    both(p2_fwd, "gu", 1)
    both(p1_fwd, "dn")

    acc_t[...] = jnp.zeros_like(acc_t)

    def sum_step(c, run, masked=False):
        soft = jnp.exp2(scores_of(c, masked) - row_max)
        soft_b = soft.astype(BF16)
        probs[pl.ds(pl.multiple_of(c * KC, KC), KC), :] = soft_b
        acc_t[...] += contract_rows(keys_of(c)[1], soft_b)
        return run + fold(soft, jnp.sum)

    total = lax.fori_loop(0, n_steps - 1, sum_step, jnp.zeros((8, ROWS), F32))
    total = sum_step(n_steps - 1, total, True)
    total = jnp.sum(total, axis=0, keepdims=True)
    inverse = 1.0 / total
    out_t = (acc_t[...] / total).astype(BF16)
    delta = jnp.sum(out_t.astype(F32) * dot_t[...].astype(F32), axis=0, keepdims=True)
    for j in range(GRP):
        cols = slice(j * HD, (j + 1) * HD)
        out_ref[:, cols] = out_t[:, cols].astype(F32).T.astype(BF16)

    mask = mask_ref[...]
    ones = jnp.broadcast_to(mask.astype(F32), (8, TOK)).astype(BF16)
    before = lax.broadcasted_iota(jnp.int32, (TOK, TOK), 0) <= lax.broadcasted_iota(jnp.int32, (TOK, TOK), 1)
    rank = dot(ones, jnp.where(before, 1.0, 0.0).astype(BF16))[0:1, :] - 1.0
    slot = lax.broadcasted_iota(jnp.int32, (CAP, TOK), 0).astype(F32)
    chosen = jnp.where(rank == slot, jnp.where(mask == 1, 1.0, 0.0), 0.0)
    valid = jnp.sum(chosen, axis=1, keepdims=True) > 0.5
    cond[xl, h] = dot(chosen.astype(BF16), out_ref[...]).astype(BF16)
    cond_sent = []
    for i, (dx, dh) in enumerate(line):
        copy = pltpu.make_async_remote_copy(
            src_ref=cond.at[xl, h], dst_ref=cond.at[xl, h], send_sem=cssem.at[i],
            recv_sem=crsem.at[xl * N_HEAD + h], device_id=on_line(dx, dh)[2], device_id_type=MESH,
        )
        copy.start()
        cond_sent.append(copy)

    both(p2_fwd, "gu", 3)

    acc_t[...] = jnp.zeros_like(acc_t)

    def grad_step(c, carry):
        keys, values = keys_of(c)
        prob = probs[pl.ds(pl.multiple_of(c * KC, KC), KC), :].astype(F32) * inverse
        ds = (prob * (dot(values, dot_t[...]) - delta)).astype(BF16)
        acc_t[...] += contract_rows(keys, ds)
        dkv[pl.ds(2 * c, 2), 0:TOK, :] = (dot(ds, qs[...]) * SCALE).astype(BF16).reshape(2, TOK, HD)
        dkv[pl.ds(2 * c, 2), TOK : 2 * TOK, :] = dot(prob.astype(BF16), dos[...]).astype(BF16).reshape(2, TOK, HD)
        return carry

    def cross_copy(kb):
        return pltpu.make_async_remote_copy(
            src_ref=dkv.at[kb], dst_ref=mterm.at[kb], send_sem=xssem.at[kb], recv_sem=xrsem.at[kb],
            device_id=(mate, h), device_id_type=MESH,
        )

    for part in range(4):
        lax.fori_loop(part * 4, jnp.minimum(n_steps, part * 4 + 4), grad_step, 0)
        if part == 0:
            both(p2_fwd, "gu", 2)
            both(p1_fin, "dn")
            both(p2_send, "dn", 0)
            both(p2_send, "dn", 1)
        if part == 2:
            both(p2_send, "dn", 3)
        if part < 2:

            def send_cross(kb, carry):
                cross_copy(kb).start()
                return carry

            @pl.when(xl == 1)
            def _():
                lax.fori_loop(part * 8, part * 8 + 8, send_cross, 0)

    for j in range(GRP):
        cols = slice(j * HD, (j + 1) * HD)
        dq_ref[:, cols] = (acc_t[:, cols] * SCALE).T.astype(BF16)

    for dx, dh in line:
        ox, oh, dev = on_line(dx, dh)
        pltpu.make_async_remote_copy(
            src_ref=cond.at[ox, oh], dst_ref=cond.at[ox, oh], send_sem=cssem.at[0],
            recv_sem=crsem.at[ox * N_HEAD + oh], device_id=dev, device_id_type=MESH,
        ).wait_recv()

    def norm_rows(g, carry):
        rows = pl.ds(pl.multiple_of(g * CAP, CAP), CAP)
        square = jnp.zeros((CAP, 1), F32)
        for hh in range(N_HEAD):
            cols = slice(hh * HEADW, (hh + 1) * HEADW)
            base = le[rows, cols] + cond[lax.rem(g, 2), hh].astype(F32)
            le[rows, cols] = base
            square += jnp.sum(base * base, axis=1, keepdims=True)
        scale = lax.rsqrt(square * (1.0 / D) + 1e-06)
        for hh in range(N_HEAD):
            cols = slice(hh * HEADW, (hh + 1) * HEADW)
            nm[rows, cols] = (le[rows, cols] * scale * ngain_ref[cols].reshape(1, HEADW)).astype(BF16)
        return carry

    lax.fori_loop(0, 2 * NOISE, norm_rows, 0)
    for d in (0, 1, 3, 2):
        both(p2_fin, "gu", d)

    SUB = 4 * FEAT
    mine = pl.ds(pl.multiple_of((core * 4 + x) * CAP, CAP), CAP)
    for at in range(4):
        for other_at in range(4):
            c0 = other_at * SUB + at * FEAT
            to = slice(other_at * FEAT, (other_at + 1) * FEAT)
            fin[0, at, :, to] = le[mine, c0 : c0 + FEAT]
            og[0, at, :, to] = jnp.broadcast_to(ogain_ref[c0 : c0 + FEAT].reshape(1, FEAT), (8, FEAT))
            lo[0, at, :, to] = lout_ref[:, c0 : c0 + FEAT]
        c1 = HALF + at * SUB
        fin[1, at] = le[mine, c1 : c1 + SUB]
        og[1, at] = jnp.broadcast_to(ogain_ref[c1 : c1 + SUB].reshape(1, SUB), (8, SUB))
        lo[1, at] = lout_ref[:, c1 : c1 + SUB]

    for k in range(4):
        piece = gu[k // 2, (k % 2) * 8 : (k % 2) * 8 + 8].reshape(8 * FEAT, GUW)
        part = dot(nm[:, k * 896 : (k + 1) * 896], piece)
        if k == 0:
            acc[...] = part
        else:
            acc[...] += part
        if k == 1:
            both(p2_fwd, "dn", 0)

    both(p2_fwd, "dn", 1)
    both(p2_send, "dn", 2)

    def silu(value):
        return value / (1.0 + jnp.exp(-value))

    mixed = acc[:, 2 * MAIN :]
    turned = pltpu.roll(mixed, 64, 1)
    lower_half = lax.broadcasted_iota(jnp.int32, (2 * NOISE * CAP, 128), 1) < 64

    @pl.when(xl == 0)
    def _():
        hid[:, 0:MAIN] = (silu(acc[:, 0:MAIN]) * acc[:, MAIN : 2 * MAIN]).astype(BF16)
        hid[:, MAIN:DNW] = jnp.where(lower_half, silu(mixed) * turned, 0.0).astype(BF16)

    @pl.when(xl == 1)
    def _():
        hid[:, 128:DNW] = (silu(acc[:, 0:MAIN]) * acc[:, MAIN : 2 * MAIN]).astype(BF16)
        hid[:, 0:128] = jnp.where(lower_half, 0.0, silu(turned) * mixed).astype(BF16)

    def term_copy(b, kb):
        return pltpu.make_async_remote_copy(
            src_ref=dkv.at[b * 16 + kb], dst_ref=drecv.at[b, zy], send_sem=dssem.at[b * 16 + kb],
            recv_sem=drsem.at[b * 16 + zy], device_id=(xl * 16 + kb, h), device_id_type=MESH,
        )

    def forward_copy(kb):
        return pltpu.make_async_remote_copy(
            src_ref=mterm.at[kb], dst_ref=drecv.at[0, zy], send_sem=dssem.at[kb], recv_sem=drsem.at[zy],
            device_id=(kb, h), device_id_type=MESH,
        )

    def some_terms(first, last):
        def step(i, carry):
            kb = lax.rem(zy + i, 16)

            pl.when((xl == 1) & (kb < zy))(lambda: term_copy(1, kb).start())
            return carry

        lax.fori_loop(first, last, step, 0)

    def term_at(dz, dy):
        return lax.rem(z + dz, 4) * 4 + lax.rem(y + dy, 4)

    def relay_copy(dz):
        return pltpu.make_async_remote_copy(
            src_ref=mterm.at[term_at(dz, 2)], dst_ref=rterm.at[dz], send_sem=rssem.at[dz], recv_sem=rrsem.at[dz],
            device_id=(z * 4 + back(y, 1), h), device_id_type=MESH,
        )

    def ready_term(dz, dy):
        kb = term_at(dz, dy)
        cross_copy(kb).wait_recv()

        @pl.when(kb < zy)
        def _():
            mterm[kb] = (mterm[kb].astype(F32) + dkv[kb].astype(F32)).astype(BF16)

        return kb

    def plane_terms():
        def far(dz, carry):
            ready_term(dz, 2)
            relay_copy(dz).start()
            return carry

        def near(dz, carry):
            forward_copy(ready_term(dz, 1)).start()
            return carry

        def column(dz, carry):
            forward_copy(ready_term(dz, 0)).start()
            return carry

        def joined(dz, carry):
            kb = ready_term(dz, 3)
            relay_copy(dz).wait_recv()
            mterm[kb] = (mterm[kb].astype(F32) + rterm[dz].astype(F32)).astype(BF16)
            forward_copy(kb).start()
            return carry

        lax.fori_loop(0, 4, far, 0)
        lax.fori_loop(0, 4, near, 0)
        lax.fori_loop(1, 4, column, 0)
        lax.fori_loop(0, 4, joined, 0)

    def plane_terms_left():
        def step(dz, carry):
            relay_copy(dz).wait_send()
            forward_copy(term_at(dz, 1)).wait_send()
            pl.when(dz > 0)(lambda: forward_copy(term_at(dz, 0)).wait_send())
            forward_copy(term_at(dz, 3)).wait_send()
            return carry

        lax.fori_loop(0, 4, step, 0)

    def add_terms(first, last):
        def step(i, carry):
            src = lax.rem(zy + 16 - i, 16)

            @pl.when(((xl == 0) & (lax.rem(y + 4 - lax.rem(src, 4), 4) != 2)) | ((xl == 1) & (src > zy)))
            def _():
                pltpu.make_async_remote_copy(
                    src_ref=drecv.at[xl, src], dst_ref=drecv.at[xl, src], send_sem=dssem.at[0],
                    recv_sem=drsem.at[xl * 16 + src], device_id=(mate, h), device_id_type=MESH,
                ).wait_recv()
                tsum[...] += drecv[xl, src].astype(F32)

            return carry

        lax.fori_loop(first, last, step, 0)

    def along_x(step):
        to = lax.rem(x + 4 + step, 4)
        return (lax.rem(to, 2) * 16 + zy, lax.div(to, 2) * 2 + core)

    def pick(step):
        return lax.rem(x + 4 + step, 4) * CAP

    order = (0, 1, 3, 2)

    def lanes(k):
        return slice(k * 512, k * 512 + SUB)

    def tot(k, r, step):
        first = pl.multiple_of(r * 256 + pick(step), CAP)
        return acc[pl.ds(first, CAP), lanes(k % 2)]

    sibling = (s, h + 1 - 2 * core)

    def stage0(k):
        for r in (0, 1):
            p2_fin("dn", r, order[k])
        pieces = []
        for r in (0, 1):
            at = back(y if r == 0 else z, order[k]) * 4
            piece = dn[r, pl.ds(at, 4)].reshape(SUB, DNW)
            pieces.append(piece)
            theirs = hid[pl.ds(pl.multiple_of((1 - core) * 256, 256), 256), :]
            part = lax.dot_general(theirs, piece, (((1,), (1,)), ((), ())), preferred_element_type=F32)
            s1[k, r] = part.astype(BF16)
            start(lambda r=r: (s1.at[k, r], r1.at[k, r], sibling), ("r1", k, r))
        for r in (0, 1):
            ours = hid[pl.ds(pl.multiple_of(core * 256, 256), 256), :]
            acc[r * 256 : r * 256 + 256, lanes(k % 2)] = lax.dot_general(ours, pieces[r], (((1,), (1,)), ((), ())), preferred_element_type=F32)

    def stage1(k):
        for r in (0, 1):
            landed(r1.at[k, r], ("r1", k, r), sibling)
            far = r1[k, r, pl.ds(pl.multiple_of(pick(2), CAP), CAP), :].astype(F32)
            s23[0, k, r] = (tot(k, r, 2) + far).astype(BF16)
            start(lambda r=r: (s23.at[0, k, r], r2.at[k, r], along_x(1 - 2 * r)), ("r2", k, r))
        for r in (0, 1):
            acc[r * 256 : r * 256 + 256, lanes(k % 2)] += r1[k, r].astype(F32)

    def stage2(k):
        for r in (0, 1):
            landed(r2.at[k, r], ("r2", k, r), along_x(1))
            for way, step in ((0, 1), (1, -1)):
                near = tot(k, r, step)
                if way == r:
                    near += r2[k, r].astype(F32)
                s23[1 + way, k, r] = near.astype(BF16)
                start(
                    lambda r=r, way=way, step=step: (s23.at[1 + way, k, r], r3.at[k, r, way], along_x(step)),
                    ("r3", k, r, way),
                )
            fin[r, back(y if r == 0 else z, order[k])] += tot(k, r, 0)

    def stage3(k):
        for r in (0, 1):
            at = back(y if r == 0 else z, order[k])
            for way in (0, 1):
                landed(r3.at[k, r, way], ("r3", k, r, way), along_x(1))
                fin[r, at] += r3[k, r, way].astype(F32)

    stage0(0)
    both(p2_fwd, "dn", 3)
    stage1(0)
    stage0(1)
    stage2(0)
    stage1(1)
    both(p2_fwd, "dn", 2)
    some_terms(1, 16)
    pl.when(xl == 0)(plane_terms)
    stage2(1)
    stage0(2)
    stage1(2)
    stage0(3)
    stage2(2)
    stage1(3)
    tsum[...] = dkv[s].astype(F32)
    add_terms(1, 4)
    stage2(3)
    add_terms(4, 8)
    for k in range(4):
        stage3(k)

    square = jnp.zeros((CAP, 1), F32)
    for r in (0, 1):
        for at in range(4):
            rows = fin[r, at]
            square += jnp.sum(rows * rows, axis=1, keepdims=True)
    scale = lax.rsqrt(square * (1.0 / D) + 1e-06)
    result = jnp.zeros((CAP, LAT), F32)
    for r in (0, 1):
        for at in range(4):
            final = (fin[r, at] * scale * og[r, at, 0:1, :]).astype(BF16)
            result += lax.dot_general(final, lo[r, at], (((1,), (1,)), ((), ())), preferred_element_type=F32)
    pred_ref[...] = jnp.where(valid, result, 0.0)

    @pl.when(xl == 0)
    def _():
        cross_copy(zy).wait_recv()
        tsum[...] += mterm[zy].astype(F32)

    add_terms(8, 16)
    dk_ref[...] = tsum[0:TOK].astype(BF16)
    dv_ref[...] = tsum[TOK : 2 * TOK].astype(BF16)

    all_left()
    for copy in cond_sent:
        copy.wait_send()

    def left(copy):
        def step(kb, carry):
            copy(kb).wait_send()
            return carry

        return step

    @pl.when(xl == 1)
    def _():
        lax.fori_loop(0, 16, left(cross_copy), 0)
        lax.fori_loop(0, zy, left(lambda kb: term_copy(1, kb)), 0)

    @pl.when(xl == 0)
    def _():
        plane_terms_left()


def hand_over(*refs):
    for i in range(5):
        refs[5 + i][...] = refs[i][...]


def shards(
    queries, key_vectors, value_vectors, out_cotangent, latent_mask, clean_latents, noise_draws, timesteps,
    latent_in, norm_gain, gate_weight, up_weight, down_weight, out_gain, latent_out,
):
    frequencies = np.exp(-math.log(10000.0) * np.arange(HALF, dtype=np.float32) / HALF).astype(np.float32)
    vmem = pl.BlockSpec(memory_space=pltpu.VMEM)
    hbm = pl.BlockSpec(memory_space=pl.ANY)
    dma = pltpu.SemaphoreType.DMA
    n_sems = 176
    results = pl.pallas_call(
        kernel,
        out_shape=(
            jax.ShapeDtypeStruct((TOK, ROWS), BF16),
            jax.ShapeDtypeStruct((TOK, ROWS), BF16),
            jax.ShapeDtypeStruct((TOK, HD), BF16),
            jax.ShapeDtypeStruct((TOK, HD), BF16),
            jax.ShapeDtypeStruct((CAP, LAT), F32),
        ),
        in_specs=[hbm if i in (0, 3, 5, 6, 8, 12, 14) else vmem for i in range(16)],
        out_specs=(vmem,) * 5,
        scratch_shapes=[
            pltpu.VMEM((2, 16, 2 * TOK, HD), BF16),
            pltpu.VMEM((2, 16, FEAT, GUW), BF16),
            pltpu.VMEM((2, 16, FEAT, DNW), BF16),
            pltpu.VMEM((FEAT, GUW), BF16),
            pltpu.VMEM((FEAT, DNW), BF16),
            pltpu.VMEM((ROWS, HD), BF16),
            pltpu.VMEM((HD, ROWS), BF16),
            pltpu.VMEM((ROWS, HD), BF16),
            pltpu.VMEM((HD, ROWS), BF16),
            pltpu.VMEM((N_SEQ * TOK, ROWS), BF16),
            pltpu.VMEM((HD, ROWS), F32),
            pltpu.VMEM((N_SEQ, 2 * TOK, HD), BF16),
            pltpu.VMEM((2, 16, 2 * TOK, HD), BF16),
            pltpu.VMEM((2, N_HEAD, CAP, HEADW), BF16),
            pltpu.VMEM((2, NOISE * CAP, 128), BF16),
            pltpu.VMEM((2, CAP, 128), jnp.int32),
            pltpu.VMEM((4, 128, HALF), BF16),
            pltpu.VMEM((2 * NOISE * CAP, 128), BF16),
            pltpu.VMEM((2 * NOISE * CAP, 128), BF16),
            pltpu.VMEM((2 * NOISE * CAP, D), F32),
            pltpu.VMEM((2 * NOISE * CAP, D), BF16),
            pltpu.VMEM((2 * NOISE * CAP, GUW), F32),
            pltpu.VMEM((2 * NOISE * CAP, DNW), BF16),
            pltpu.VMEM((4, 2, 4 * CAP, 4 * FEAT), BF16),
            pltpu.VMEM((3, 4, 2, CAP, 4 * FEAT), BF16),
            pltpu.VMEM((4, 2, 4 * CAP, 4 * FEAT), BF16),
            pltpu.VMEM((4, 2, CAP, 4 * FEAT), BF16),
            pltpu.VMEM((4, 2, 2, CAP, 4 * FEAT), BF16),
            pltpu.VMEM((2, 4, CAP, 4 * FEAT), F32),
            pltpu.VMEM((2, 4, 8, 4 * FEAT), F32),
            pltpu.VMEM((2, 4, LAT, 4 * FEAT), BF16),
            pltpu.VMEM((16, 2 * TOK, HD), BF16),
            pltpu.VMEM((2 * TOK, HD), F32),
            pltpu.VMEM((4, 2 * TOK, HD), BF16),
            pltpu.VMEM((TOK, ROWS), BF16),
            pltpu.VMEM((TOK, ROWS), BF16),
            pltpu.VMEM((CAP, LAT), F32),
            pltpu.VMEM((CAP, NOISE * LAT), F32),
            pltpu.VMEM((LAT, D), BF16),
            pltpu.VMEM((FEAT, 1408), BF16),
            pltpu.VMEM((LAT, D), BF16),
            dma((n_sems,)),
            dma((n_sems,)),
            dma((N_SEQ,)),
            dma((N_SEQ,)),
            dma((7,)),
            dma((8,)),
            dma((16,)),
            dma((16,)),
            dma((7,)),
            dma((4,)),
            dma((4,)),
        ],
        compiler_params=pltpu.CompilerParams(
            collective_id=0, has_side_effects=True, vmem_limit_bytes=63 * 1024 * 1024
        ),
    )(
        queries, key_vectors, value_vectors, out_cotangent, latent_mask.reshape(1, TOK), clean_latents, noise_draws,
        timesteps.T, latent_in, norm_gain, gate_weight, up_weight, down_weight, out_gain,
        latent_out.T, jnp.asarray(frequencies.reshape(1, HALF)),
    )
    return pl.pallas_call(
        hand_over,
        out_shape=tuple(jax.ShapeDtypeStruct(a.shape, a.dtype) for a in results),
        in_specs=[vmem] * 5,
        out_specs=(vmem,) * 5,
        compiler_params=pltpu.CompilerParams(vmem_limit_bytes=63 * 1024 * 1024),
    )(*results)


def solution(mesh):
    placed = (
        P("seq", "head"),
        P("seq", "head"),
        P("seq", "head"),
        P("seq", "head"),
        P("seq"),
        P("seq", None),
        P("seq", None),
        P("seq", None),
        P(),
        P(),
        P("seq", "head"),
        P("seq", "head"),
        P("seq", "head"),
        P(),
        P(),
    )
    return jax.shard_map(
        shards,
        mesh=mesh,
        in_specs=placed,
        out_specs=(P("seq", "head"),) * 5,
        check_vma=False,
    )
```
